32 devices in a mesh: dp: 4 (over x, core), lat: 8 (over z, y).
Axes of the slice: x: 2, y: 2, z: 4, core: 2. Of those that a mesh axis runs over, the one named last changes fastest.
Arguments:
- fields: float32 [8, 189, 128, 512], P('dp', None, 'lat'), may hold values from -6 to 6
- target: float32 [8, 189, 128, 512], P('dp', None, 'lat'), may hold values from -6 to 6
- valid_mask: int32 [8, 128, 512], P('dp', 'lat'), may hold values 0 or 1
- sample_index: int32 [8], P('dp'), may hold values from 0 to 15
- weight_table: float32 [16], replicated, may hold values from 0.1 to 10
- lon_shift: int32 [8], P('dp'), may hold values from 0 to 127
- w_embed: float32 [3024, 192], P(None, 'lat'), may hold values from -0.109375 to 0.109375
- w_in: float32 [2, 192, 1344], P(None, None, 'lat'), may hold values from -0.4375 to 0.4375
- w_out: float32 [2, 960, 192], P(None, 'lat'), may hold values from -0.625 to 0.625
- w_merge: float32 [2, 192, 384], P(None, None, 'lat'), may hold values from -0.4375 to 0.4375
- w_fin: float32 [384, 2688], P(None, 'lat'), may hold values from -0.3125 to 0.3125
- w_fout: float32 [1920, 384], P('lat'), may hold values from -0.4375 to 0.4375
- w_head: float32 [192, 3024], P('lat'), may hold values from -0.4375 to 0.4375
- gains: float32 [9, 192], P(None, 'lat'), may hold values from 0.5 to 1.5
- row_stats: float32 [8208], replicated, may hold values from 1.5258789e-09 to 1.2207031e-08
- col_stats: float32 [10128], replicated, may hold values from 1.5258789e-09 to 1.2207031e-08
- v_gain: float32 [9, 192], P(None, 'lat'), may hold values from 1.5258789e-09 to 1.2207031e-08
Outputs:
- loss: float32 [], replicated
- new_embed: float32 [3024, 192], P(None, 'lat')
- new_in: float32 [2, 192, 1344], P(None, None, 'lat')
- new_out: float32 [2, 960, 192], P(None, 'lat')
- new_merge: float32 [2, 192, 384], P(None, None, 'lat')
- new_fin: float32 [384, 2688], P(None, 'lat')
- new_fout: float32 [1920, 384], P('lat')
- new_head: float32 [192, 3024], P('lat')
- new_gains: float32 [9, 192], P(None, 'lat')
- next_rows: float32 [8208], replicated
- next_cols: float32 [10128], replicated
- next_v_gain: float32 [9, 192], P(None, 'lat')
- copy_embed: bfloat16 [3024, 192], P(None, 'lat')
- copy_in: bfloat16 [2, 192, 1344], P(None, None, 'lat')
- copy_out: bfloat16 [2, 960, 192], P(None, 'lat')
- copy_merge: bfloat16 [2, 192, 384], P(None, None, 'lat')
- copy_fin: bfloat16 [384, 2688], P(None, 'lat')
- copy_fout: bfloat16 [1920, 384], P('lat')
- copy_head: bfloat16 [192, 3024], P('lat')
- copy_gains: bfloat16 [9, 192], P(None, 'lat')
The draws below stay inside these ranges and needn't reach their ends.
All inputs are finite; a program needn't handle non-finite values. No bound on the sum of `valid_mask` on one device may be relied on, other than what follows from the above.
Results may differ from the reference program's by a relative error of at most 0.001.
Values sent between devices are 32-bit elements; how exact they have to be, the bound alone decides.
No kernel may reach another device: no remote copies, remote signals or barrier semaphores. Data moves between devices by JAX's collectives and lax.ppermute only.
A program may use at most 384 MiB of HBM per device.

```python
import math
import jax
import jax.numpy as jnp
from jax import lax

C = 189
D = 192
HEAD = 32
FF = 768
DF = 384
FF2 = 1536
PATCH = 4
WR = 4
WC = 16
NB = 2
TABLE = 16
LON = 128
PD = 3024
NS = 8
HPIX = 128
WPIX = 512
NROW = 8208
NCOL = 10128


def set_ends(drawn, key, low, high):
    longest = drawn.shape.index(max(drawn.shape))
    spots = []
    for shift in (0, 1):
        where = [jax.random.randint(jax.random.fold_in(key, axis), (), 0, length) for axis, length in enumerate(drawn.shape)]
        where[longest] = (where[longest] + shift) % drawn.shape[longest]
        spots.append(tuple(where))
    return drawn.at[spots[0]].set(low).at[spots[1]].set(high)


def block_scale(key, extent, split, smallest, high):
    loudness = 1.0
    for axis_at, shards_of in split:
        heights = jax.random.uniform(jax.random.fold_in(jax.random.fold_in(key, 6), axis_at), (shards_of,), jnp.float32, smallest / len(split), high / len(split))
        loudness = loudness * jnp.repeat(jnp.exp(heights), extent[axis_at] // shards_of).reshape((-1,) + (1,) * (len(extent) - 1 - axis_at))
    return loudness


def scatter_about(key, dims, scale, limit, shards=(), held_as=jnp.bfloat16):
    loudness = block_scale(key, dims, shards, -0.22, 0.18) if shards else 1.0
    entries = jax.random.normal(key, dims, jnp.float32) * scale * loudness
    return jnp.minimum(jnp.maximum(entries, -limit), limit).astype(held_as)


def setup_inputs(seed: int = 0) -> dict:
    streams_of = jax.random.split(jax.random.key(seed), 18)
    fields = scatter_about(streams_of[0], (NS, C, HPIX, WPIX), 1.0, 6.0, ((0, 4), (2, 8)), jnp.float32)
    target = scatter_about(streams_of[1], (NS, C, HPIX, WPIX), 1.0, 6.0, ((0, 4), (2, 8)), jnp.float32)
    valid_mask = set_ends((jax.random.randint(streams_of[2], (NS, HPIX, WPIX), 0, 10) < 7).astype(jnp.int32), jax.random.fold_in(streams_of[2], 1), 0, 1)
    sample_index = set_ends(jax.random.randint(streams_of[3], (NS,), 0, TABLE), jax.random.fold_in(streams_of[3], 1), 0, TABLE - 1).astype(jnp.int32)
    weight_table = jnp.clip(jnp.exp(jax.random.uniform(streams_of[4], (TABLE,), jnp.float32, math.log(0.1), math.log(10.0))), 0.1, 10.0)
    lon_shift = set_ends(jax.random.randint(streams_of[5], (NS,), 0, LON), jax.random.fold_in(streams_of[5], 1), 0, LON - 1).astype(jnp.int32)
    w_embed = scatter_about(streams_of[6], (PD, D), PD ** -0.5, 0.109375, ((1, 8),), jnp.float32)
    w_in = scatter_about(streams_of[7], (NB, D, 3 * D + FF), D ** -0.5, 0.4375, ((2, 8),), jnp.float32)
    w_out = scatter_about(streams_of[8], (NB, D + FF, D), (D // 2) ** -0.5, 0.625, ((1, 8),), jnp.float32)
    w_merge = scatter_about(streams_of[9], (2, D, DF), D ** -0.5, 0.4375, ((2, 8),), jnp.float32)
    w_fin = scatter_about(streams_of[10], (DF, 3 * DF + FF2), DF ** -0.5, 0.3125, ((1, 8),), jnp.float32)
    w_fout = scatter_about(streams_of[11], (DF + FF2, DF), (DF // 2) ** -0.5, 0.4375, ((0, 8),), jnp.float32)
    w_head = scatter_about(streams_of[12], (D, PD), D ** -0.5, 0.4375, ((0, 8),), jnp.float32)
    gains = jnp.clip(1.0 + 0.1 * jax.random.normal(streams_of[13], (2 * NB + 5, D), jnp.float32), 0.5, 1.5)
    row_stats = jnp.clip(jnp.exp(jax.random.uniform(streams_of[14], (NROW,), jnp.float32, math.log(1.5258788677030566e-09), math.log(1.2207030941624453e-08))), 1.5258788677030566e-09, 1.2207030941624453e-08)
    col_stats = jnp.clip(jnp.exp(jax.random.uniform(streams_of[15], (NCOL,), jnp.float32, math.log(1.5258788677030566e-09), math.log(1.2207030941624453e-08))), 1.5258788677030566e-09, 1.2207030941624453e-08)
    v_gain = jnp.clip(jnp.exp(math.log(1.2207030941624453e-08) - 2.0794415 * jax.random.uniform(streams_of[16], (2 * NB + 5, D), jnp.float32) ** block_scale(streams_of[16], (2 * NB + 5, D), ((1, 8),), -0.2, 0.2)), 1.5258788677030566e-09, 1.2207030941624453e-08)
    return dict(fields=fields, target=target, valid_mask=valid_mask, sample_index=sample_index, weight_table=weight_table, lon_shift=lon_shift, w_embed=w_embed, w_in=w_in, w_out=w_out, w_merge=w_merge, w_fin=w_fin, w_fout=w_fout, w_head=w_head, gains=gains, row_stats=row_stats, col_stats=col_stats, v_gain=v_gain)


HIGH = lax.Precision.HIGHEST
clip_level = 0.25

@jax.custom_vjp
def low(v):
    return lax.optimization_barrier(v.astype(jnp.bfloat16)).astype(jnp.float32)

@jax.custom_vjp
def low_back(v):
    return v

def low_keep(v):
    return (low(v), None)

def low_pass(kept, grad):
    return (grad,)

def back_keep(v):
    return (v, None)

def back_low(kept, grad):
    return (low(grad),)
low.defvjp(low_keep, low_pass)
low_back.defvjp(back_keep, back_low)

def layer_norm(stream, gain):
    average = lax.optimization_barrier(jnp.mean(stream, axis=-1, keepdims=True))
    centred = stream - average
    spread = lax.optimization_barrier(jnp.mean(centred * centred, axis=-1, keepdims=True))
    return centred * lax.rsqrt(spread + 1e-05) * gain

def window_block(stream, w_in_b, w_out_b, gain_att, gain_mlp):
    samples, rows, cols, width = stream.shape
    heads = width // HEAD
    normed = layer_norm(stream, gain_att)
    projected = jnp.einsum('srld,de->srle', normed, w_in_b[:, :3 * width], precision=HIGH)
    projected = projected.reshape(samples, rows // WR, WR, cols // WC, WC, 3, heads, HEAD)
    projected = projected.transpose(0, 1, 3, 5, 6, 2, 4, 7).reshape(samples, rows // WR, cols // WC, 3, heads, WR * WC, HEAD)
    queries, keys, values = (projected[:, :, :, 0], projected[:, :, :, 1], projected[:, :, :, 2])
    scores = jnp.einsum('abchqe,abchke->abchqk', queries, keys, precision=HIGH) * HEAD ** (-0.5)
    attention = jax.nn.softmax(scores, axis=-1)
    attended = jnp.einsum('abchqk,abchke->abchqe', attention, values, precision=HIGH)
    attended = attended.reshape(samples, rows // WR, cols // WC, heads, WR, WC, HEAD)
    attended = attended.transpose(0, 1, 4, 2, 5, 3, 6).reshape(samples, rows, cols, width)
    stream = stream + jnp.einsum('srld,de->srle', attended, w_out_b[:width], precision=HIGH)
    normed = layer_norm(stream, gain_mlp)
    hidden = jax.nn.gelu(jnp.einsum('srld,de->srle', normed, w_in_b[:, 3 * width:], precision=HIGH))
    return stream + jnp.einsum('srle,ed->srld', hidden, w_out_b[width:], precision=HIGH)

def patchify(fields):
    samples, chans, height, across = fields.shape
    blocks = fields.reshape(samples, chans, height // PATCH, PATCH, across // PATCH, PATCH)
    return blocks.transpose(0, 2, 4, 1, 3, 5).reshape(samples, height // PATCH, across // PATCH, chans * PATCH * PATCH)

def unpatchify(flat):
    samples, rows, cols, pixels = flat.shape
    chans = pixels // (PATCH * PATCH)
    blocks = flat.reshape(samples, rows, cols, chans, PATCH, PATCH)
    return blocks.transpose(0, 3, 1, 4, 2, 5).reshape(samples, chans, rows * PATCH, cols * PATCH)

def roll_columns(stream, shifts, sign):
    return jax.vmap(lambda one, amount: jnp.roll(one, sign * amount, axis=1))(stream, shifts)

def forward_loss(params, patches, target, weight, shifts):
    w_embed, w_in, w_out, w_merge, w_fin, w_fout, w_head, gains = params
    stream = jnp.einsum('srlp,pd->srld', patches, w_embed, precision=HIGH)
    stream = window_block(stream, w_in[0], w_out[0], gains[0], gains[1])
    wide = jnp.einsum('srld,de->srle', stream, w_merge[0], precision=HIGH)
    wide = roll_columns(jnp.roll(wide, -(WR // 2), axis=1), shifts, -1)
    base = 2 * NB + 1
    wide = window_block(wide, w_fin, w_fout, gains[base:base + 2].reshape(-1), gains[base + 2:base + 4].reshape(-1))
    wide = jnp.roll(roll_columns(wide, shifts, 1), WR // 2, axis=1)
    stream = stream + jnp.einsum('srle,de->srld', wide, w_merge[1], precision=HIGH)
    stream = window_block(stream, w_in[1], w_out[1], gains[2], gains[3])
    normed = layer_norm(stream, gains[2 * NB])
    pred = unpatchify(jnp.einsum('srld,dp->srlp', normed, w_head, precision=HIGH))
    differ = pred - target
    total = jnp.sum(weight[:, None] * differ * differ)
    count = C * jnp.sum(weight)
    return total / count

def finish(weight, update, axes):
    rms_update = jnp.sqrt(lax.optimization_barrier(jnp.mean(update * update, axis=axes, keepdims=True)))
    update = update / jnp.maximum(1.0, rms_update / clip_level)
    rms_weight = jnp.sqrt(lax.optimization_barrier(jnp.mean(weight * weight, axis=axes, keepdims=True)))
    return weight - jnp.maximum(0.001, rms_weight) * update

def factored(weight, gradient, row_stat, col_stat):
    square = gradient * gradient + 1e-30
    row_new = 0.5 * row_stat + 0.5 * lax.optimization_barrier(jnp.mean(square, axis=-1))
    col_new = 0.5 * col_stat + 0.5 * lax.optimization_barrier(jnp.mean(square, axis=-2))
    row_mean = lax.optimization_barrier(jnp.mean(row_new, axis=-1))
    update = gradient * lax.rsqrt(row_new[..., :, None] * col_new[..., None, :] / row_mean[..., None, None])
    return (finish(weight, update, (-2, -1)), row_new, col_new)

def reference(fields, target, valid_mask, sample_index, weight_table, lon_shift, w_embed, w_in, w_out, w_merge, w_fin, w_fout, w_head, gains, row_stats, col_stats, v_gain):
    patches = patchify(fields)
    pixel_rows = jnp.arange(HPIX, dtype=jnp.float32)
    coslat = jnp.cos((90.0 - (pixel_rows + 0.5) * 180.0 / HPIX) * (jnp.pi / 180.0))
    weight = weight_table[sample_index][:, None, None] * coslat[None, :, None] * valid_mask.astype(jnp.float32)
    params = (w_embed, w_in, w_out, w_merge, w_fin, w_fout, w_head, gains)
    loss, puller = jax.vjp(lambda p: forward_loss(p, patches, target, weight, lon_shift), params)
    grads = puller(jnp.ones((), jnp.float32))[0]
    mats = [w_embed[None], w_in, w_out, w_merge, w_fin[None], w_fout[None], w_head[None]]
    gmats = [grads[0][None], grads[1], grads[2], grads[3], grads[4][None], grads[5][None], grads[6][None]]
    new_mats, row_parts, col_parts = ([], [], [])
    row_at, col_at = (0, 0)
    for matrix, gradient in zip(mats, gmats):
        stack, rows_n, cols_n = matrix.shape
        row_stat = row_stats[row_at:row_at + stack * rows_n].reshape(stack, rows_n)
        col_stat = col_stats[col_at:col_at + stack * cols_n].reshape(stack, cols_n)
        row_at += stack * rows_n
        col_at += stack * cols_n
        new_matrix, row_new, col_new = factored(matrix, gradient, row_stat, col_stat)
        new_mats.append(new_matrix)
        row_parts.append(row_new.reshape(-1))
        col_parts.append(col_new.reshape(-1))
    g_gain = grads[7]
    next_v_gain = 0.5 * v_gain + 0.5 * (g_gain * g_gain + 1e-30)
    new_gains = finish(gains, g_gain * lax.rsqrt(next_v_gain), (-1,))
    new_embed, new_in, new_out, new_merge = (new_mats[0][0], new_mats[1], new_mats[2], new_mats[3])
    new_fin, new_fout, new_head = (new_mats[4][0], new_mats[5][0], new_mats[6][0])
    return (loss, new_embed, new_in, new_out, new_merge, new_fin, new_fout, new_head, new_gains, jnp.concatenate(row_parts), jnp.concatenate(col_parts), next_v_gain, new_embed.astype(jnp.bfloat16), new_in.astype(jnp.bfloat16), new_out.astype(jnp.bfloat16), new_merge.astype(jnp.bfloat16), new_fin.astype(jnp.bfloat16), new_fout.astype(jnp.bfloat16), new_head.astype(jnp.bfloat16), new_gains.astype(jnp.bfloat16))
```

```python
import functools
import math

import jax
import jax.numpy as jnp
from jax import lax
from jax.experimental import pallas as pl
from jax.experimental.pallas import tpu as pltpu
from jax.sharding import PartitionSpec as P

F32 = jnp.float32
BF16 = jnp.bfloat16
HEAD = 32
PATCH = 4
WR = 4
WC = 16
CH = 192
VMEM = 60 * 1024 * 1024
ROOT = math.sqrt(2.0 / math.pi)
NN, NT, TN = (1, 0), (1, 1), (0, 0)


def params(steps):
    return pltpu.CompilerParams(
        dimension_semantics=("arbitrary",) * steps, vmem_limit_bytes=VMEM
    )


def split(value):
    high = value.astype(BF16)
    return high, (value - high.astype(F32)).astype(BF16)


def dg(a, b, dims):
    return lax.dot_general(
        a, b, (((dims[0],), (dims[1],)), ((), ())), preferred_element_type=F32
    )


def dot3(a, b, dims):
    return dg(a[0], b[0], dims) + (dg(a[0], b[1], dims) + dg(a[1], b[0], dims))


def normalise(stream):
    centred = stream - jnp.mean(stream, axis=0, keepdims=True)
    scale = lax.rsqrt(jnp.mean(centred * centred, axis=0, keepdims=True) + 1e-05)
    return centred * scale, scale


def normalise_back(grad, hat, scale, gain):
    weighted = grad * gain
    return scale * (
        weighted
        - jnp.mean(weighted, axis=0, keepdims=True)
        - hat * jnp.mean(weighted * hat, axis=0, keepdims=True)
    )


def iota(shape, axis):
    return lax.broadcasted_iota(jnp.int32, shape, axis)


def roll_matrix(shift, tokens):
    lane = iota((tokens, tokens), 0)
    out = iota((tokens, tokens), 1)
    half, inner = out // (tokens // 2), out % (tokens // 2)
    row = jnp.where(half == 0, 2, 0) + (inner // WC) % 2
    columns = tokens // WR
    moved = ((inner // (2 * WC)) * WC + inner % WC + shift) % columns
    source = (moved // WC) * (WR * WC) + row * WC + moved % WC
    return (lane == source).astype(BF16)


def order_matrix(tokens):
    lane = iota((tokens, tokens), 0)
    out = iota((tokens, tokens), 1)
    window, row, col = out // (WR * WC), (out // WC) % WR, out % WC
    source = (row // 2) * (tokens // 2) + window * (2 * WC) + (row % 2) * WC + col
    return (lane == source).astype(BF16)


def permute(value, onehot, dims):
    high, low = split(value)
    rest = (value - high.astype(F32) - low.astype(F32)).astype(BF16)
    return dg(high, onehot, dims) + (dg(low, onehot, dims) + dg(rest, onehot, dims))


def pixel_matrix():
    lane = iota((512, 512), 0)
    out = iota((512, 512), 1)
    b, window, row, col = out // 128, (out // 64) % 2, (out // 16) % 4, out % 16
    return (lane == row * 128 + window * 64 + col * 4 + b).astype(BF16)


def prep_kernel(chans, with_weight, *refs):
    if with_weight:
        x_ref, w_ref, out_ref, perm = refs
    else:
        x_ref, hi_ref, lo_ref, perm = refs
    block = 64

    @pl.when((pl.program_id(0) == 0) & (pl.program_id(1) == 0) & (pl.program_id(2) == 0))
    def _():
        perm[...] = pixel_matrix()

    row = iota((block, 512), 0) + pl.program_id(2) * block
    for a in range(PATCH):
        tile = jnp.concatenate(
            [x_ref[pl.ds(4 * r + a, block, stride=16), :] for r in range(WR)], axis=1
        )
        tile = jnp.where(row < chans, tile, 0.0)
        if with_weight:
            extra = jnp.concatenate([w_ref[4 * r + a : 4 * r + a + 1, :] for r in range(WR)], axis=1)
            tile = jnp.where(row == chans, extra, tile)
        high, low = split(tile)
        high, low = dg(high, perm[...], NN), dg(low, perm[...], NN)
        for b in range(PATCH):
            piece = slice(b * 128, b * 128 + 128)
            if with_weight:
                out_ref[b, a] = high[:, piece] + low[:, piece]
            else:
                hi_ref[b, a] = high[:, piece].astype(BF16)
                lo_ref[b, a] = low[:, piece].astype(BF16)


def prep(fields, weight=None):
    samples, chans, height, across = fields.shape
    flat = fields.reshape(samples, chans * height, across)
    padded = 192
    shape = (samples, 4, 4, padded, across)
    spec = pl.BlockSpec((None, 4, 4, 64, 128), lambda s, p, c: (s, 0, 0, c, p))
    in_specs = [pl.BlockSpec((None, 64 * height, 128), lambda s, p, c: (s, c, p))]
    if weight is not None:
        in_specs.append(pl.BlockSpec((None, height, 128), lambda s, p, c: (s, 0, p)))
        out_shape, out_specs = jax.ShapeDtypeStruct(shape, F32), spec
    else:
        out_shape = [jax.ShapeDtypeStruct(shape, BF16)] * 2
        out_specs = [spec] * 2
    outs = pl.pallas_call(
        functools.partial(prep_kernel, chans, weight is not None),
        out_shape=out_shape,
        grid=(samples, across // 128, padded // 64),
        in_specs=in_specs,
        out_specs=out_specs,
        scratch_shapes=[pltpu.VMEM((512, 512), BF16)],
        compiler_params=params(3),
        name="prep",
    )(*([flat] if weight is None else [flat, weight]))
    return jax.tree.map(lambda a: a.reshape(samples, 16 * padded, across), outs)


def embed_kernel(w_ref, hi_ref, lo_ref, out_ref):
    total = None
    for at in range(0, w_ref.shape[1], 768):
        part = dot3(
            split(w_ref[:, at : at + 768]),
            (hi_ref[at : at + 768, :], lo_ref[at : at + 768, :]),
            NN,
        )
        total = part if total is None else total + part
    out_ref[...] = total


def embed(weight, high, low):
    samples, depth, tokens = high.shape
    width = weight.shape[0]
    big = pl.BlockSpec((None, depth, tokens), lambda s: (s, 0, 0))
    return pl.pallas_call(
        embed_kernel,
        out_shape=jax.ShapeDtypeStruct((samples, width, tokens), F32),
        grid=(samples,),
        in_specs=[pl.BlockSpec((width, depth), lambda s: (0, 0)), big, big],
        out_specs=pl.BlockSpec((None, width, tokens), lambda s: (s, 0, 0)),
        compiler_params=params(1),
        name="embed",
    )(weight, high, low)


def embed_back_kernel(g_ref, hi_ref, lo_ref, out_ref):
    grad = split(g_ref[...])

    @pl.when(pl.program_id(0) == 0)
    def _():
        out_ref[...] = jnp.zeros_like(out_ref)

    for at in range(0, out_ref.shape[1], 768):
        out_ref[:, at : at + 768] += dot3(
            grad, (hi_ref[at : at + 768, :], lo_ref[at : at + 768, :]), NT
        )


def embed_back(grad, high, low):
    samples, depth, tokens = high.shape
    width = grad.shape[1]
    big = pl.BlockSpec((None, depth, tokens), lambda s: (s, 0, 0))
    return pl.pallas_call(
        embed_back_kernel,
        out_shape=jax.ShapeDtypeStruct((width, depth), F32),
        grid=(samples,),
        in_specs=[pl.BlockSpec((None, width, tokens), lambda s: (s, 0, 0)), big, big],
        out_specs=pl.BlockSpec((width, depth), lambda s: (0, 0)),
        compiler_params=params(1),
        name="embed_back",
    )(grad, high, low)


def rows_of(at, count=CH):
    return pl.ds(pl.multiple_of(at * count, count), count)


def attend(qkv_ref, a_ref, p_ref, width):
    heads = width // HEAD
    first = iota((64, 128), 1) < 64

    def one(pair, head):
        lanes = pl.ds(pl.multiple_of(pair * 128, 128), 128)
        where = lambda part: pl.ds(pl.multiple_of(part * width + head * HEAD, HEAD), HEAD)
        qh, ql = split(qkv_ref[where(0), lanes] * HEAD**-0.5)
        kh, kl = split(qkv_ref[where(1), lanes])
        vh, vl = split(qkv_ref[where(2), lanes])
        scores = dg(
            jnp.concatenate([kh, kh, kl], axis=0), jnp.concatenate([qh, ql, qh], axis=0), TN
        )
        scores = jnp.where(first, scores[:64], scores[64:])
        weight = jnp.exp(scores - jnp.max(scores, axis=0, keepdims=True))
        weight = weight / jnp.sum(weight, axis=0, keepdims=True)
        p_ref[pair, head] = weight
        ph, plo = spread(weight, first)
        a_ref[where(0), lanes] = dg(
            jnp.concatenate([vh, vh, vl], axis=1), jnp.concatenate([ph, plo, ph], axis=0), NN
        )

    def body(at, carry):
        pair, group = at // (heads // 6), at % (heads // 6)
        for h in range(6):
            one(pair, group * 6 + h)
        return carry

    lax.fori_loop(0, 4 * (heads // 6), body, 0)


def spread(compact, first):
    full = jnp.concatenate(
        [jnp.where(first, compact, 0.0), jnp.where(first, 0.0, compact)], axis=0
    )
    return split(full)


def attend_back(qkv_ref, p_ref, da_ref, dqkv_ref, width):
    heads = width // HEAD
    first = iota((64, 128), 1) < 64

    def one(pair, head):
        lanes = pl.ds(pl.multiple_of(pair * 128, 128), 128)
        where = lambda part: pl.ds(pl.multiple_of(part * width + head * HEAD, HEAD), HEAD)
        qh, ql = split(qkv_ref[where(0), lanes] * HEAD**-0.5)
        kh, kl = split(qkv_ref[where(1), lanes])
        vh, vl = split(qkv_ref[where(2), lanes])
        oh, ol = split(da_ref[where(0), lanes])
        weight = p_ref[pair, head]
        dp = dg(
            jnp.concatenate([vh, vh, vl], axis=0), jnp.concatenate([oh, ol, oh], axis=0), TN
        )
        dp = jnp.where(first, dp[:64], dp[64:])
        ds = weight * (dp - jnp.sum(dp * weight, axis=0, keepdims=True))
        ph, plo = spread(weight, first)
        sh, slo = spread(ds, first)
        dqkv_ref[where(2), lanes] = dg(
            jnp.concatenate([oh, oh, ol], axis=1), jnp.concatenate([ph, plo, ph], axis=1), NT
        )
        dqkv_ref[where(0), lanes] = (
            dg(jnp.concatenate([kh, kh, kl], axis=1), jnp.concatenate([sh, slo, sh], axis=0), NN)
            * HEAD**-0.5
        )
        dqkv_ref[where(1), lanes] = dg(
            jnp.concatenate([qh, qh, ql], axis=1), jnp.concatenate([sh, slo, sh], axis=1), NT
        )

    def body(at, carry):
        pair, group = at // (heads // 6), at % (heads // 6)
        for h in range(6):
            one(pair, group * 6 + h)
        return carry

    lax.fori_loop(0, 4 * (heads // 6), body, 0)


def block_forward(x, win_ref, wout_ref, ga, gm, qkv_ref, a_ref, mid_ref, u_ref, p_ref):
    width = x.shape[0]
    hat, _ = normalise(x)
    normed = split(hat * ga)

    def project(at, carry):
        qkv_ref[rows_of(at), :] = dot3(split(win_ref[rows_of(at), :]), normed, NN)
        return carry

    lax.fori_loop(0, 3 * width // CH, project, 0)
    attend(qkv_ref, a_ref, p_ref, width)
    mid = x
    for at in range(0, width, CH):
        mid = mid + dot3(split(wout_ref[at : at + CH, :]), split(a_ref[at : at + CH, :]), TN)
    mid_ref[...] = mid
    hat, _ = normalise(mid)
    normed = split(hat * gm)

    def feed(at, total):
        u = dot3(split(win_ref[rows_of(3 * width // CH + at), :]), normed, NN)
        u_ref[rows_of(at), :] = u
        hidden = 0.5 * u * (1.0 + jnp.tanh(ROOT * (u + 0.044715 * u * u * u)))
        return total + dot3(
            split(wout_ref[rows_of(width // CH + at), :]), split(hidden), TN
        )

    return lax.fori_loop(0, u_ref.shape[0] // CH, feed, mid)


def block_backward(
    dy, x, mid_ref, win_ref, wout_ref, ga, gm, qkv_ref, a_ref, u_ref, p_ref,
    gwin_ref, gwout_ref, gga_ref, ggm_ref, da_ref, dqkv_ref,
):
    width = x.shape[0]
    hat, scale = normalise(mid_ref[...])
    normed = split(hat * gm)
    dys = split(dy)

    def feed(at, total):
        u = u_ref[rows_of(at), :]
        t = jnp.tanh(ROOT * (u + 0.044715 * u * u * u))
        hidden = 0.5 * u * (1.0 + t)
        slope = 0.5 * (1.0 + t) + 0.5 * ROOT * u * (1.0 - t * t) * (1.0 + 3 * 0.044715 * u * u)
        out_rows, in_rows = rows_of(width // CH + at), rows_of(3 * width // CH + at)
        du = split(slope * dot3(split(wout_ref[out_rows, :]), dys, NN))
        gwout_ref[out_rows, :] += dot3(split(hidden), dys, NT)
        gwin_ref[in_rows, :] += dot3(du, normed, NT)
        return total + dot3(split(win_ref[in_rows, :]), du, TN)

    dn = lax.fori_loop(0, u_ref.shape[0] // CH, feed, jnp.zeros_like(x))
    ggm_ref[...] += fold(dn * hat)
    dmid = dy + normalise_back(dn, hat, scale, gm)
    dmids = split(dmid)
    for at in range(0, width, CH):
        da_ref[at : at + CH, :] = dot3(split(wout_ref[at : at + CH, :]), dmids, NN)
        gwout_ref[at : at + CH, :] += dot3(split(a_ref[at : at + CH, :]), dmids, NT)
    attend_back(qkv_ref, p_ref, da_ref, dqkv_ref, width)
    hat, scale = normalise(x)
    normed = split(hat * ga)

    def project(at, total):
        grad = split(dqkv_ref[rows_of(at), :])
        gwin_ref[rows_of(at), :] += dot3(grad, normed, NT)
        return total + dot3(split(win_ref[rows_of(at), :]), grad, TN)

    dn = lax.fori_loop(0, 3 * width // CH, project, jnp.zeros_like(x))
    gga_ref[...] += fold(dn * hat)
    return dmid + normalise_back(dn, hat, scale, ga)


def fold(value):
    return sum(value[:, at : at + 128] for at in range(0, value.shape[1], 128))


def saved_shapes(samples, width, hidden, tokens):
    heads = width // HEAD
    return [
        jax.ShapeDtypeStruct((samples, 3 * width, tokens), F32),
        jax.ShapeDtypeStruct((samples, width, tokens), F32),
        jax.ShapeDtypeStruct((samples, width, tokens), F32),
        jax.ShapeDtypeStruct((samples, hidden, tokens), F32),
        jax.ShapeDtypeStruct((samples, tokens // 128, heads, 64, 128), F32),
    ]


def per_sample(shape):
    tail = len(shape) - 1
    return pl.BlockSpec((None,) + tuple(shape[1:]), lambda s: (s,) + (0,) * tail)


def whole(shape):
    return pl.BlockSpec(tuple(shape), lambda s: (0,) * len(shape))


def call(body, outs, ins, accumulated, name, scratch=(), smem=()):
    samples = next(a.shape[0] for a, each in ins if each)
    in_specs = [per_sample(a.shape) if each else whole(a.shape) for a, each in ins]
    in_specs = [pl.BlockSpec(memory_space=pltpu.SMEM)] * len(smem) + in_specs
    out_specs = [per_sample(o.shape) for o in outs] + [whole(o.shape) for o in accumulated]
    return pl.pallas_call(
        body,
        out_shape=list(outs) + list(accumulated),
        grid=(samples,),
        in_specs=in_specs,
        out_specs=out_specs,
        scratch_shapes=list(scratch),
        compiler_params=params(1),
        name=name,
    )(*smem, *[a for a, _ in ins])


def clear(*refs):
    @pl.when(pl.program_id(0) == 0)
    def _():
        for ref in refs:
            ref[...] = jnp.zeros_like(ref)


def encoder_kernel(shift_ref, x_ref, win, wout, ga, gm, y, stay, send, qkv, a, mid, u, p):
    tokens = x_ref.shape[1]
    out = block_forward(x_ref[...], win, wout, ga[...], gm[...], qkv, a, mid, u, p)
    y[...] = out
    packed = permute(out, roll_matrix(shift_ref[pl.program_id(0)], tokens), NN)
    stay[...] = packed[:, : tokens // 2]
    send[...] = packed[:, tokens // 2 :]


def encoder(shift, x, win, wout, ga, gm):
    samples, width, tokens = x.shape
    half = jax.ShapeDtypeStruct((samples, width, tokens // 2), F32)
    outs = [jax.ShapeDtypeStruct(x.shape, F32), half, half]
    outs += saved_shapes(samples, width, win.shape[0] - 3 * width, tokens)
    return call(
        encoder_kernel, outs,
        [(x, True), (win, False), (wout, False), (ga, False), (gm, False)],
        [], "encoder", smem=(shift,),
    )


def merging_kernel(stay_in, send_in, wup, wback, win, wout, ga, gm,
                   x, wide, last, stay, send, qkv, a, mid, u, p):
    tokens = x.shape[1]
    order = order_matrix(tokens)
    start = permute(jnp.concatenate([stay_in[...], send_in[...]], axis=1), order, NN)
    x[...] = start
    raised = dot3(split(wup[...]), split(start), NN)
    wide[...] = raised
    out = block_forward(raised, win, wout, ga[...], gm[...], qkv, a, mid, u, p)
    last[...] = out
    lowered = permute(dot3(split(wback[...]), split(out), TN), order, NT)
    stay[...] = lowered[:, : tokens // 2]
    send[...] = lowered[:, tokens // 2 :]


def merging(stay, arrived, wup, wback, win, wout, ga, gm):
    samples, narrow, half = stay.shape
    width, tokens = wup.shape[0], 2 * half
    wide = jax.ShapeDtypeStruct((samples, width, tokens), F32)
    halved = jax.ShapeDtypeStruct(stay.shape, F32)
    outs = [jax.ShapeDtypeStruct((samples, narrow, tokens), F32), wide, wide, halved, halved]
    outs += saved_shapes(samples, width, win.shape[0] - 3 * width, tokens)
    weights = [(w, False) for w in (wup, wback, win, wout, ga, gm)]
    return call(
        merging_kernel, outs, [(stay, True), (arrived, True)] + weights, [], "merging"
    )


def decoder_kernel(shift_ref, y_ref, stay_in, send_in, win, wout, ga, gm,
                   x, out, qkv, a, mid, u, p):
    tokens = y_ref.shape[1]
    packed = jnp.concatenate([stay_in[...], send_in[...]], axis=1)
    onehot = roll_matrix(shift_ref[pl.program_id(0)], tokens)
    start = y_ref[...] + permute(packed, onehot, NT)
    x[...] = start
    out[...] = block_forward(start, win, wout, ga[...], gm[...], qkv, a, mid, u, p)


def decoder(shift, y, stay, arrived, win, wout, ga, gm):
    samples, width, tokens = y.shape
    full = jax.ShapeDtypeStruct(y.shape, F32)
    outs = [full, full] + saved_shapes(samples, width, win.shape[0] - 3 * width, tokens)
    weights = [(w, False) for w in (win, wout, ga, gm)]
    return call(
        decoder_kernel, outs, [(y, True), (stay, True), (arrived, True)] + weights,
        [], "decoder", smem=(shift,),
    )


def head_kernel(chans, x_ref, gain, w_ref, t_ref, gx, gw_ref, gg_ref, sums, acc):
    s, k = pl.program_id(0), pl.program_id(1)
    rows = t_ref.shape[0]
    hat, scale = normalise(x_ref[...])
    normed = split(hat * gain[...])

    @pl.when((s == 0) & (k == 0))
    def _():
        gg_ref[...] = jnp.zeros_like(gg_ref)
        sums[...] = jnp.zeros_like(sums)

    weight = split(w_ref[...])
    pred = dot3(weight, normed, TN)
    dps = []
    for at in range(0, rows, CH):
        target = t_ref[at : at + CH, :]
        scaled = target[chans : chans + 1, :]
        differ = jnp.where(iota(target.shape, 0) < chans, pred[at : at + CH, :] - target, 0.0)
        dp = scaled * differ
        sums[0:1, :] += jnp.sum(dp * differ, axis=0, keepdims=True)
        sums[1:2, :] += scaled
        dps.append(dp)
    grad = split(jnp.concatenate(dps, axis=0))
    at = pl.ds(pl.multiple_of(k * rows, rows), rows)
    update = dot3(normed, grad, NT)

    @pl.when(s == 0)
    def _():
        gw_ref[:, at] = update

    @pl.when(s != 0)
    def _():
        gw_ref[:, at] += update

    back = dot3(weight, grad, NN)

    @pl.when(k == 0)
    def _():
        acc[...] = back

    @pl.when(k != 0)
    def _():
        acc[...] += back

    @pl.when(k == pl.num_programs(1) - 1)
    def _():
        dn = acc[...]
        gg_ref[...] += fold(dn * hat)
        gx[...] = normalise_back(dn, hat, scale, gain[...])


def head(x, gain, weight, target, chans):
    samples, width, tokens = x.shape
    depth = weight.shape[1]
    rows = 2 * CH
    stream = pl.BlockSpec((None, width, tokens), lambda s, k: (s, 0, 0))
    fixed = lambda shape: pl.BlockSpec(shape, lambda s, k: (0, 0))
    return pl.pallas_call(
        functools.partial(head_kernel, chans),
        out_shape=[
            jax.ShapeDtypeStruct(x.shape, F32),
            jax.ShapeDtypeStruct(weight.shape, F32),
            jax.ShapeDtypeStruct((width, 128), F32),
            jax.ShapeDtypeStruct((8, tokens), F32),
        ],
        grid=(samples, depth // rows),
        in_specs=[
            stream,
            fixed((width, 1)),
            pl.BlockSpec((width, rows), lambda s, k: (0, k)),
            pl.BlockSpec((None, rows, tokens), lambda s, k: (s, k, 0)),
        ],
        out_specs=[stream, fixed(weight.shape), fixed((width, 128)), fixed((8, tokens))],
        scratch_shapes=[pltpu.VMEM((width, tokens), F32)],
        compiler_params=params(2),
        name="head",
    )(x, gain, weight, target)


def decoder_back_kernel(shift_ref, dy, x, qkv, a, mid, u, p, win, wout, ga, gm,
                        dx, stay, send, gwin, gwout, gga, ggm, da, dqkv):
    tokens = x.shape[1]
    clear(gwin, gwout, gga, ggm)
    grad = block_backward(
        dy[...], x[...], mid, win, wout, ga[...], gm[...], qkv, a, u, p,
        gwin, gwout, gga, ggm, da, dqkv,
    )
    dx[...] = grad
    packed = permute(grad, roll_matrix(shift_ref[pl.program_id(0)], tokens), NN)
    stay[...] = packed[:, : tokens // 2]
    send[...] = packed[:, tokens // 2 :]


def back_scratch(width, tokens):
    return [pltpu.VMEM((width, tokens), F32), pltpu.VMEM((3 * width, tokens), F32)]


def grad_shapes(win, wout):
    gain = jax.ShapeDtypeStruct((win.shape[1], 128), F32)
    return [jax.ShapeDtypeStruct(w.shape, F32) for w in (win, wout)] + [gain, gain]


def decoder_back(shift, dy, x, saved, win, wout, ga, gm):
    samples, width, tokens = x.shape
    half = jax.ShapeDtypeStruct((samples, width, tokens // 2), F32)
    ins = [(v, True) for v in (dy, x, *saved)] + [(w, False) for w in (win, wout, ga, gm)]
    return call(
        decoder_back_kernel, [jax.ShapeDtypeStruct(x.shape, F32), half, half], ins,
        grad_shapes(win, wout), "decoder_back", back_scratch(width, tokens), (shift,),
    )


def merging_back_kernel(stay_in, send_in, x, wide, last, qkv, a, mid, u, p,
                        wup, wback, win, wout, ga, gm,
                        stay, send, gup, gback, gwin, gwout, gga, ggm, da, dqkv):
    tokens = x.shape[1]
    clear(gup, gback, gwin, gwout, gga, ggm)
    order = order_matrix(tokens)
    dz = split(permute(jnp.concatenate([stay_in[...], send_in[...]], axis=1), order, NN))
    gback[...] += dot3(split(last[...]), dz, NT)
    dlast = dot3(split(wback[...]), dz, NN)
    grad = split(block_backward(
        dlast, wide[...], mid, win, wout, ga[...], gm[...], qkv, a, u, p,
        gwin, gwout, gga, ggm, da, dqkv,
    ))
    gup[...] += dot3(grad, split(x[...]), NT)
    lowered = permute(dot3(split(wup[...]), grad, TN), order, NT)
    stay[...] = lowered[:, : tokens // 2]
    send[...] = lowered[:, tokens // 2 :]


def merging_back(stay, arrived, x, wide, last, saved, wup, wback, win, wout, ga, gm):
    width, tokens = wide.shape[1:]
    half = jax.ShapeDtypeStruct(stay.shape, F32)
    ins = [(v, True) for v in (stay, arrived, x, wide, last, *saved)]
    ins += [(w, False) for w in (wup, wback, win, wout, ga, gm)]
    accumulated = [jax.ShapeDtypeStruct(w.shape, F32) for w in (wup, wback)]
    return call(
        merging_back_kernel, [half, half], ins, accumulated + grad_shapes(win, wout),
        "merging_back", back_scratch(width, tokens),
    )


def encoder_back_kernel(shift_ref, dy, stay_in, send_in, x, qkv, a, mid, u, p,
                        win, wout, ga, gm, dx, gwin, gwout, gga, ggm, da, dqkv):
    tokens = x.shape[1]
    clear(gwin, gwout, gga, ggm)
    onehot = roll_matrix(shift_ref[pl.program_id(0)], tokens)
    packed = jnp.concatenate([stay_in[...], send_in[...]], axis=1)
    start = dy[...] + permute(packed, onehot, NT)
    dx[...] = block_backward(
        start, x[...], mid, win, wout, ga[...], gm[...], qkv, a, u, p,
        gwin, gwout, gga, ggm, da, dqkv,
    )


def encoder_back(shift, dy, stay, arrived, x, saved, win, wout, ga, gm):
    samples, width, tokens = x.shape
    ins = [(v, True) for v in (dy, stay, arrived, x, *saved)]
    ins += [(w, False) for w in (win, wout, ga, gm)]
    return call(
        encoder_back_kernel, [jax.ShapeDtypeStruct(x.shape, F32)], ins,
        grad_shapes(win, wout), "encoder_back", back_scratch(width, tokens), (shift,),
    )


def pixel_columns(flat):
    rows, depth = flat.shape
    moved = flat.reshape(rows, depth // 16, 4, 4).transpose(0, 3, 2, 1)
    return jnp.pad(moved, ((0, 0), (0, 0), (0, 0), (0, CH - depth // 16))).reshape(rows, 16 * CH)


def channel_columns(flat, chans):
    rows = flat.shape[0]
    moved = flat.reshape(rows, 4, 4, CH)[..., :chans]
    return moved.transpose(0, 3, 2, 1).reshape(rows, chans * 16)


def shifted(value, axis, by):
    peers = lax.axis_size(axis)
    return lax.ppermute(value, axis, [(i, (i + by) % peers) for i in range(peers)])


def place(values, band_count, band_index):
    full = jnp.zeros((values.shape[0] * band_count,), F32)
    return lax.dynamic_update_slice_in_dim(full, values, band_index * values.shape[0], axis=0)


def gather(shard):
    return lax.all_gather(shard, "lat", axis=0, tiled=True)


def scatter(grad):
    return lax.psum_scatter(grad, "lat", scatter_dimension=0, tiled=True)


def on_device(
    fields, target, valid_mask, sample_index, weight_table, lon_shift, w_embed, w_in, w_out,
    w_merge, w_fin, w_fout, w_head, gains, row_stats, col_stats, v_gain,
):
    band_count = lax.axis_size("lat")
    band_index = lax.axis_index("lat")
    samples, chans, rows_dev, across = fields.shape
    width = w_in.shape[1]
    total_rows = rows_dev * band_count
    pixel_rows = (band_index * rows_dev + jnp.arange(rows_dev)).astype(F32)
    coslat = jnp.cos((90.0 - (pixel_rows + 0.5) * 180.0 / total_rows) * (jnp.pi / 180.0))
    picked = (sample_index[:, None] == jnp.arange(weight_table.shape[0])[None, :]).astype(F32)
    sample_weight = jnp.sum(picked * weight_table[None, :], axis=1)
    weight = sample_weight[:, None, None] * coslat[None, :, None] * valid_mask.astype(F32)

    mats = [
        (w_embed.T, True),
        (w_in[0].T, True),
        (w_in[1].T, True),
        (w_out[0], False),
        (w_out[1], False),
        (w_merge[0].T, True),
        (w_merge[1].T, True),
        (w_fin.T, True),
        (w_fout, False),
        (w_head, False),
    ]
    f_embed = gather(pixel_columns(mats[0][0]))
    f_gains = gather(gains.T).T
    f_in0, f_out0, f_up, f_fin, f_fout, f_back, f_in1, f_out1 = (
        gather(mats[at][0]) for at in (1, 3, 5, 7, 8, 6, 2, 4)
    )
    f_head = gather(pixel_columns(mats[9][0]))
    gain = [f_gains[at].reshape(width, 1) for at in range(5)]
    gain_a, gain_m = f_gains[5:7].reshape(-1, 1), f_gains[7:9].reshape(-1, 1)

    high, low = prep(fields)
    wanted = prep(target, weight)
    stream = embed(f_embed, high, low)
    own, stay, send, *kept_e = encoder(lon_shift, stream, f_in0, f_out0, gain[0], gain[1])
    send = shifted(send, "lat", -1)
    rolled, wide, last, stay, send, *kept_m = merging(
        stay, send, f_up, f_back, f_fin, f_fout, gain_a, gain_m
    )
    send = shifted(send, "lat", 1)
    start, out, *kept_d = decoder(lon_shift, own, stay, send, f_in1, f_out1, gain[2], gain[3])
    grad, g_head, gg_final, sums = head(out, gain[4], f_head, wanted, chans)
    grad, stay, send, g_in1, g_out1, gg_2, gg_3 = decoder_back(
        lon_shift, grad, start, kept_d, f_in1, f_out1, gain[2], gain[3]
    )
    send = shifted(send, "lat", -1)
    stay, send, g_up, g_back, g_fin, g_fout, gg_a, gg_m = merging_back(
        stay, send, rolled, wide, last, kept_m, f_up, f_back, f_fin, f_fout, gain_a, gain_m
    )
    send = shifted(send, "lat", 1)
    grad, g_in0, g_out0, gg_0, gg_1 = encoder_back(
        lon_shift, grad, stay, send, stream, kept_e, f_in0, f_out0, gain[0], gain[1]
    )
    g_embed = embed_back(grad, high, low)

    g_gain = jnp.concatenate(
        [jnp.sum(g, axis=1) for g in (gg_0, gg_1, gg_2, gg_3, gg_final, gg_a, gg_m)]
    ).reshape(gains.shape[0], width)
    total, count = lax.psum(
        (jnp.sum(sums[0]), chans * jnp.sum(sums[1])), ("dp", "lat")
    )
    loss = total / count
    rescale = 2.0 / count
    grads = [g_embed, g_in0, g_in1, g_out0, g_out1, g_up, g_back, g_fin, g_fout, g_head]
    grads = [scatter(g) for g in grads]
    grads, g_gain = lax.psum((grads, scatter(g_gain.T).T), "dp")
    grads[0], grads[9] = channel_columns(grads[0], chans), channel_columns(grads[9], chans)
    grads = [g * rescale for g in grads]
    g_gain = g_gain * rescale

    row_parts, col_parts, wsq_parts = [], [], []
    for (matrix, turned), gradient in zip(mats, grads):
        square = gradient * gradient + 1e-30
        own_sum = place(jnp.sum(square, axis=1) / square.shape[1], band_count, band_index)
        other = jnp.sum(square, axis=0) / (square.shape[0] * band_count)
        row_parts.append(other if turned else own_sum)
        col_parts.append(own_sum if turned else other)
        wsq_parts.append(jnp.sum(matrix * matrix))
    row_means, col_means, weight_sq, gain_wsq = lax.psum(
        (
            jnp.concatenate(row_parts),
            jnp.concatenate(col_parts),
            jnp.stack(wsq_parts),
            jnp.sum(gains * gains, axis=-1),
        ),
        "lat",
    )
    next_rows = 0.5 * row_stats + 0.5 * row_means
    next_cols = 0.5 * col_stats + 0.5 * col_means
    updates, usq_parts = [], []
    row_at, col_at = 0, 0
    for (matrix, turned), gradient in zip(mats, grads):
        rows_l, cols = matrix.shape
        rows = rows_l * band_count
        n_row, n_col = (cols, rows) if turned else (rows, cols)
        row_new, col_new = next_rows[row_at : row_at + n_row], next_cols[col_at : col_at + n_col]
        row_at, col_at = row_at + n_row, col_at + n_col
        row_mean = jnp.mean(row_new)
        mine, other = (col_new, row_new) if turned else (row_new, col_new)
        mine = lax.dynamic_slice_in_dim(mine, band_index * rows_l, rows_l, axis=0)
        update = gradient * lax.rsqrt(mine[:, None] * other[None, :] / row_mean)
        updates.append(update)
        usq_parts.append(jnp.sum(update * update))
    next_v_gain = 0.5 * v_gain + 0.5 * (g_gain * g_gain + 1e-30)
    gain_update = g_gain * lax.rsqrt(next_v_gain)
    update_sq, gain_usq = lax.psum(
        (jnp.stack(usq_parts), jnp.sum(gain_update * gain_update, axis=-1)), "lat"
    )

    def finish(matrix, update, update_sq, weight_sq, entries):
        rms_update = jnp.sqrt(update_sq / entries)
        update = update / jnp.maximum(1.0, rms_update / 0.25)
        rms_weight = jnp.sqrt(weight_sq / entries)
        return matrix - jnp.maximum(0.001, rms_weight) * update

    new = []
    for at, ((matrix, turned), update) in enumerate(zip(mats, updates)):
        entries = matrix.size * band_count
        result = finish(matrix, update, update_sq[at], weight_sq[at], entries)
        new.append(result.T if turned else result)
    new_gains = finish(
        gains, gain_update, gain_usq[:, None], gain_wsq[:, None], gains.shape[1] * band_count
    )
    results = [
        new[0], jnp.stack(new[1:3]), jnp.stack(new[3:5]), jnp.stack(new[5:7]),
        new[7], new[8], new[9], new_gains,
    ]
    copies = [r.astype(BF16) for r in results]
    return (loss, *results, next_rows, next_cols, next_v_gain, *copies)


def solution(mesh):
    placed = (
        P("dp", None, "lat", None),
        P("dp", None, "lat", None),
        P("dp", "lat", None),
        P("dp"),
        P(),
        P("dp"),
        P(None, "lat"),
        P(None, None, "lat"),
        P(None, "lat", None),
        P(None, None, "lat"),
        P(None, "lat"),
        P("lat", None),
        P("lat", None),
        P(None, "lat"),
        P(),
        P(),
        P(None, "lat"),
    )
    weights = placed[6:14]
    return jax.shard_map(
        on_device,
        mesh=mesh,
        in_specs=placed,
        out_specs=(P(), *weights, P(), P(), P(None, "lat"), *weights),
        check_vma=False,
    )
```

```python
import functools
import math

import jax
import jax.numpy as jnp
from jax import lax
from jax.experimental import pallas as pl
from jax.experimental.pallas import tpu as pltpu
from jax.sharding import PartitionSpec as P

F32 = jnp.float32
BF16 = jnp.bfloat16
HEAD = 32
PATCH = 4
WR = 4
WC = 16
CH = 192
VMEM = 60 * 1024 * 1024
ROOT = math.sqrt(2.0 / math.pi)
NN, NT, TN = (1, 0), (1, 1), (0, 0)


def takes(us):
    return pl.CostEstimate(
        flops=int(us * 1.15e9), bytes_accessed=int(us * 3.69e6), transcendentals=0
    )


def params(steps):
    return pltpu.CompilerParams(
        dimension_semantics=("arbitrary",) * steps, vmem_limit_bytes=VMEM
    )


def split(value):
    high = value.astype(BF16)
    return high, (value - high.astype(F32)).astype(BF16)


def dg(a, b, dims):
    return lax.dot_general(
        a, b, (((dims[0],), (dims[1],)), ((), ())), preferred_element_type=F32
    )


def dot3(a, b, dims):
    return dg(a[0], b[0], dims) + (dg(a[0], b[1], dims) + dg(a[1], b[0], dims))


def normalise(stream):
    centred = stream - jnp.mean(stream, axis=0, keepdims=True)
    scale = lax.rsqrt(jnp.mean(centred * centred, axis=0, keepdims=True) + 1e-05)
    return centred * scale, scale


def normalise_back(grad, hat, scale, gain):
    weighted = grad * gain
    return scale * (
        weighted
        - jnp.mean(weighted, axis=0, keepdims=True)
        - hat * jnp.mean(weighted * hat, axis=0, keepdims=True)
    )


def iota(shape, axis):
    return lax.broadcasted_iota(jnp.int32, shape, axis)


def roll_matrix(shift, tokens):
    lane = iota((tokens, tokens), 0)
    out = iota((tokens, tokens), 1)
    half, inner = out // (tokens // 2), out % (tokens // 2)
    row = jnp.where(half == 0, 2, 0) + (inner // WC) % 2
    columns = tokens // WR
    moved = ((inner // (2 * WC)) * WC + inner % WC + shift) % columns
    source = (moved // WC) * (WR * WC) + row * WC + moved % WC
    return (lane == source).astype(BF16)


def order_matrix(tokens):
    lane = iota((tokens, tokens), 0)
    out = iota((tokens, tokens), 1)
    window, row, col = out // (WR * WC), (out // WC) % WR, out % WC
    source = (row // 2) * (tokens // 2) + window * (2 * WC) + (row % 2) * WC + col
    return (lane == source).astype(BF16)


def permute(value, onehot, dims):
    high, low = split(value)
    rest = (value - high.astype(F32) - low.astype(F32)).astype(BF16)
    return dg(high, onehot, dims) + (dg(low, onehot, dims) + dg(rest, onehot, dims))


def pixel_matrix():
    lane = iota((512, 512), 0)
    out = iota((512, 512), 1)
    b, window, row, col = out // 128, (out // 64) % 2, (out // 16) % 4, out % 16
    return (lane == row * 128 + window * 64 + col * 4 + b).astype(BF16)


def prep_kernel(chans, with_weight, *refs):
    if with_weight:
        x_ref, w_ref, out_ref, perm = refs
    else:
        x_ref, hi_ref, lo_ref, perm = refs
    block = 64

    @pl.when((pl.program_id(0) == 0) & (pl.program_id(1) == 0) & (pl.program_id(2) == 0))
    def _():
        perm[...] = pixel_matrix()

    row = iota((block, 512), 0) + pl.program_id(2) * block
    tiles = []
    for a in range(PATCH):
        tile = jnp.concatenate(
            [x_ref[pl.ds(4 * r + a, block, stride=16), :] for r in range(WR)], axis=1
        )
        tile = jnp.where(row < chans, tile, 0.0)
        if with_weight:
            extra = jnp.concatenate([w_ref[4 * r + a : 4 * r + a + 1, :] for r in range(WR)], axis=1)
            tile = jnp.where(row == chans, extra, tile)
        tiles.append(tile)
    high, low = split(jnp.concatenate(tiles, axis=0))
    moved = dg(jnp.concatenate([high, low], axis=0), perm[...], NN)
    for a in range(PATCH):
        for b in range(PATCH):
            at, piece = a * block, slice(b * 128, b * 128 + 128)
            above, below = moved[at : at + block, piece], moved[at + 256 : at + 256 + block, piece]
            if with_weight:
                out_ref[b, a] = above + below
            else:
                hi_ref[b, a] = above.astype(BF16)
                lo_ref[b, a] = below.astype(BF16)


def prep(fields, weight=None):
    samples, chans, height, across = fields.shape
    flat = fields.reshape(samples, chans * height, across)
    padded = 192
    shape = (samples, 4, 4, padded, across)
    spec = pl.BlockSpec((None, 4, 4, 64, 128), lambda s, p, c: (s, 0, 0, c, p))
    in_specs = [pl.BlockSpec((None, 64 * height, 128), lambda s, p, c: (s, c, p))]
    if weight is not None:
        in_specs.append(pl.BlockSpec((None, height, 128), lambda s, p, c: (s, 0, p)))
        out_shape, out_specs = jax.ShapeDtypeStruct(shape, F32), spec
    else:
        out_shape = [jax.ShapeDtypeStruct(shape, BF16)] * 2
        out_specs = [spec] * 2
    outs = pl.pallas_call(
        functools.partial(prep_kernel, chans, weight is not None),
        out_shape=out_shape,
        grid=(samples, across // 128, padded // 64),
        in_specs=in_specs,
        out_specs=out_specs,
        scratch_shapes=[pltpu.VMEM((512, 512), BF16)],
        compiler_params=params(3),
        cost_estimate=takes(22),
        name="prep",
    )(*([flat] if weight is None else [flat, weight]))
    return jax.tree.map(lambda a: a.reshape(samples, 16 * padded, across), outs)


def embed_kernel(w_ref, hi_ref, lo_ref, out_ref):
    total = None
    rows = w_ref.shape[2]
    for k in range(w_ref.shape[0]):
        at = slice(k * rows, k * rows + rows)
        part = dot3(split(w_ref[k]), (hi_ref[at, :], lo_ref[at, :]), NN)
        total = part if total is None else total + part
    out_ref[...] = total


def embed(weight, high, low):
    samples, depth, tokens = high.shape
    width = weight.shape[1]
    big = pl.BlockSpec((None, depth, tokens), lambda s: (s, 0, 0))
    return pl.pallas_call(
        embed_kernel,
        out_shape=jax.ShapeDtypeStruct((width, samples * tokens), F32),
        grid=(samples,),
        in_specs=[pl.BlockSpec(weight.shape, lambda s: (0, 0, 0)), big, big],
        out_specs=pl.BlockSpec((width, tokens), lambda s: (0, s)),
        compiler_params=params(1),
        cost_estimate=takes(10),
        name="embed",
    )(weight, high, low)


def put_bands(out_ref, value):
    rows = out_ref.shape[1]
    for band in range(out_ref.shape[0]):
        out_ref[band] = value[band * rows : band * rows + rows, :]


def embed_back_kernel(g_ref, hi_ref, lo_ref, out_ref):
    samples, _, tokens = hi_ref.shape
    total = None
    for s in range(samples):
        part = dot3(split(g_ref[:, s * tokens : s * tokens + tokens]), (hi_ref[s], lo_ref[s]), NT)
        total = part if total is None else total + part
    put_bands(out_ref, total)


def embed_back(grad, high, low, bands):
    samples, depth, tokens = high.shape
    width = grad.shape[0]
    rows = 2 * CH
    big = pl.BlockSpec((samples, rows, tokens), lambda k: (0, k, 0))
    return pl.pallas_call(
        embed_back_kernel,
        out_shape=jax.ShapeDtypeStruct((bands, depth // rows * width // bands, rows), F32),
        grid=(depth // rows,),
        in_specs=[pl.BlockSpec(grad.shape, lambda k: (0, 0)), big, big],
        out_specs=pl.BlockSpec((bands, width // bands, rows), lambda k: (0, k, 0)),
        compiler_params=params(1),
        cost_estimate=takes(12),
        name="embed_back",
    )(grad, high, low)


def rows_of(at, count):
    return pl.ds(pl.multiple_of(at * count, 16), count)


def chunk_of(rows):
    return next(c for c in (384, 288, 192) if rows % c == 0)


def loop(rows, body):
    count = chunk_of(rows)

    def step(at, carry):
        body(at, count)
        return carry

    lax.fori_loop(0, rows // count, step, 0)


def put(pair, value):
    pair[0][...], pair[1][...] = split(value)


def both(pair):
    return pair[0][...], pair[1][...]


def spread(compact, first):
    high, low = split(compact)
    zero = jnp.zeros_like(high)
    grow = lambda v: jnp.concatenate(
        [jnp.where(first, v, zero), jnp.where(first, zero, v)], axis=0
    )
    return grow(high), grow(low)


def thrice(high, low):
    above = jnp.concatenate([high, high], axis=1)
    return jnp.concatenate([above, jnp.concatenate([low, jnp.zeros_like(low)], axis=1)], axis=0)


def halves(value):
    return value[:HEAD] + value[HEAD:]


def head_rows(width, part, head):
    return slice(part * width + head * HEAD, part * width + head * HEAD + HEAD)


def attend(qkv, out, weights, width):
    heads = width // HEAD
    first = iota((64, 128), 1) < 64

    def body(pair, carry):
        lanes = pl.ds(pl.multiple_of(pair * 128, 128), 128)
        scores = []
        for h in range(heads):
            qh, ql = split(qkv[head_rows(width, 0, h), lanes] * HEAD**-0.5)
            kh, kl = split(qkv[head_rows(width, 1, h), lanes])
            full = dg(
                jnp.concatenate([kh, kh, kl], axis=0), jnp.concatenate([qh, ql, qh], axis=0), TN
            )
            scores.append(jnp.where(first, full[:64], full[64:]))
        scores = jnp.stack(scores)
        scores = jnp.exp(scores - jnp.max(scores, axis=1, keepdims=True))
        scores = scores * (1.0 / jnp.sum(scores, axis=1, keepdims=True))
        weights[pair] = scores
        for h in range(heads):
            values = thrice(*split(qkv[head_rows(width, 2, h), lanes]))
            full = jnp.concatenate(spread(scores[h], first), axis=0)
            out[head_rows(width, 0, h), lanes] = halves(dg(values, full, NN))
        return carry

    lax.fori_loop(0, weights.shape[0], body, 0)


def attend_back(qkv, weights, grad, high_out, low_out, width):
    heads = width // HEAD
    first = iota((64, 128), 1) < 64
    group = 6

    def body(at, carry):
        pair, base = at // (heads // group), (at % (heads // group)) * group
        lanes = pl.ds(pl.multiple_of(pair * 128, 128), 128)
        where = lambda part, h: pl.ds(
            pl.multiple_of(part * width + (base + h) * HEAD, HEAD), HEAD
        )
        def keep(part, h, value):
            rows = where(part, h)
            high_out[rows, lanes], low_out[rows, lanes] = split(value)

        dp = []
        for h in range(group):
            vh, vl = split(qkv[where(2, h), lanes])
            oh, ol = split(grad[where(0, h), lanes])
            full = dg(
                jnp.concatenate([vh, vh, vl], axis=0), jnp.concatenate([oh, ol, oh], axis=0), TN
            )
            dp.append(jnp.where(first, full[:64], full[64:]))
        dp = jnp.stack(dp)
        p = weights[pair, pl.ds(base, group)]
        ds = p * (dp - jnp.sum(dp * p, axis=1, keepdims=True))
        for h in range(group):
            full = jnp.concatenate(spread(p[h], first), axis=1)
            values = thrice(*split(grad[where(0, h), lanes]))
            keep(2, h, halves(dg(values, full, NT)))
        for h in range(group):
            high, low = spread(ds[h], first)
            keys = thrice(*split(qkv[where(1, h), lanes]))
            queries = thrice(*split(qkv[where(0, h), lanes] * HEAD**-0.5))
            full = dg(keys, jnp.concatenate([high, low], axis=0), NN)
            keep(0, h, halves(full) * HEAD**-0.5)
            full = dg(queries, jnp.concatenate([high, low], axis=1), NT)
            keep(1, h, halves(full))
        return carry

    lax.fori_loop(0, weights.shape[0] * (heads // group), body, 0)


def gelu_parts(u):
    t = jnp.tanh(ROOT * (u + 0.044715 * u * u * u))
    return 0.5 * u * (1.0 + t), t


def lane_sums(value):
    column = jnp.sum(value, axis=1, keepdims=True)
    shape = (value.shape[0],) * 2
    return jnp.sum(jnp.where(iota(shape, 0) == iota(shape, 1), column, 0.0), axis=0, keepdims=True)


def saved_shapes(width, hidden, tokens):
    return [
        (3 * width, tokens),
        (width, tokens),
        (width, tokens),
        (hidden, tokens),
        (tokens // 128, width // HEAD, 64, 128),
    ]


def forward_scratch(width, hidden, tokens):
    scratch = [pltpu.VMEM(s, F32) for s in saved_shapes(width, hidden, tokens)]
    scratch += [pltpu.VMEM((width, tokens), BF16)] * 2 + [pltpu.VMEM((hidden, tokens), BF16)] * 2
    return scratch + [pltpu.SemaphoreType.DMA((5,))]


def block_forward(x, win, wout, ga, gm, kept, scratch):
    qkv, out, mid, hidden, weights, nh, nl, hh, hl, sems = scratch
    width = x.shape[0]
    copies = [
        pltpu.make_async_copy(v, k, sems.at[i])
        for i, (v, k) in enumerate(zip((qkv, out, mid, hidden, weights), kept))
    ]
    put((nh, nl), normalise(x)[0] * ga)

    def project(at, count):
        rows = rows_of(at, count)
        qkv[rows, :] = dot3(split(win[rows, :]), both((nh, nl)), NN)

    loop(3 * width, project)
    copies[0].start()
    attend(qkv, out, weights, width)
    copies[1].start()
    copies[4].start()
    mid[...] = x + dot3(split(wout[:width, :]), split(out[...]), TN)
    copies[2].start()
    put((nh, nl), normalise(mid[...])[0] * gm)

    def feed(at, count):
        rows = rows_of(at, count)
        from_rows = pl.ds(pl.multiple_of(3 * width + at * count, 16), count)
        u = dot3(split(win[from_rows, :]), both((nh, nl)), NN)
        hidden[rows, :] = u
        hh[rows, :], hl[rows, :] = split(gelu_parts(u)[0])

    loop(hidden.shape[0], feed)
    copies[3].start()
    return mid[...] + dot3(split(wout[width:, :]), both((hh, hl)), TN), copies


def backward_scratch(width, hidden, tokens):
    scratch = [pltpu.VMEM(s, F32) for s in saved_shapes(width, hidden, tokens)]
    scratch += [pltpu.VMEM((width, tokens), F32)]
    scratch += [pltpu.VMEM((width, tokens), BF16)] * 4 + [pltpu.VMEM((hidden, tokens), BF16)] * 2
    return scratch + [pltpu.SemaphoreType.DMA((5,))]


def fetch(kept, slots, sems):
    copies = [
        pltpu.make_async_copy(k, v, sems.at[i]) for i, (k, v) in enumerate(zip(kept, slots))
    ]
    for copy in copies:
        copy.start()
    return copies


def mlp_back(dy, win, wout, gm, copies, slots, pairs, da, gwin, gwout, ggm):
    mid, hidden, out = slots
    norm, grad, wide = pairs
    width = dy.shape[0]
    put(grad, dy)
    copies[0].wait()
    hat, scale = normalise(mid[...])
    put(norm, hat * gm)
    copies[1].wait()

    def feed(at, count):
        rows = rows_of(at, count)
        out_rows = pl.ds(pl.multiple_of(width + at * count, 16), count)
        u = hidden[rows, :]
        value, t = gelu_parts(u)
        slope = 0.5 * (1.0 + t) + 0.5 * ROOT * u * (1.0 - t * t) * (1.0 + 3 * 0.044715 * u * u)
        gwout[out_rows, :] = dot3(split(value), both(grad), NT)
        du = split(slope * dot3(split(wout[out_rows, :]), both(grad), NN))
        wide[0][rows, :], wide[1][rows, :] = du
        gwin[rows, :] = dot3(du, both(norm), NT)

    loop(hidden.shape[0], feed)
    dn = dot3(split(win[...]), both(wide), TN)
    ggm[...] = lane_sums(dn * hat)
    dmid = dy + normalise_back(dn, hat, scale, gm)
    put(grad, dmid)
    da[...] = dot3(split(wout[:width, :]), both(grad), NN)
    copies[2].wait()
    gwout[:width, :] = dot3(split(out[...]), both(grad), NT)
    return dmid


def attention_back(dmid, x, win, ga, copies, slots, pairs, da, gwin, gga):
    weights, qkv = slots
    norm, wide = pairs
    width = x.shape[0]
    for copy in copies:
        copy.wait()
    attend_back(qkv, weights, da, *wide, width)
    hat, scale = normalise(x)
    put(norm, hat * ga)

    def project(at, count):
        rows = rows_of(at, count)
        gwin[rows, :] = dot3((wide[0][rows, :], wide[1][rows, :]), both(norm), NT)

    loop(3 * width, project)
    grads = wide[0][: 3 * width, :], wide[1][: 3 * width, :]
    dn = dot3(split(win[...]), grads, TN)
    gga[...] = lane_sums(dn * hat)
    return dmid + normalise_back(dn, hat, scale, ga)


def block_backward(dy, x, win, wout, ga, gm, kept, scratch, gwin, gwout, gga, ggm):
    qkv, out, mid, hidden, weights, da, nh, nl, yh, yl, hh, hl, _ = scratch
    at = 3 * x.shape[0]
    norm, grad, wide = (nh, nl), (yh, yl), (hh, hl)
    dmid = mlp_back(
        dy, win.at[at:], wout, gm, kept[:3], (mid, hidden, out), (norm, grad, wide), da,
        gwin.at[at:], gwout, ggm,
    )
    return attention_back(
        dmid, x, win.at[:at], ga, kept[3:], (weights, qkv), (norm, wide), da, gwin.at[:at], gga
    )


def fetch_block(kept, scratch):
    order = (2, 3, 1, 4, 0)
    return fetch([kept[i] for i in order], [scratch[i] for i in order], scratch[-1])


def call(body, outs, ins, kept_in=(), kept_out=(), scratch=(), smem=(), name=None, aliases=None, cost=4):
    vmem = pl.BlockSpec(memory_space=pltpu.VMEM)
    hbm = pl.BlockSpec(memory_space=pl.ANY)
    shape = lambda s: jax.ShapeDtypeStruct(tuple(s), F32)
    return pl.pallas_call(
        body,
        out_shape=[shape(s) for s in (*outs, *kept_out)],
        in_specs=[pl.BlockSpec(memory_space=pltpu.SMEM)] * len(smem)
        + [vmem] * len(ins)
        + [hbm] * len(kept_in),
        out_specs=[vmem] * len(outs) + [hbm] * len(kept_out),
        scratch_shapes=list(scratch),
        input_output_aliases=aliases or {},
        cost_estimate=takes(cost),
        compiler_params=pltpu.CompilerParams(vmem_limit_bytes=VMEM),
        name=name,
    )(*smem, *ins, *kept_in)


def pack(shift_ref, value, stay, send):
    samples = shift_ref.shape[0]
    tokens = value.shape[1] // samples
    for s in range(samples):
        part = value[:, s * tokens : s * tokens + tokens]
        moved = permute(part, roll_matrix(shift_ref[s], tokens), NN)
        stay[s] = moved[:, : tokens // 2]
        send[s] = moved[:, tokens // 2 :]


def unpack(shift_ref, stay, send):
    parts = []
    for s in range(stay.shape[0]):
        joined = jnp.concatenate([stay[s], send[s]], axis=1)
        parts.append(permute(joined, roll_matrix(shift_ref[s], joined.shape[1]), NT))
    return jnp.concatenate(parts, axis=1)


def to_windows(stay, send):
    parts = [jnp.concatenate([stay[s], send[s]], axis=1) for s in range(stay.shape[0])]
    order = order_matrix(parts[0].shape[1])
    return jnp.concatenate([permute(p, order, NN) for p in parts], axis=1)


def from_windows(value, stay, send):
    tokens = value.shape[1] // stay.shape[0]
    order = order_matrix(tokens)
    for s in range(stay.shape[0]):
        moved = permute(value[:, s * tokens : s * tokens + tokens], order, NT)
        stay[s] = moved[:, : tokens // 2]
        send[s] = moved[:, tokens // 2 :]


def half_shape(shift, width, tokens):
    samples = shift.shape[0]
    return (samples, width, tokens // samples // 2)


def encoder_kernel(shift, x, win, wout, ga, gm, y, stay, send, *rest):
    out, copies = block_forward(x[...], win, wout, ga[...], gm[...], rest[:5], rest[5:])
    y[...] = out
    pack(shift, out, stay, send)
    for copy in copies:
        copy.wait()


def encoder(shift, x, win, wout, ga, gm):
    width, tokens = x.shape
    hidden = win.shape[0] - 3 * width
    half = half_shape(shift, width, tokens)
    return call(
        encoder_kernel, [x.shape, half, half], [x, win, wout, ga, gm],
        kept_out=saved_shapes(width, hidden, tokens),
        scratch=forward_scratch(width, hidden, tokens), smem=[shift], name="encoder", cost=14,
    )


def merging_kernel(stay_in, send_in, wup, wback, win, wout, ga, gm, x, wide, last, stay, send, *rest):
    start = to_windows(stay_in, send_in)
    x[...] = start
    raised = dot3(split(wup[...]), split(start), NN)
    wide[...] = raised
    out, copies = block_forward(raised, win, wout, ga[...], gm[...], rest[:5], rest[5:])
    last[...] = out
    from_windows(dot3(split(wback[...]), split(out), TN), stay, send)
    for copy in copies:
        copy.wait()


def merging(stay, arrived, wup, wback, win, wout, ga, gm):
    samples, narrow, half = stay.shape
    width, tokens = wup.shape[0], samples * 2 * half
    hidden = win.shape[0] - 3 * width
    wide = (width, tokens)
    return call(
        merging_kernel, [(narrow, tokens), wide, wide, stay.shape, stay.shape],
        [stay, arrived, wup, wback, win, wout, ga, gm],
        kept_out=saved_shapes(width, hidden, tokens),
        scratch=forward_scratch(width, hidden, tokens), name="merging", cost=32,
    )


def decoder_kernel(shift, y, stay_in, send_in, win, wout, ga, gm, x, last, *rest):
    start = y[...] + unpack(shift, stay_in, send_in)
    x[...] = start
    out, copies = block_forward(start, win, wout, ga[...], gm[...], rest[:5], rest[5:])
    last[...] = out
    for copy in copies:
        copy.wait()


def decoder(shift, y, stay, arrived, win, wout, ga, gm):
    width, tokens = y.shape
    hidden = win.shape[0] - 3 * width
    return call(
        decoder_kernel, [y.shape, y.shape], [y, stay, arrived, win, wout, ga, gm],
        kept_out=saved_shapes(width, hidden, tokens),
        scratch=forward_scratch(width, hidden, tokens), smem=[shift], name="decoder", cost=15,
    )


def gain_shape(win):
    return (1, win.shape[1])


def decoder_back_kernel(shift, dy, x, win, wout, ga, gm, *rest):
    kept, (dx, stay, send, gwin, gwout, gga, ggm), scratch = rest[:5], rest[5:12], rest[12:]
    copies = fetch_block(kept, scratch)
    grad = block_backward(
        dy[...], x[...], win, wout, ga[...], gm[...], copies, scratch, gwin, gwout, gga, ggm
    )
    dx[...] = grad
    pack(shift, grad, stay, send)


def decoder_back(shift, dy, x, saved, win, wout, ga, gm):
    width, tokens = x.shape
    half = half_shape(shift, width, tokens)
    return call(
        decoder_back_kernel,
        [x.shape, half, half, win.shape, wout.shape, gain_shape(win), gain_shape(win)],
        [dy, x, win, wout, ga, gm], kept_in=saved,
        scratch=backward_scratch(width, win.shape[0] - 3 * width, tokens),
        smem=[shift], name="decoder_back", cost=24,
    )


def merging_mlp_back_kernel(stay_in, send_in, last, wback, win, wout, gm, *rest):
    kept, (gback, gwout, ggm, dmid, da, gwin_out), scratch = rest[:3], rest[3:9], rest[9:]
    *slots, nh, nl, yh, yl, hh, hl, gwin, sems, sem = scratch
    copies = fetch(kept, slots, sems)
    dz = split(to_windows(stay_in, send_in))
    gback[...] = dot3(split(last[...]), dz, NT)
    dlast = dot3(split(wback[...]), dz, NN)
    at = win.shape[0] - gwin.shape[0]
    dmid[...] = mlp_back(
        dlast, win.at[at:], wout, gm[...], copies, slots, ((nh, nl), (yh, yl), (hh, hl)), da,
        gwin, gwout, ggm,
    )
    copy = pltpu.make_async_copy(gwin, gwin_out.at[at:], sem)
    copy.start()
    copy.wait()


def merging_mlp_back(stay, arrived, last, saved, wback, win, wout, gm):
    width, tokens = last.shape
    hidden = win.shape[0] - 3 * width
    wide = (width, tokens)
    scratch = [pltpu.VMEM(s, F32) for s in (wide, (hidden, tokens), wide)]
    scratch += [pltpu.VMEM(wide, BF16)] * 4 + [pltpu.VMEM((hidden, tokens), BF16)] * 2
    scratch += [pltpu.VMEM((hidden, width), F32), pltpu.SemaphoreType.DMA((3,)), pltpu.SemaphoreType.DMA]
    return call(
        merging_mlp_back_kernel, [wback.shape, wout.shape, gain_shape(win), wide, wide],
        [stay, arrived, last, wback, win, wout, gm],
        kept_in=[saved[2], saved[3], saved[1]], kept_out=[win.shape], scratch=scratch,
        name="merging_mlp_back", cost=36,
    )


def merging_attention_back_kernel(dmid, da, x, wide_x, wup, ga, *rest):
    (p_in, qkv_in, win_in, _), (stay, send, gup, gga, gwin_out) = rest[:4], rest[4:9]
    weights, qkv, win, nh, nl, hh, hl, gwin, sems, sem = rest[9:]
    copies = fetch([p_in, qkv_in, win_in.at[: win.shape[0]]], [weights, qkv, win], sems)
    grad = attention_back(
        dmid[...], wide_x[...], win, ga[...], copies, (weights, qkv), ((nh, nl), (hh, hl)), da,
        gwin, gga,
    )
    copy = pltpu.make_async_copy(gwin, gwin_out.at[: gwin.shape[0]], sem)
    copy.start()
    grad = split(grad)
    gup[...] = dot3(grad, split(x[...]), NT)
    from_windows(dot3(split(wup[...]), grad, TN), stay, send)
    copy.wait()


def merging_attention_back(dmid, da, x, wide_x, saved, wup, win, ga, gwin, halved):
    width, tokens = wide_x.shape
    rows = 3 * width
    scratch = [pltpu.VMEM(saved[4].shape, F32), pltpu.VMEM(saved[0].shape, F32)]
    scratch += [pltpu.VMEM((rows, width), F32)] + [pltpu.VMEM((width, tokens), BF16)] * 2
    scratch += [pltpu.VMEM((rows, tokens), BF16)] * 2 + [pltpu.VMEM((rows, width), F32)]
    return call(
        merging_attention_back_kernel, [halved, halved, wup.shape, gain_shape(win)],
        [dmid, da, x, wide_x, wup, ga], kept_in=[saved[4], saved[0], win, gwin],
        kept_out=[win.shape],
        scratch=scratch + [pltpu.SemaphoreType.DMA((3,)), pltpu.SemaphoreType.DMA],
        name="merging_attention_back", cost=27, aliases={9: 4},
    )


def encoder_back_kernel(shift, dy, stay_in, send_in, x, win, wout, ga, gm, *rest):
    kept, (dx, gwin, gwout, gga, ggm), scratch = rest[:5], rest[5:10], rest[10:]
    copies = fetch_block(kept, scratch)
    start = dy[...] + unpack(shift, stay_in, send_in)
    dx[...] = block_backward(
        start, x[...], win, wout, ga[...], gm[...], copies, scratch, gwin, gwout, gga, ggm
    )


def encoder_back(shift, dy, stay, arrived, x, saved, win, wout, ga, gm):
    width, tokens = x.shape
    return call(
        encoder_back_kernel,
        [x.shape, win.shape, wout.shape, gain_shape(win), gain_shape(win)],
        [dy, stay, arrived, x, win, wout, ga, gm], kept_in=saved,
        scratch=backward_scratch(width, win.shape[0] - 3 * width, tokens),
        smem=[shift], name="encoder_back", cost=23,
    )


def head_kernel(chans, x_ref, gain, w_ref, t_ref, gx, gw_ref, gg_ref, sums, nh, nl, dh, dl, acc, loss):
    k = pl.program_id(0)
    samples, rows, tokens = t_ref.shape

    @pl.when(k == 0)
    def _():
        put((nh, nl), normalise(x_ref[...])[0] * gain[...])
        loss[...] = jnp.zeros_like(loss)
        acc[...] = jnp.zeros_like(acc)

    weight = split(w_ref[...])
    pred = dot3(weight, both((nh, nl)), TN)
    for s in range(samples):
        lanes = slice(s * tokens, s * tokens + tokens)
        for at in range(0, rows, CH):
            target = t_ref[s, at : at + CH, :]
            scaled = target[chans : chans + 1, :]
            differ = pred[at : at + CH, lanes] - target
            differ = jnp.where(iota(target.shape, 0) < chans, differ, 0.0)
            dp = scaled * differ
            loss[0:1, :] += jnp.sum(dp * differ, axis=0, keepdims=True)
            loss[1:2, :] += scaled
            dh[at : at + CH, lanes], dl[at : at + CH, lanes] = split(dp)
    put_bands(gw_ref, dot3(both((nh, nl)), both((dh, dl)), NT))
    acc[...] += dot3(weight, both((dh, dl)), NN)

    @pl.when(k == pl.num_programs(0) - 1)
    def _():
        hat, scale = normalise(x_ref[...])
        dn = acc[...]
        gg_ref[...] = lane_sums(dn * hat)
        gx[...] = normalise_back(dn, hat, scale, gain[...])
        sums[...] = jnp.sum(loss[...], axis=1, keepdims=True) + jnp.zeros_like(sums)


def head(x, gain, weight, target, chans, bands):
    samples, _, tokens = target.shape
    width = x.shape[0]
    chunks, _, rows = weight.shape
    fixed = lambda shape: pl.BlockSpec(shape, lambda k: (0,) * len(shape))
    piece = pl.BlockSpec((None, width, rows), lambda k: (k, 0, 0))
    return pl.pallas_call(
        functools.partial(head_kernel, chans),
        out_shape=[
            jax.ShapeDtypeStruct(x.shape, F32),
            jax.ShapeDtypeStruct((bands, chunks * width // bands, rows), F32),
            jax.ShapeDtypeStruct((1, width), F32),
            jax.ShapeDtypeStruct((8, 128), F32),
        ],
        grid=(chunks,),
        in_specs=[
            fixed(x.shape),
            fixed((width, 1)),
            piece,
            pl.BlockSpec((samples, rows, tokens), lambda k: (0, k, 0)),
        ],
        out_specs=[
            fixed(x.shape),
            pl.BlockSpec((bands, width // bands, rows), lambda k: (0, k, 0)),
            fixed((1, width)),
            fixed((8, 128)),
        ],
        scratch_shapes=[pltpu.VMEM(x.shape, BF16)] * 2
        + [pltpu.VMEM((rows, x.shape[1]), BF16)] * 2
        + [pltpu.VMEM(x.shape, F32), pltpu.VMEM((8, tokens), F32)],
        compiler_params=params(1),
        cost_estimate=takes(25),
        name="head",
    )(x, gain, weight, target)


def swap(value, axis, bit):
    return lax.ppermute(value, axis, [(i, i ^ bit) for i in range(lax.axis_size(axis))])


def pick(value, at, axis):
    return lax.dynamic_index_in_dim(value, at, axis, keepdims=False)


def place_of():
    lat, dp = lax.axis_index("lat"), lax.axis_index("dp")
    return lat // 2, lat % 2, dp // 2, dp % 2


def along(first, last):
    return [(2 * k + y, 2 * (k + 1) + y) for k in range(first, last) for y in range(2)]


def backwards(pairs):
    return [(7 - a, 7 - b) for a, b in pairs]


def line_sum(parts, z, meanwhile=()):
    right = left = None
    for step in (1, 2, 3):
        ahead = pick(parts, jnp.clip(z + 4 - step, 0, 3), 0)
        behind = pick(parts, jnp.clip(z + step - 4, 0, 3), 0)
        if right is not None:
            ahead, behind = ahead + right, behind + left
        right = lax.ppermute(ahead, "lat", along(0, step))
        left = lax.ppermute(behind, "lat", backwards(along(0, step)))
        if step <= len(meanwhile):
            right, left = tie((right, left), meanwhile[step - 1])
    return pick(parts, z, 0) + right + left


def ordered(mine, other, which, axis=0):
    shape = mine.shape
    at = jnp.arange(2).reshape((1,) * axis + (2,) + (1,) * (mine.ndim - axis))
    joined = jnp.where(at == which, jnp.expand_dims(mine, axis), jnp.expand_dims(other, axis))
    return joined.reshape(shape[:axis] + (2 * shape[axis],) + shape[axis + 1 :])


def core_half(buf, beside=None):
    bands, rows, lanes = buf.shape
    c = place_of()[3]
    parts = buf.reshape(8, 2, rows // 2, lanes)
    return pick(parts, c, 1) + tie(swap(pick(parts, 1 - c, 1), "dp", 1), beside)


def x_half(buf, beside=None):
    bands, rows, lanes = buf.shape
    x = place_of()[2]
    parts = buf.reshape(8, 2, rows // 2, lanes)
    return pick(parts, x, 1) + tie(swap(pick(parts, 1 - x, 1), "dp", 2), beside)


def y_half(buf, beside=None):
    bands, rows, lanes = buf.shape
    y = place_of()[1]
    parts = buf.reshape(4, 2, rows, lanes)
    return pick(parts, y, 1) + tie(swap(pick(parts, 1 - y, 1), "lat", 1), beside)


def over_x(quarters, sums):
    x = place_of()[2]
    return [ordered(v, swap(v, "dp", 2), x) for v in quarters] + [v + swap(v, "dp", 2) for v in sums]


def collect_kernel(sizes, core, *refs):
    halves_in, outs = refs[:10], refs[10:]
    first = core[0] == 0

    def joined(at):
        mine, got = halves_in[at][...], halves_in[at + 5][...]
        return jnp.concatenate([jnp.where(first, mine, got), jnp.where(first, got, mine)], axis=0)

    embed_o, in0_o, in1_o, out0_o, out1_o, up_o, back_o, fin_o, fout_o, head_o, extra_o = outs
    n_fin, n_in, n_out = sizes
    width = in0_o.shape[1]
    rows = embed_o.shape[1]
    part = joined(0)
    fin_o[...] = part[:n_fin, :]
    up_o[...], back_o[...] = part[n_fin:, :width], part[n_fin:, width:]
    part, late, early = joined(1), joined(2), joined(4)
    fout_o[...] = joined(3)
    for k in range(embed_o.shape[0]):
        embed_o[k] = part[k * rows : k * rows + rows, :]
        head_o[k] = late[k * rows : k * rows + rows, :]
    at = embed_o.shape[0] * rows
    n_pair = (n_in + n_out) // 2
    for block, into_in, into_out in ((late[at:, :], in1_o, out1_o), (early, in0_o, out0_o)):
        tall = jnp.concatenate([block[:n_pair, :width], block[:n_pair, width:]], axis=0)
        into_in[...] = tall[:n_in, :]
        into_out[...] = tall[n_in:, :]
    extra_o[...] = early[n_pair : n_pair + 8, :]


def collect(parts, rows_in, rows_out, rows_fin, rows_up, width):
    got = [swap(p, "dp", 1) for p in parts]
    shapes = [
        (8, width // 8, 2 * width), (rows_in, width), (rows_in, width), (rows_out, width),
        (rows_out, width), (rows_up, width), (rows_up, width), (rows_fin, 2 * width),
        (2 * parts[3].shape[0], 2 * width), (8, width // 8, 2 * width), (8, 2 * width),
    ]
    core = place_of()[3].reshape(1)
    return call(
        functools.partial(collect_kernel, (rows_fin, rows_in, rows_out)), shapes,
        [*parts, *got], smem=[core], name="collect",
    )


def tie(first, second):
    if second is None:
        return first
    return lax.optimization_barrier((first, second))[0]


def line_gather(piece, z, meanwhile):
    right = left = piece
    arrived = []
    for step in (1, 2, 3):
        right = lax.ppermute(right, "lat", along(step - 1, 3))
        left = lax.ppermute(left, "lat", backwards(along(step - 1, 3)))
        if step <= len(meanwhile):
            right, left = tie((right, left), meanwhile[step - 1])
        arrived.append((step, right, left))
    def at(k):
        chosen = piece
        for step, right, left in arrived:
            if k + step < 4:
                chosen = jnp.where(z == k + step, right, chosen)
            if k - step >= 0:
                chosen = jnp.where(z == k - step, left, chosen)
        return chosen

    return jnp.stack([at(k) for k in range(4)])


def gather_bands(q, h, meanwhile):
    z, y, x, c = place_of()
    lanes = q.shape[-1]
    quarter, rest = q.shape[0] // 4, h.shape[0] // 2
    q = pick(q.reshape(4, quarter, lanes), c * 2 + x, 0)
    h = pick(h.reshape(2, rest, lanes), c, 0)
    full = line_gather(jnp.concatenate([q, h]), z, meanwhile)
    return full, swap(full, "lat", 1), quarter


def gather_x(mine, got, quarter):
    z, y, x, c = place_of()
    full = ordered(mine, got, y, axis=1) if mine.ndim == 4 else ordered(mine[:, None], got[:, None], y, axis=1)
    full = full.reshape(8, *mine.shape[1:])
    q, h = full[:, :quarter], full[:, quarter:]
    return q, swap(q, "dp", 2), h


def join_kernel(core, q, q_got, h, h_got, q_out, h_out):
    first = core[0] == 0
    bands = q.shape[0]
    for mine, got, out in ((q, q_got, q_out), (h, h_got, h_out)):
        rows, half = out.shape[0] // bands, mine.shape[1]
        for band in range(bands):
            at = band * rows
            low, high = mine[band], got[band]
            out[at : at + half, :] = jnp.where(first, low, high)
            out[at + half : at + rows, :] = jnp.where(first, high, low)[: rows - half, :]


def join_cores(q, q_got, h, h_got, rows_q, rows_h):
    shapes = [(8 * rows_q, q.shape[2]), (8 * rows_h, q.shape[2])]
    core = place_of()[3].reshape(1)
    return call(join_kernel, shapes, [q, q_got, h, h_got], smem=[core], name="join", cost=6)


def gather_all(shard):
    rows, lanes = shard.shape
    mine = pick(shard.reshape(4, rows // 4, lanes), lax.axis_index("dp"), 0)
    return lax.all_gather(mine, ("lat", "dp"), axis=0, tiled=True).reshape(-1, rows, lanes)


def widen_pair(top, bottom):
    both = jnp.concatenate([top, bottom], axis=-2)
    half = both.shape[-2] // 2
    return jnp.concatenate([both[..., :half, :], both[..., half:, :]], axis=-1)


def narrow_pair(both, rows):
    width = both.shape[-1] // 2
    flat = jnp.concatenate([both[..., :width], both[..., width:]], axis=-2)
    return flat[..., :rows, :], flat[..., rows:, :]


def flat(value):
    return value.reshape(-1, value.shape[-1])


def banded(value, bands):
    return value.reshape(bands, -1, value.shape[-1])


def gather_weights(shards, gains, meanwhile):
    in0, in1, out0, out1, up, back, fin, fout, embed_w, head_w = shards
    if (lax.axis_size("dp"), lax.axis_size("lat")) != (4, 8):
        whole_of = lambda s: lax.all_gather(s, "lat", axis=0, tiled=True)
        embed_w, head_w = (
            whole_of(s.transpose(1, 0, 2)).transpose(1, 0, 2) for s in (embed_w, head_w)
        )
        rest = [whole_of(s) for s in shards[:8]]
        columns = [g.reshape(-1, 1) for g in whole_of(gains.T).T]
        columns[5:] = [jnp.concatenate(columns[5:7]), jnp.concatenate(columns[7:9])]
        return [*rest, embed_w, head_w], columns
    n_in, n_fin, width = in0.shape[0], fin.shape[0], in0.shape[1]
    n_embed = 8 * (width // 8)
    pair = widen_pair(in0, out0)
    n_pair = pair.shape[0]
    row = jnp.pad(gains.reshape(1, -1), ((0, 31), (0, 2 * width - gains.size)))
    early = jnp.concatenate([flat(embed_w), pair, jnp.concatenate([up, back], axis=-1), row])
    early = gather_all(early)
    spare = -n_fin % 32
    middle = gather_bands(jnp.pad(fin, ((0, spare), (0, 0))), fout, meanwhile)
    late = [widen_pair(in1, out1), flat(head_w), jnp.zeros((16, 2 * width), F32)]
    late = gather_all(jnp.concatenate(late))
    n_out = out0.shape[0]
    w_embed, w_in0, w_out0, w_up, w_back, *all_gains = unpack_early(
        early, n_embed, n_in, n_out, up.shape[0], gains.shape[0], width
    )
    w_head, w_in1, w_out1 = unpack_late(late, n_embed, n_in, n_out, width)
    return [
        w_in0, w_in1, w_out0, w_out1, w_up, w_back, middle, None, w_embed, w_head
    ], all_gains


def unpack_chunks(ref, at, out):
    bands, chunks = ref.shape[0], out.shape[0]
    rows = out.shape[1] // bands
    for band in range(bands):
        for k in range(chunks):
            start = at + k * rows
            out[k, band * rows : band * rows + rows, :] = ref[band, start : start + rows, :]


def unpack_pair(ref, at, into_in, into_out):
    bands = ref.shape[0]
    width = into_in.shape[1]
    n_in, n_out = into_in.shape[0] // bands, into_out.shape[0] // bands
    end = at + (n_in + n_out) // 2
    for band in range(bands):
        block = ref[band, at:end, :]
        tall = jnp.concatenate([block[:, :width], block[:, width:]], axis=0)
        into_in[band * n_in : band * n_in + n_in, :] = tall[:n_in, :]
        into_out[band * n_out : band * n_out + n_out, :] = tall[n_in:, :]


def unpack_early_kernel(n_embed, early, embed_o, in_o, out_o, up_o, back_o, *gain_o):
    bands, width = early.shape[0], in_o.shape[1]
    unpack_chunks(early, 0, embed_o)
    unpack_pair(early, n_embed, in_o, out_o)
    n_up = up_o.shape[0] // bands
    at = n_embed + (in_o.shape[0] + out_o.shape[0]) // bands // 2
    part = width // bands
    for band in range(bands):
        rows = slice(band * n_up, band * n_up + n_up)
        up_o[rows, :] = early[band, at : at + n_up, :width]
        back_o[rows, :] = early[band, at : at + n_up, width:]
        line = early[band, at + n_up : at + n_up + 1, :]
        shape = (part, line.shape[1])
        start = 0
        for out in gain_o:
            for block in range(out.shape[0] // width):
                hit = iota(shape, 1) == start + iota(shape, 0)
                column = jnp.sum(jnp.where(hit, line, 0.0), axis=1, keepdims=True)
                row = block * width + band * part
                out[row : row + part, :] = column
                start += part


def unpack_early(early, n_embed, n_in, n_out, n_up, n_gain, width):
    shapes = [
        (8, width, early.shape[2]), (8 * n_in, width), (8 * n_out, width), (8 * n_up, width),
        (8 * n_up, width), *[(width, 1)] * (n_gain - 4), (2 * width, 1), (2 * width, 1),
    ]
    body = functools.partial(unpack_early_kernel, n_embed)
    return call(body, shapes, [early], name="unpack_early")


def unpack_late_kernel(late, head_o, in_o, out_o):
    unpack_pair(late, 0, in_o, out_o)
    unpack_chunks(late, (in_o.shape[0] + out_o.shape[0]) // late.shape[0] // 2, head_o)


def unpack_late(late, n_embed, n_in, n_out, width):
    shapes = [(8, width, late.shape[2]), (8 * n_in, width), (8 * n_out, width)]
    return call(unpack_late_kernel, shapes, [late], name="unpack_late")


def pack_early_kernel(gwin, gwout, gg0, gg1, gg2, gg3, gg4, gga, ggm, sums, out):
    bands, width = out.shape[0], gwin.shape[1]
    n_in, n_out = gwin.shape[0] // bands, gwout.shape[0] // bands
    n_pair, part = (n_in + n_out) // 2, width // bands
    for band in range(bands):
        tall = jnp.concatenate(
            [gwin[band * n_in : band * n_in + n_in, :], gwout[band * n_out : band * n_out + n_out, :]],
            axis=0,
        )
        out[band, :n_pair, :width] = tall[:n_pair, :]
        out[band, :n_pair, width:] = tall[n_pair:, :]
        line = jnp.zeros((1, out.shape[2]), F32)
        at = 0
        for ref in (gg0, gg1, gg2, gg3, gg4, gga, ggm):
            for block in range(ref.shape[1] // width):
                shape = (width, out.shape[2])
                value = ref[:, block * width : block * width + width]
                source, lane = iota(shape, 0), iota(shape, 1)
                hit = (source - band * part == lane - at) & (lane >= at) & (lane < at + part)
                column = jnp.sum(jnp.where(iota((width, width), 0) == iota((width, width), 1), value, 0.0), axis=1, keepdims=True)
                line = line + jnp.sum(jnp.where(hit, column, 0.0), axis=0, keepdims=True)
                at += part
        lane = iota(line.shape, 1)
        line = jnp.where(lane == at, sums[0:1, 0:1], jnp.where(lane == at + 1, sums[1:2, 0:1], line))
        out[band, n_pair:, :] = jnp.where(iota((out.shape[1] - n_pair, 1), 0) == 0, line, 0.0)


def pack_early(gwin, gwout, gains, sums):
    rows = (gwin.shape[0] + gwout.shape[0]) // 16 + 16
    shape = (8, rows, 2 * gwin.shape[1])
    return call(pack_early_kernel, [shape], [gwin, gwout, *gains, sums], name="pack_early")[0]


LINE = 384
OTHERS = 24
OWN_AT = 32


def pieces(ref):
    return [slice(at, min(at + LINE, ref.shape[1])) for at in range(0, ref.shape[1], LINE)]


def chunks_of(ref):
    return [ref[:, piece] for piece in pieces(ref)]


def squares(value, rescale):
    value = value * rescale
    return value * value + 1e-30


def as_lane(column):
    shape = (column.shape[0], LINE)
    return jnp.sum(jnp.where(iota(shape, 0) == iota(shape, 1), column, 0.0), axis=0, keepdims=True)


def as_column(line, rows):
    shape = (rows, LINE)
    return jnp.sum(jnp.where(iota(shape, 0) == iota(shape, 1), line, 0.0), axis=1, keepdims=True)


def at_lane(value, lane):
    return jnp.where(iota((1, LINE), 1) == lane, value, 0.0)


def total(value):
    return jnp.sum(jnp.sum(value, axis=1, keepdims=True), axis=0, keepdims=True)


def stats_kernel(bands, count, *refs):
    grads, mats = refs[:count], refs[count : 2 * count]
    rescale_ref, gains, out = refs[2 * count :]
    rescale = rescale_ref[...]
    out[...] = jnp.zeros_like(out)
    row = 0
    energy = jnp.zeros((1, LINE), F32)
    for i, (g, w) in enumerate(zip(grads, mats)):
        own = 0.0
        for part, weight in zip(chunks_of(g), chunks_of(w)):
            square = squares(part, rescale)
            own = own + jnp.sum(square, axis=1, keepdims=True)
            other = jnp.sum(square, axis=0, keepdims=True) / (square.shape[0] * bands)
            out[row : row + 1, : other.shape[1]] = other
            row += 1
            energy = energy + at_lane(total(weight * weight), i)
        out[OWN_AT + i : OWN_AT + i + 1, :] = as_lane(own / g.shape[1])
    out[row : row + 1, :] = energy
    out[row + 1 : row + 2, :] = as_lane(jnp.sum(gains[...] * gains[...], axis=1, keepdims=True))


def new_stats(i, row, g, rescale, turned, sums, other_stats, own_stats, own_mean):
    parts = chunks_of(g)
    own, others, mean_sum, stat_sum = 0.0, [], 0.0, 0.0
    for k, part in enumerate(parts):
        own = own + jnp.sum(squares(part, rescale), axis=1, keepdims=True)
        wide = part.shape[1]
        mean = sums[row + k : row + k + 1, :wide]
        stat = other_stats[row + k : row + k + 1, :wide]
        others.append(0.5 * stat + 0.5 * mean)
        mean_sum = mean_sum + total(mean)
        stat_sum = stat_sum + total(stat)
    columns = g.shape[1]
    own = 0.5 * as_column(own_stats[i : i + 1, :], own.shape[0]) + 0.5 * (own / columns)
    stat_mean = stat_sum / columns if turned else own_mean[0:1, i : i + 1]
    return others, own, 0.5 * stat_mean + 0.5 * (mean_sum / columns)


def update_kernel(turned, count, *refs):
    grads, own_stats = refs[:count], refs[count]
    rescale_ref, sums, other_stats, own_mean, g_gain, v_gain, out, next_v, *updates = refs[count + 1 :]
    rescale = rescale_ref[...]
    row = 0
    energy = jnp.zeros((1, LINE), F32)
    for i, g in enumerate(grads):
        others, own, mean = new_stats(
            i, row, g, rescale, turned[i], sums, other_stats, own_stats, own_mean
        )
        for piece, other in zip(pieces(g), others):
            update = g[:, piece] * rescale * lax.rsqrt(own * other / mean)
            updates[i][:, piece] = update
            energy = energy + at_lane(total(update * update), i)
        row += len(others)
    grad = g_gain[...] * rescale
    value = 0.5 * v_gain[...] + 0.5 * (grad * grad + 1e-30)
    next_v[...] = value
    update = grad * lax.rsqrt(value)
    updates[count][...] = update
    out[...] = jnp.zeros_like(out)
    out[0:1, :] = energy
    out[1:2, :] = as_lane(jnp.sum(update * update, axis=1, keepdims=True))


def step_kernel(bands, count, *refs):
    updates, mats = refs[: count + 1], refs[count + 1 : 2 * count + 2]
    squares_u, squares_w = refs[2 * count + 2 : 2 * count + 4]
    outs = refs[2 * count + 4 :]
    news, copies = outs[: len(outs) // 2], outs[len(outs) // 2 :]
    where = [(0, None), (1, 0), (1, 1), (2, 0), (2, 1), (3, 0), (3, 1)]
    where += [(4, None), (5, None), (6, None), (7, None)]
    for i, (u, w, (out, pair)) in enumerate(zip(updates, mats, where)):
        new, copy = news[out], copies[out]
        if i < count:
            entries = u.shape[0] * u.shape[1] * bands
            energy_u, energy_w = squares_u[0:1, i : i + 1], squares_w[0:1, i : i + 1]
        else:
            entries = u.shape[1] * bands
            energy_u, energy_w = (
                as_column(s[1:2, :], u.shape[0]) for s in (squares_u, squares_w)
            )
        clip = jnp.maximum(1.0, jnp.sqrt(energy_u / entries) / 0.25)
        size = jnp.maximum(0.001, jnp.sqrt(energy_w / entries))
        value = w[...] - size * (u[...] / clip)
        if out == 2:
            value = value.T
        at = Ellipsis if pair is None else pair
        new[at] = value
        copy[at] = value.astype(BF16)


def plain_call(body, shapes, args, name, rounded=()):
    vmem = pl.BlockSpec(memory_space=pltpu.VMEM)
    outs = [jax.ShapeDtypeStruct(tuple(s), F32) for s in shapes]
    outs += [jax.ShapeDtypeStruct(tuple(s), BF16) for s in rounded]
    shapes = outs
    return pl.pallas_call(
        body,
        out_shape=outs,
        in_specs=[vmem] * len(args),
        out_specs=[vmem] * len(shapes),
        compiler_params=pltpu.CompilerParams(vmem_limit_bytes=VMEM),
        cost_estimate=takes(4),
        name=name,
    )(*args)


def band_sum_and_gather(sums, mine):
    bit = 1
    while bit < lax.axis_size("lat"):
        got = swap(jnp.concatenate([sums, mine]), "lat", bit)
        n = sums.shape[0]
        sums = sums + got[:n]
        mine = ordered(mine, got[n:], (lax.axis_index("lat") // bit) % 2)
        bit *= 2
    return sums, mine


def lines(line):
    return jnp.pad(line, (0, -line.shape[0] % LINE)).reshape(-1, LINE)


class Moments:
    def __init__(self, mats, turned, row_stats, col_stats):
        bands, band = lax.axis_size("lat"), lax.axis_index("lat")
        self.mats, self.turned, self.bands = mats, turned, bands
        self.rows = [m.shape[-2] for m in mats]
        other_lines, self.own, means = [], [], []
        row_at = col_at = 0
        for m, turn in zip(mats, turned):
            split_size = m.shape[-2] * bands
            columns = m.shape[1]
            n_row, n_col = (columns, split_size) if turn else (split_size, columns)
            row, col = row_stats[row_at : row_at + n_row], col_stats[col_at : col_at + n_col]
            row_at, col_at = row_at + n_row, col_at + n_col
            other, mine = (row, col) if turn else (col, row)
            other_lines.append(lines(other))
            mine = lax.dynamic_slice_in_dim(mine, band * m.shape[-2], m.shape[-2])
            self.own.append(lines(mine))
            means.append(jnp.mean(row).reshape(1, 1))
        self.other = jnp.concatenate(other_lines)
        self.own = jnp.pad(jnp.concatenate(self.own), ((0, 16 - len(mats)), (0, 0)))
        self.mean = jnp.pad(jnp.concatenate(means, axis=1), ((0, 0), (0, LINE - len(mats))))
        self.row_stats, self.col_stats = row_stats, col_stats

    def step(self, grads, rescale, gains, g_gain, v_gain):
        count = len(grads)
        rescale = rescale.reshape(1, 1)
        shape = (OWN_AT + 16, LINE)
        (stats,) = plain_call(
            functools.partial(stats_kernel, self.bands, count), [shape],
            [*grads, *self.mats, rescale, gains], "stats",
        )
        sums, own = band_sum_and_gather(stats[:OWN_AT], stats[OWN_AT:])
        out, next_v, *updates = plain_call(
            functools.partial(update_kernel, tuple(self.turned), count),
            [(8, LINE), gains.shape, *[g.shape for g in grads], gains.shape],
            [*grads, self.own, rescale, sums, self.other, self.mean, g_gain, v_gain], "update",
        )
        bit = 1
        while bit < self.bands:
            out = out + swap(out, "lat", bit)
            bit *= 2
        shapes = [g.shape for g in grads]
        shapes = [
            shapes[0], (2, *shapes[1]), (2, *shapes[3][::-1]), (2, *shapes[5]), *shapes[7:], gains.shape
        ]
        news = plain_call(
            functools.partial(step_kernel, self.bands, count), shapes,
            [*updates, *self.mats, gains, out, sums[OTHERS : OTHERS + 8]], "step", shapes,
        )
        own = own.reshape(self.bands, 16, LINE)
        row_means, col_means = [], []
        row = 0
        for i, (m, turn) in enumerate(zip(self.mats, self.turned)):
            mine = own[:, i, : self.rows[i]].reshape(-1)
            taken = -(-m.shape[1] // LINE)
            other = sums[row : row + taken].reshape(-1)[: m.shape[1]]
            row += taken
            row_means.append(other if turn else mine)
            col_means.append(mine if turn else other)
        next_rows = 0.5 * self.row_stats + 0.5 * jnp.concatenate(row_means)
        next_cols = 0.5 * self.col_stats + 0.5 * jnp.concatenate(col_means)
        return news[: len(shapes)], news[len(shapes) :], next_rows, next_cols, next_v


def pixel_columns(flat_rows):
    rows, depth = flat_rows.shape
    moved = flat_rows.reshape(rows, depth // 16, 4, 4).transpose(3, 2, 0, 1)
    moved = jnp.pad(moved, ((0, 0), (0, 0), (0, 0), (0, CH - depth // 16)))
    return moved.reshape(8, 2, rows, CH).transpose(0, 2, 1, 3).reshape(8, rows, 2 * CH)


def channel_columns(chunks, chans):
    rows = chunks.shape[1]
    moved = chunks.reshape(4, 2, rows, 2, CH)[..., :chans]
    return moved.transpose(2, 4, 1, 3, 0).reshape(rows, chans * 16)


def shifted(value, axis, by):
    peers = lax.axis_size(axis)
    return lax.ppermute(value, axis, [(i, (i + by) % peers) for i in range(peers)])


def scatter_plain(grads, chunked, g_gain, total, count):
    scatter = lambda g, axis: lax.psum_scatter(g, "lat", scatter_dimension=axis, tiled=True)
    total, count = lax.psum((total, count), ("dp", "lat"))
    grads = [scatter(g, 0) for g in grads]
    chunked = [scatter(g, 1) for g in chunked]
    grads, chunked, g_gain = lax.psum((grads, chunked, scatter(g_gain, 1)), "dp")
    return grads, chunked, g_gain, total, count


def on_device(
    fields, target, valid_mask, sample_index, weight_table, lon_shift, w_embed, w_in, w_out,
    w_merge, w_fin, w_fout, w_head, gains, row_stats, col_stats, v_gain,
):
    band_count = lax.axis_size("lat")
    band_index = lax.axis_index("lat")
    samples, chans, rows_dev, across = fields.shape
    width = w_in.shape[1]
    total_rows = rows_dev * band_count
    pixel_rows = (band_index * rows_dev + jnp.arange(rows_dev)).astype(F32)
    coslat = jnp.cos((90.0 - (pixel_rows + 0.5) * 180.0 / total_rows) * (jnp.pi / 180.0))
    picked = (sample_index[:, None] == jnp.arange(weight_table.shape[0])[None, :]).astype(F32)
    sample_weight = jnp.sum(picked * weight_table[None, :], axis=1)
    weight = sample_weight[:, None, None] * coslat[None, :, None] * valid_mask.astype(F32)

    mats = [
        w_embed.T, w_in[0].T, w_in[1].T, w_out[0], w_out[1], w_merge[0].T, w_merge[1].T, w_fin.T,
        w_fout, w_head,
    ]
    turned = [True, True, True, False, False, True, True, True, False, False]
    moments = Moments(mats, turned, row_stats, col_stats)
    shards = mats[1:9] + [pixel_columns(mats[0]), pixel_columns(mats[9])]
    apart = (lax.axis_size("dp"), band_count) == (4, 8)
    high, low = prep(fields)
    wanted = prep(target, weight)
    ready = (wanted, moments.own, moments.other, moments.mean)
    whole_weights, (*gain, gain_a, gain_m) = gather_weights(shards, gains, (high, ready))
    f_in0, f_in1, f_out0, f_out1, f_up, f_back, f_fin, f_fout, f_embed, f_head = whole_weights
    stream = embed(f_embed, high, low)
    own, stay, send, *kept_e = encoder(lon_shift, stream, f_in0, f_out0, gain[0], gain[1])
    if apart:
        mine, got, quarter = f_fin
        q, q_got, h = gather_x(mine, tie(got, stream), quarter)
        q = ordered(q, tie(q_got, own), place_of()[2], axis=1)
        q_got, h_got = swap(q, "dp", 1), swap(h, "dp", 1)
        f_fin, f_fout = join_cores(q, q_got, h, h_got, w_fin.shape[1], w_fout.shape[0])
    send = shifted(send, "lat", -1)
    rolled, wide, last, stay, send, *kept_m = merging(
        stay, send, f_up, f_back, f_fin, f_fout, gain_a, gain_m
    )
    send = shifted(send, "lat", 1)
    start, out, *kept_d = decoder(lon_shift, own, stay, send, f_in1, f_out1, gain[2], gain[3])
    grad, g_head, gg_final, sums = head(
        out, gain[4], f_head, wanted, chans, 8 if apart else 1
    )
    b = lambda g: banded(g, 8)
    grad, stay, send, g_in1, g_out1, gg_2, gg_3 = decoder_back(
        lon_shift, grad, start, kept_d, f_in1, f_out1, gain[2], gain[3]
    )
    send = shifted(send, "lat", -1)
    if apart:
        s_a = core_half(jnp.concatenate([g_head, widen_pair(b(g_in1), b(g_out1))], axis=1))
        s_a = lax.psum_scatter(flat(s_a), "lat", scatter_dimension=0, tiled=True)
    g_back, g_fout, gg_m, between, attended, g_fin = merging_mlp_back(
        stay, send, last, kept_m, f_back, f_fin, f_fout, gain_m
    )
    stay, send, g_up, gg_a, g_fin = merging_attention_back(
        between, attended, rolled, wide, kept_m, f_up, f_fin, gain_a, g_fin, stay.shape
    )
    send = shifted(send, "lat", 1)
    grad, g_in0, g_out0, gg_0, gg_1 = encoder_back(
        lon_shift, grad, stay, send, stream, kept_e, f_in0, f_out0, gain[0], gain[1]
    )
    g_embed = embed_back(grad, high, low, 8 if apart else 1)
    gain_rows = [gg_0, gg_1, gg_2, gg_3, gg_final, gg_a, gg_m]
    if apart:
        z = place_of()[0]
        s_f = core_half(b(g_fout), stay)
        s_f = y_half(s_f, grad)
        s_m = [b(g_fin), jnp.concatenate([b(g_up), b(g_back)], axis=-1)]
        s_m = core_half(jnp.concatenate(s_m, axis=1), grad)
        s_m = y_half(x_half(s_m, g_embed))
        s_c = core_half(pack_early(g_in0, g_out0, gain_rows, sums))
        s_d = core_half(g_embed)
        s_d, s_c = x_half(s_d), y_half(s_c)
        s_d = y_half(s_d)
        n_d = s_d.shape[1]
        s_f = line_sum(s_f, z, (g_embed,))
        s_m = line_sum(s_m, z)
        s_c = line_sum(jnp.concatenate([s_d, s_c], axis=1), z)
        parts = over_x([s_m, s_c[:n_d]], [s_a, s_f, s_c[n_d:]])
        n_in, n_out, n_fin, n_up = (g.shape[0] // 8 for g in (g_in0, g_out0, g_fin, g_up))
        g_embed, *grads, g_head, row = collect(parts, n_in, n_out, n_fin, n_up, width)
        n_extra = gains.shape[0] * gains.shape[1]
        total, count = row[0, n_extra], chans * row[0, n_extra + 1]
        g_gain = row[0, :n_extra].reshape(gains.shape)
    else:
        g_gain = jnp.concatenate(gain_rows, axis=1).reshape(gains.shape[0], width)
        chunked = [g.reshape(8, width, -1) for g in (g_embed, g_head)]
        grads = [g_in0, g_in1, g_out0, g_out1, g_up, g_back, g_fin, g_fout]
        grads, (g_embed, g_head), g_gain, total, count = scatter_plain(
            grads, chunked, g_gain, sums[0, 0], chans * sums[1, 0]
        )
    grads = [channel_columns(g_embed, chans), *grads, channel_columns(g_head, chans)]
    loss = total / count
    rescale = 2.0 / count
    new, rounded, next_rows, next_cols, next_v_gain = moments.step(
        grads, rescale, gains, g_gain, v_gain
    )

    def laid_out(new):
        n_embed, n_in, n_out, n_merge, n_fin, n_fout, n_head, n_gains = new
        turn = lambda v: v.transpose(0, 2, 1)
        return [
            n_embed.T, turn(n_in), turn(n_out), turn(n_merge), n_fin.T,
            n_fout, n_head, n_gains,
        ]

    results, copies = laid_out(new), laid_out(rounded)
    return (loss, *results, next_rows, next_cols, next_v_gain, *copies)


def solution(mesh):
    placed = (
        P("dp", None, "lat", None),
        P("dp", None, "lat", None),
        P("dp", "lat", None),
        P("dp"),
        P(),
        P("dp"),
        P(None, "lat"),
        P(None, None, "lat"),
        P(None, "lat", None),
        P(None, None, "lat"),
        P(None, "lat"),
        P("lat", None),
        P("lat", None),
        P(None, "lat"),
        P(),
        P(),
        P(None, "lat"),
    )
    weights = placed[6:14]
    return jax.shard_map(
        on_device,
        mesh=mesh,
        in_specs=placed,
        out_specs=(P(), *weights, P(), P(), P(None, "lat"), *weights),
        check_vma=False,
    )
```

```python
import functools
import math

import jax
import jax.numpy as jnp
from jax import lax
from jax.experimental import pallas as pl
from jax.experimental.pallas import tpu as pltpu
from jax.sharding import PartitionSpec as P

F32 = jnp.float32
BF16 = jnp.bfloat16
HEAD = 32
PATCH = 4
WR = 4
WC = 16
CH = 192
VMEM = 60 * 1024 * 1024
ROOT = math.sqrt(2.0 / math.pi)
NN, NT, TN = (1, 0), (1, 1), (0, 0)


def takes(us):
    return pl.CostEstimate(
        flops=int(us * 0.4e9), bytes_accessed=int(us * 1.3e6), transcendentals=0
    )


def params(steps):
    return pltpu.CompilerParams(
        dimension_semantics=("arbitrary",) * steps, vmem_limit_bytes=VMEM
    )


def split(value):
    high = value.astype(BF16)
    return high, (value - high.astype(F32)).astype(BF16)


def dg(a, b, dims):
    return lax.dot_general(
        a, b, (((dims[0],), (dims[1],)), ((), ())), preferred_element_type=F32
    )


def dot3(a, b, dims):
    return dg(a[0], b[0], dims) + (dg(a[0], b[1], dims) + dg(a[1], b[0], dims))


def normalise(stream):
    centred = stream - jnp.mean(stream, axis=0, keepdims=True)
    scale = lax.rsqrt(jnp.mean(centred * centred, axis=0, keepdims=True) + 1e-05)
    return centred * scale, scale


def normalise_back(grad, hat, scale, gain):
    weighted = grad * gain
    return scale * (
        weighted
        - jnp.mean(weighted, axis=0, keepdims=True)
        - hat * jnp.mean(weighted * hat, axis=0, keepdims=True)
    )


def iota(shape, axis):
    return lax.broadcasted_iota(jnp.int32, shape, axis)


def roll_matrix(shift, tokens):
    lane = iota((tokens, tokens), 0)
    out = iota((tokens, tokens), 1)
    half, inner = out // (tokens // 2), out % (tokens // 2)
    row = jnp.where(half == 0, 2, 0) + (inner // WC) % 2
    columns = tokens // WR
    moved = ((inner // (2 * WC)) * WC + inner % WC + shift) % columns
    source = (moved // WC) * (WR * WC) + row * WC + moved % WC
    return (lane == source).astype(BF16)


def order_matrix(tokens):
    lane = iota((tokens, tokens), 0)
    out = iota((tokens, tokens), 1)
    window, row, col = out // (WR * WC), (out // WC) % WR, out % WC
    source = (row // 2) * (tokens // 2) + window * (2 * WC) + (row % 2) * WC + col
    return (lane == source).astype(BF16)


def permute(value, onehot, dims):
    high, low = split(value)
    rest = (value - high.astype(F32) - low.astype(F32)).astype(BF16)
    return dg(high, onehot, dims) + (dg(low, onehot, dims) + dg(rest, onehot, dims))


def pixel_matrix():
    lane = iota((512, 512), 0)
    out = iota((512, 512), 1)
    b, window, row, col = out // 128, (out // 64) % 2, (out // 16) % 4, out % 16
    return (lane == row * 128 + window * 64 + col * 4 + b).astype(BF16)


def prep_kernel(chans, with_weight, *refs):
    if with_weight:
        _, x_ref, w_ref, out_ref, perm = refs
    else:
        _, x_ref, hi_ref, lo_ref, perm = refs
    block = 64

    @pl.when((pl.program_id(0) == 0) & (pl.program_id(1) == 0) & (pl.program_id(2) == 0))
    def _():
        perm[...] = pixel_matrix()

    row = iota((block, 512), 0) + pl.program_id(2) * block
    tiles = []
    for a in range(PATCH):
        tile = jnp.concatenate(
            [x_ref[pl.ds(4 * r + a, block, stride=16), :] for r in range(WR)], axis=1
        )
        tile = jnp.where(row < chans, tile, 0.0)
        if with_weight:
            extra = jnp.concatenate([w_ref[4 * r + a : 4 * r + a + 1, :] for r in range(WR)], axis=1)
            tile = jnp.where(row == chans, extra, tile)
        tiles.append(tile)
    high, low = split(jnp.concatenate(tiles, axis=0))
    moved = dg(jnp.concatenate([high, low], axis=0), perm[...], NN)
    for a in range(PATCH):
        for b in range(PATCH):
            at, piece = a * block, slice(b * 128, b * 128 + 128)
            above, below = moved[at : at + block, piece], moved[at + 256 : at + 256 + block, piece]
            if with_weight:
                out_ref[b, a] = above + below
            else:
                hi_ref[b, a] = above.astype(BF16)
                lo_ref[b, a] = below.astype(BF16)


def prep(token, fields, weight=None):
    samples, chans, height, across = fields.shape
    flat = fields.reshape(samples, chans * height, across)
    padded = 192
    shape = (samples, 4, 4, padded, across)
    spec = pl.BlockSpec((None, 4, 4, 64, 128), lambda s, p, c: (s, 0, 0, c, p))
    in_specs = [pl.BlockSpec(memory_space=pltpu.SMEM)]
    in_specs.append(pl.BlockSpec((None, 64 * height, 128), lambda s, p, c: (s, c, p)))
    if weight is not None:
        in_specs.append(pl.BlockSpec((None, height, 128), lambda s, p, c: (s, 0, p)))
        out_shape, out_specs = jax.ShapeDtypeStruct(shape, F32), spec
    else:
        out_shape = [jax.ShapeDtypeStruct(shape, BF16)] * 2
        out_specs = [spec] * 2
    outs = pl.pallas_call(
        functools.partial(prep_kernel, chans, weight is not None),
        out_shape=out_shape,
        grid=(samples, across // 128, padded // 64),
        in_specs=in_specs,
        out_specs=out_specs,
        scratch_shapes=[pltpu.VMEM((512, 512), BF16)],
        compiler_params=params(3),
        cost_estimate=takes(22),
        name="prep",
    )(token, *([flat] if weight is None else [flat, weight]))
    return jax.tree.map(lambda a: a.reshape(samples, 16 * padded, across), outs)


def embed_kernel(w_ref, hi_ref, lo_ref, out_ref):
    total = None
    rows = w_ref.shape[2]
    for k in range(w_ref.shape[0]):
        at = slice(k * rows, k * rows + rows)
        part = dot3(split(w_ref[k]), (hi_ref[at, :], lo_ref[at, :]), NN)
        total = part if total is None else total + part
    out_ref[...] = total


def embed(weight, high, low):
    samples, depth, tokens = high.shape
    width = weight.shape[1]
    big = pl.BlockSpec((None, depth, tokens), lambda s: (s, 0, 0))
    return pl.pallas_call(
        embed_kernel,
        out_shape=jax.ShapeDtypeStruct((width, samples * tokens), F32),
        grid=(samples,),
        in_specs=[pl.BlockSpec(weight.shape, lambda s: (0, 0, 0)), big, big],
        out_specs=pl.BlockSpec((width, tokens), lambda s: (0, s)),
        compiler_params=params(1),
        cost_estimate=takes(10),
        name="embed",
    )(weight, high, low)


def put_bands(out_ref, value):
    rows = out_ref.shape[1]
    for band in range(out_ref.shape[0]):
        out_ref[band] = value[band * rows : band * rows + rows, :]


def embed_back_kernel(g_ref, hi_ref, lo_ref, out_ref):
    samples, _, tokens = hi_ref.shape
    total = None
    for s in range(samples):
        part = dot3(split(g_ref[:, s * tokens : s * tokens + tokens]), (hi_ref[s], lo_ref[s]), NT)
        total = part if total is None else total + part
    put_bands(out_ref, total)


def embed_back(grad, high, low, bands):
    samples, depth, tokens = high.shape
    width = grad.shape[0]
    rows = 2 * CH
    big = pl.BlockSpec((samples, rows, tokens), lambda k: (0, k, 0))
    return pl.pallas_call(
        embed_back_kernel,
        out_shape=jax.ShapeDtypeStruct((bands, depth // rows * width // bands, rows), F32),
        grid=(depth // rows,),
        in_specs=[pl.BlockSpec(grad.shape, lambda k: (0, 0)), big, big],
        out_specs=pl.BlockSpec((bands, width // bands, rows), lambda k: (0, k, 0)),
        compiler_params=params(1),
        cost_estimate=takes(12),
        name="embed_back",
    )(grad, high, low)


def rows_of(at, count):
    return pl.ds(pl.multiple_of(at * count, 16), count)


def chunk_of(rows):
    return next(c for c in (384, 288, 192) if rows % c == 0)


def loop(rows, body):
    count = chunk_of(rows)

    def step(at, carry):
        body(at, count)
        return carry

    lax.fori_loop(0, rows // count, step, 0)


def put(pair, value):
    pair[0][...], pair[1][...] = split(value)


def both(pair):
    return pair[0][...], pair[1][...]


def spread(compact, first):
    high, low = split(compact)
    zero = jnp.zeros_like(high)
    grow = lambda v: jnp.concatenate(
        [jnp.where(first, v, zero), jnp.where(first, zero, v)], axis=0
    )
    return grow(high), grow(low)


def thrice(high, low):
    above = jnp.concatenate([high, high], axis=1)
    return jnp.concatenate([above, jnp.concatenate([low, jnp.zeros_like(low)], axis=1)], axis=0)


def halves(value):
    return value[:HEAD] + value[HEAD:]


def head_rows(width, part, head):
    return slice(part * width + head * HEAD, part * width + head * HEAD + HEAD)


def attend(qkv, out, weights, width):
    heads = width // HEAD
    first = iota((64, 128), 1) < 64

    def body(pair, carry):
        lanes = pl.ds(pl.multiple_of(pair * 128, 128), 128)
        scores = []
        for h in range(heads):
            qh, ql = split(qkv[head_rows(width, 0, h), lanes] * HEAD**-0.5)
            kh, kl = split(qkv[head_rows(width, 1, h), lanes])
            full = dg(
                jnp.concatenate([kh, kh, kl], axis=0), jnp.concatenate([qh, ql, qh], axis=0), TN
            )
            scores.append(jnp.where(first, full[:64], full[64:]))
        scores = jnp.stack(scores)
        scores = jnp.exp(scores - jnp.max(scores, axis=1, keepdims=True))
        scores = scores * (1.0 / jnp.sum(scores, axis=1, keepdims=True))
        weights[pair] = scores
        for h in range(heads):
            values = thrice(*split(qkv[head_rows(width, 2, h), lanes]))
            full = jnp.concatenate(spread(scores[h], first), axis=0)
            out[head_rows(width, 0, h), lanes] = halves(dg(values, full, NN))
        return carry

    lax.fori_loop(0, weights.shape[0], body, 0)


def attend_back(qkv, weights, grad, high_out, low_out, width):
    heads = width // HEAD
    first = iota((64, 128), 1) < 64
    group = 6

    def body(at, carry):
        pair, base = at // (heads // group), (at % (heads // group)) * group
        lanes = pl.ds(pl.multiple_of(pair * 128, 128), 128)
        where = lambda part, h: pl.ds(
            pl.multiple_of(part * width + (base + h) * HEAD, HEAD), HEAD
        )
        def keep(part, h, value):
            rows = where(part, h)
            high_out[rows, lanes], low_out[rows, lanes] = split(value)

        dp = []
        for h in range(group):
            vh, vl = split(qkv[where(2, h), lanes])
            oh, ol = split(grad[where(0, h), lanes])
            full = dg(
                jnp.concatenate([vh, vh, vl], axis=0), jnp.concatenate([oh, ol, oh], axis=0), TN
            )
            dp.append(jnp.where(first, full[:64], full[64:]))
        dp = jnp.stack(dp)
        p = weights[pair, pl.ds(base, group)]
        ds = p * (dp - jnp.sum(dp * p, axis=1, keepdims=True))
        for h in range(group):
            full = jnp.concatenate(spread(p[h], first), axis=1)
            values = thrice(*split(grad[where(0, h), lanes]))
            keep(2, h, halves(dg(values, full, NT)))
        for h in range(group):
            high, low = spread(ds[h], first)
            keys = thrice(*split(qkv[where(1, h), lanes]))
            queries = thrice(*split(qkv[where(0, h), lanes] * HEAD**-0.5))
            full = dg(keys, jnp.concatenate([high, low], axis=0), NN)
            keep(0, h, halves(full) * HEAD**-0.5)
            full = dg(queries, jnp.concatenate([high, low], axis=1), NT)
            keep(1, h, halves(full))
        return carry

    lax.fori_loop(0, weights.shape[0] * (heads // group), body, 0)


def gelu_parts(u):
    t = jnp.tanh(ROOT * (u + 0.044715 * u * u * u))
    return 0.5 * u * (1.0 + t), t


def lane_sums(value):
    column = jnp.sum(value, axis=1, keepdims=True)
    shape = (value.shape[0],) * 2
    return jnp.sum(jnp.where(iota(shape, 0) == iota(shape, 1), column, 0.0), axis=0, keepdims=True)


def saved_shapes(width, hidden, tokens):
    return [
        (3 * width, tokens),
        (width, tokens),
        (width, tokens),
        (hidden, tokens),
        (tokens // 128, width // HEAD, 64, 128),
    ]


def forward_scratch(width, hidden, tokens):
    scratch = [pltpu.VMEM(s, F32) for s in saved_shapes(width, hidden, tokens)]
    scratch += [pltpu.VMEM((width, tokens), BF16)] * 2 + [pltpu.VMEM((hidden, tokens), BF16)] * 2
    return scratch + [pltpu.SemaphoreType.DMA((5,))]


def block_forward(x, win, wout, ga, gm, kept, scratch):
    qkv, out, mid, hidden, weights, nh, nl, hh, hl, sems = scratch
    width = x.shape[0]
    copies = [
        pltpu.make_async_copy(v, k, sems.at[i])
        for i, (v, k) in enumerate(zip((qkv, out, mid, hidden, weights), kept))
    ]
    put((nh, nl), normalise(x)[0] * ga)

    def project(at, count):
        rows = rows_of(at, count)
        qkv[rows, :] = dot3(split(win[rows, :]), both((nh, nl)), NN)

    loop(3 * width, project)
    copies[0].start()
    attend(qkv, out, weights, width)
    copies[1].start()
    copies[4].start()
    mid[...] = x + dot3(split(wout[:width, :]), split(out[...]), TN)
    copies[2].start()
    put((nh, nl), normalise(mid[...])[0] * gm)

    def feed(at, count):
        rows = rows_of(at, count)
        from_rows = pl.ds(pl.multiple_of(3 * width + at * count, 16), count)
        u = dot3(split(win[from_rows, :]), both((nh, nl)), NN)
        hidden[rows, :] = u
        hh[rows, :], hl[rows, :] = split(gelu_parts(u)[0])

    loop(hidden.shape[0], feed)
    copies[3].start()
    return mid[...] + dot3(split(wout[width:, :]), both((hh, hl)), TN), copies


def backward_scratch(width, hidden, tokens):
    scratch = [pltpu.VMEM(s, F32) for s in saved_shapes(width, hidden, tokens)]
    scratch += [pltpu.VMEM((width, tokens), F32)]
    scratch += [pltpu.VMEM((width, tokens), BF16)] * 4 + [pltpu.VMEM((hidden, tokens), BF16)] * 2
    return scratch + [pltpu.SemaphoreType.DMA((5,))]


def fetch(kept, slots, sems):
    copies = [
        pltpu.make_async_copy(k, v, sems.at[i]) for i, (k, v) in enumerate(zip(kept, slots))
    ]
    for copy in copies:
        copy.start()
    return copies


def mlp_back(dy, win, wout, gm, copies, slots, pairs, da, gwin, gwout, ggm):
    mid, hidden, out = slots
    norm, grad, wide = pairs
    width = dy.shape[0]
    put(grad, dy)
    copies[0].wait()
    hat, scale = normalise(mid[...])
    put(norm, hat * gm)
    copies[1].wait()

    def feed(at, count):
        rows = rows_of(at, count)
        out_rows = pl.ds(pl.multiple_of(width + at * count, 16), count)
        u = hidden[rows, :]
        value, t = gelu_parts(u)
        slope = 0.5 * (1.0 + t) + 0.5 * ROOT * u * (1.0 - t * t) * (1.0 + 3 * 0.044715 * u * u)
        gwout[out_rows, :] = dot3(split(value), both(grad), NT)
        du = split(slope * dot3(split(wout[out_rows, :]), both(grad), NN))
        wide[0][rows, :], wide[1][rows, :] = du
        gwin[rows, :] = dot3(du, both(norm), NT)

    loop(hidden.shape[0], feed)
    dn = dot3(split(win[...]), both(wide), TN)
    ggm[...] = lane_sums(dn * hat)
    dmid = dy + normalise_back(dn, hat, scale, gm)
    put(grad, dmid)
    da[...] = dot3(split(wout[:width, :]), both(grad), NN)
    copies[2].wait()
    gwout[:width, :] = dot3(split(out[...]), both(grad), NT)
    return dmid


def attention_back(dmid, x, win, ga, copies, slots, pairs, da, gwin, gga):
    weights, qkv = slots
    norm, wide = pairs
    width = x.shape[0]
    for copy in copies:
        copy.wait()
    attend_back(qkv, weights, da, *wide, width)
    hat, scale = normalise(x)
    put(norm, hat * ga)

    def project(at, count):
        rows = rows_of(at, count)
        gwin[rows, :] = dot3((wide[0][rows, :], wide[1][rows, :]), both(norm), NT)

    loop(3 * width, project)
    grads = wide[0][: 3 * width, :], wide[1][: 3 * width, :]
    dn = dot3(split(win[...]), grads, TN)
    gga[...] = lane_sums(dn * hat)
    return dmid + normalise_back(dn, hat, scale, ga)


def block_backward(dy, x, win, wout, ga, gm, kept, scratch, gwin, gwout, gga, ggm):
    qkv, out, mid, hidden, weights, da, nh, nl, yh, yl, hh, hl, _ = scratch
    at = 3 * x.shape[0]
    norm, grad, wide = (nh, nl), (yh, yl), (hh, hl)
    dmid = mlp_back(
        dy, win.at[at:], wout, gm, kept[:3], (mid, hidden, out), (norm, grad, wide), da,
        gwin.at[at:], gwout, ggm,
    )
    return attention_back(
        dmid, x, win.at[:at], ga, kept[3:], (weights, qkv), (norm, wide), da, gwin.at[:at], gga
    )


def fetch_block(kept, scratch):
    order = (2, 3, 1, 4, 0)
    return fetch([kept[i] for i in order], [scratch[i] for i in order], scratch[-1])


def call(body, outs, ins, kept_in=(), kept_out=(), scratch=(), smem=(), name=None, aliases=None, cost=0.2):
    vmem = pl.BlockSpec(memory_space=pltpu.VMEM)
    hbm = pl.BlockSpec(memory_space=pl.ANY)
    shape = lambda s: jax.ShapeDtypeStruct(tuple(s), F32)
    return pl.pallas_call(
        body,
        out_shape=[shape(s) for s in (*outs, *kept_out)],
        in_specs=[pl.BlockSpec(memory_space=pltpu.SMEM)] * len(smem)
        + [vmem] * len(ins)
        + [hbm] * len(kept_in),
        out_specs=[vmem] * len(outs) + [hbm] * len(kept_out),
        scratch_shapes=list(scratch),
        input_output_aliases=aliases or {},
        cost_estimate=takes(cost),
        compiler_params=pltpu.CompilerParams(vmem_limit_bytes=VMEM),
        name=name,
    )(*smem, *ins, *kept_in)


def pack(shift_ref, value, stay, send):
    samples = shift_ref.shape[0]
    tokens = value.shape[1] // samples
    for s in range(samples):
        part = value[:, s * tokens : s * tokens + tokens]
        moved = permute(part, roll_matrix(shift_ref[s], tokens), NN)
        stay[s] = moved[:, : tokens // 2]
        send[s] = moved[:, tokens // 2 :]


def unpack(shift_ref, stay, send):
    parts = []
    for s in range(stay.shape[0]):
        joined = jnp.concatenate([stay[s], send[s]], axis=1)
        parts.append(permute(joined, roll_matrix(shift_ref[s], joined.shape[1]), NT))
    return jnp.concatenate(parts, axis=1)


def to_windows(stay, send):
    parts = [jnp.concatenate([stay[s], send[s]], axis=1) for s in range(stay.shape[0])]
    order = order_matrix(parts[0].shape[1])
    return jnp.concatenate([permute(p, order, NN) for p in parts], axis=1)


def from_windows(value, stay, send):
    tokens = value.shape[1] // stay.shape[0]
    order = order_matrix(tokens)
    for s in range(stay.shape[0]):
        moved = permute(value[:, s * tokens : s * tokens + tokens], order, NT)
        stay[s] = moved[:, : tokens // 2]
        send[s] = moved[:, tokens // 2 :]


def half_shape(shift, width, tokens):
    samples = shift.shape[0]
    return (samples, width, tokens // samples // 2)


def encoder_kernel(shift, x, win, wout, ga, gm, y, stay, send, *rest):
    out, copies = block_forward(x[...], win, wout, ga[...], gm[...], rest[:5], rest[5:])
    y[...] = out
    pack(shift, out, stay, send)
    for copy in copies:
        copy.wait()


def encoder(shift, x, win, wout, ga, gm):
    width, tokens = x.shape
    hidden = win.shape[0] - 3 * width
    half = half_shape(shift, width, tokens)
    return call(
        encoder_kernel, [x.shape, half, half], [x, win, wout, ga, gm],
        kept_out=saved_shapes(width, hidden, tokens),
        scratch=forward_scratch(width, hidden, tokens), smem=[shift], name="encoder", cost=14,
    )


def merging_kernel(stay_in, send_in, wup, wback, win, wout, ga, gm, x, wide, last, stay, send, *rest):
    start = to_windows(stay_in, send_in)
    x[...] = start
    raised = dot3(split(wup[...]), split(start), NN)
    wide[...] = raised
    out, copies = block_forward(raised, win, wout, ga[...], gm[...], rest[:5], rest[5:])
    last[...] = out
    from_windows(dot3(split(wback[...]), split(out), TN), stay, send)
    for copy in copies:
        copy.wait()


def merging(stay, arrived, wup, wback, win, wout, ga, gm):
    samples, narrow, half = stay.shape
    width, tokens = wup.shape[0], samples * 2 * half
    hidden = win.shape[0] - 3 * width
    wide = (width, tokens)
    return call(
        merging_kernel, [(narrow, tokens), wide, wide, stay.shape, stay.shape],
        [stay, arrived, wup, wback, win, wout, ga, gm],
        kept_out=saved_shapes(width, hidden, tokens),
        scratch=forward_scratch(width, hidden, tokens), name="merging", cost=32,
    )


def decoder_kernel(shift, y, stay_in, send_in, win, wout, ga, gm, x, last, *rest):
    start = y[...] + unpack(shift, stay_in, send_in)
    x[...] = start
    out, copies = block_forward(start, win, wout, ga[...], gm[...], rest[:5], rest[5:])
    last[...] = out
    for copy in copies:
        copy.wait()


def decoder(shift, y, stay, arrived, win, wout, ga, gm):
    width, tokens = y.shape
    hidden = win.shape[0] - 3 * width
    return call(
        decoder_kernel, [y.shape, y.shape], [y, stay, arrived, win, wout, ga, gm],
        kept_out=saved_shapes(width, hidden, tokens),
        scratch=forward_scratch(width, hidden, tokens), smem=[shift], name="decoder", cost=15,
    )


def gain_shape(win):
    return (1, win.shape[1])


def decoder_back_kernel(shift, dy, x, win, wout, ga, gm, *rest):
    kept, (dx, stay, send, gwin, gwout, gga, ggm), scratch = rest[:5], rest[5:12], rest[12:]
    copies = fetch_block(kept, scratch)
    grad = block_backward(
        dy[...], x[...], win, wout, ga[...], gm[...], copies, scratch, gwin, gwout, gga, ggm
    )
    dx[...] = grad
    pack(shift, grad, stay, send)


def decoder_back(shift, dy, x, saved, win, wout, ga, gm):
    width, tokens = x.shape
    half = half_shape(shift, width, tokens)
    return call(
        decoder_back_kernel,
        [x.shape, half, half, win.shape, wout.shape, gain_shape(win), gain_shape(win)],
        [dy, x, win, wout, ga, gm], kept_in=saved,
        scratch=backward_scratch(width, win.shape[0] - 3 * width, tokens),
        smem=[shift], name="decoder_back", cost=24,
    )


def merging_mlp_back_kernel(stay_in, send_in, last, wback, win, wout, gm, *rest):
    kept, (gback, gwout, ggm, dmid, da, gwin_out), scratch = rest[:3], rest[3:9], rest[9:]
    *slots, nh, nl, yh, yl, hh, hl, gwin, sems, sem = scratch
    copies = fetch(kept, slots, sems)
    dz = split(to_windows(stay_in, send_in))
    gback[...] = dot3(split(last[...]), dz, NT)
    dlast = dot3(split(wback[...]), dz, NN)
    at = win.shape[0] - gwin.shape[0]
    dmid[...] = mlp_back(
        dlast, win.at[at:], wout, gm[...], copies, slots, ((nh, nl), (yh, yl), (hh, hl)), da,
        gwin, gwout, ggm,
    )
    copy = pltpu.make_async_copy(gwin, gwin_out.at[at:], sem)
    copy.start()
    copy.wait()


def merging_mlp_back(stay, arrived, last, saved, wback, win, wout, gm):
    width, tokens = last.shape
    hidden = win.shape[0] - 3 * width
    wide = (width, tokens)
    scratch = [pltpu.VMEM(s, F32) for s in (wide, (hidden, tokens), wide)]
    scratch += [pltpu.VMEM(wide, BF16)] * 4 + [pltpu.VMEM((hidden, tokens), BF16)] * 2
    scratch += [pltpu.VMEM((hidden, width), F32), pltpu.SemaphoreType.DMA((3,)), pltpu.SemaphoreType.DMA]
    return call(
        merging_mlp_back_kernel, [wback.shape, wout.shape, gain_shape(win), wide, wide],
        [stay, arrived, last, wback, win, wout, gm],
        kept_in=[saved[2], saved[3], saved[1]], kept_out=[win.shape], scratch=scratch,
        name="merging_mlp_back", cost=36,
    )


def merging_attention_back_kernel(dmid, da, x, wide_x, wup, ga, *rest):
    (p_in, qkv_in, win_in, _), (stay, send, gup, gga, gwin_out) = rest[:4], rest[4:9]
    weights, qkv, win, nh, nl, hh, hl, gwin, sems, sem = rest[9:]
    copies = fetch([p_in, qkv_in, win_in.at[: win.shape[0]]], [weights, qkv, win], sems)
    grad = attention_back(
        dmid[...], wide_x[...], win, ga[...], copies, (weights, qkv), ((nh, nl), (hh, hl)), da,
        gwin, gga,
    )
    copy = pltpu.make_async_copy(gwin, gwin_out.at[: gwin.shape[0]], sem)
    copy.start()
    grad = split(grad)
    gup[...] = dot3(grad, split(x[...]), NT)
    from_windows(dot3(split(wup[...]), grad, TN), stay, send)
    copy.wait()


def merging_attention_back(dmid, da, x, wide_x, saved, wup, win, ga, gwin, halved):
    width, tokens = wide_x.shape
    rows = 3 * width
    scratch = [pltpu.VMEM(saved[4].shape, F32), pltpu.VMEM(saved[0].shape, F32)]
    scratch += [pltpu.VMEM((rows, width), F32)] + [pltpu.VMEM((width, tokens), BF16)] * 2
    scratch += [pltpu.VMEM((rows, tokens), BF16)] * 2 + [pltpu.VMEM((rows, width), F32)]
    return call(
        merging_attention_back_kernel, [halved, halved, wup.shape, gain_shape(win)],
        [dmid, da, x, wide_x, wup, ga], kept_in=[saved[4], saved[0], win, gwin],
        kept_out=[win.shape],
        scratch=scratch + [pltpu.SemaphoreType.DMA((3,)), pltpu.SemaphoreType.DMA],
        name="merging_attention_back", cost=27, aliases={9: 4},
    )


def encoder_back_kernel(shift, dy, stay_in, send_in, x, win, wout, ga, gm, *rest):
    kept, (dx, gwin, gwout, gga, ggm), scratch = rest[:5], rest[5:10], rest[10:]
    copies = fetch_block(kept, scratch)
    start = dy[...] + unpack(shift, stay_in, send_in)
    dx[...] = block_backward(
        start, x[...], win, wout, ga[...], gm[...], copies, scratch, gwin, gwout, gga, ggm
    )


def encoder_back(shift, dy, stay, arrived, x, saved, win, wout, ga, gm):
    width, tokens = x.shape
    return call(
        encoder_back_kernel,
        [x.shape, win.shape, wout.shape, gain_shape(win), gain_shape(win)],
        [dy, stay, arrived, x, win, wout, ga, gm], kept_in=saved,
        scratch=backward_scratch(width, win.shape[0] - 3 * width, tokens),
        smem=[shift], name="encoder_back", cost=23,
    )


def head_kernel(chans, x_ref, gain, w_ref, t_ref, gx, gw_ref, gg_ref, sums, nh, nl, dh, dl, acc, loss):
    k = pl.program_id(0)
    samples, rows, tokens = t_ref.shape

    @pl.when(k == 0)
    def _():
        put((nh, nl), normalise(x_ref[...])[0] * gain[...])
        loss[...] = jnp.zeros_like(loss)
        acc[...] = jnp.zeros_like(acc)

    weight = split(w_ref[...])
    pred = dot3(weight, both((nh, nl)), TN)
    for s in range(samples):
        lanes = slice(s * tokens, s * tokens + tokens)
        for at in range(0, rows, CH):
            target = t_ref[s, at : at + CH, :]
            scaled = target[chans : chans + 1, :]
            differ = pred[at : at + CH, lanes] - target
            differ = jnp.where(iota(target.shape, 0) < chans, differ, 0.0)
            dp = scaled * differ
            loss[0:1, :] += jnp.sum(dp * differ, axis=0, keepdims=True)
            loss[1:2, :] += scaled
            dh[at : at + CH, lanes], dl[at : at + CH, lanes] = split(dp)
    put_bands(gw_ref, dot3(both((nh, nl)), both((dh, dl)), NT))
    acc[...] += dot3(weight, both((dh, dl)), NN)

    @pl.when(k == pl.num_programs(0) - 1)
    def _():
        hat, scale = normalise(x_ref[...])
        dn = acc[...]
        gg_ref[...] = lane_sums(dn * hat)
        gx[...] = normalise_back(dn, hat, scale, gain[...])
        sums[...] = jnp.sum(loss[...], axis=1, keepdims=True) + jnp.zeros_like(sums)


def head(x, gain, weight, target, chans, bands):
    samples, _, tokens = target.shape
    width = x.shape[0]
    chunks, _, rows = weight.shape
    fixed = lambda shape: pl.BlockSpec(shape, lambda k: (0,) * len(shape))
    piece = pl.BlockSpec((None, width, rows), lambda k: (k, 0, 0))
    return pl.pallas_call(
        functools.partial(head_kernel, chans),
        out_shape=[
            jax.ShapeDtypeStruct(x.shape, F32),
            jax.ShapeDtypeStruct((bands, chunks * width // bands, rows), F32),
            jax.ShapeDtypeStruct((1, width), F32),
            jax.ShapeDtypeStruct((8, 128), F32),
        ],
        grid=(chunks,),
        in_specs=[
            fixed(x.shape),
            fixed((width, 1)),
            piece,
            pl.BlockSpec((samples, rows, tokens), lambda k: (0, k, 0)),
        ],
        out_specs=[
            fixed(x.shape),
            pl.BlockSpec((bands, width // bands, rows), lambda k: (0, k, 0)),
            fixed((1, width)),
            fixed((8, 128)),
        ],
        scratch_shapes=[pltpu.VMEM(x.shape, BF16)] * 2
        + [pltpu.VMEM((rows, x.shape[1]), BF16)] * 2
        + [pltpu.VMEM(x.shape, F32), pltpu.VMEM((8, tokens), F32)],
        compiler_params=params(1),
        cost_estimate=takes(25),
        name="head",
    )(x, gain, weight, target)


def swap(value, axis, bit):
    return lax.ppermute(value, axis, [(i, i ^ bit) for i in range(lax.axis_size(axis))])


def pick(value, at, axis):
    return lax.dynamic_index_in_dim(value, at, axis, keepdims=False)


def place_of():
    lat, dp = lax.axis_index("lat"), lax.axis_index("dp")
    return lat // 2, lat % 2, dp // 2, dp % 2


def along(first, last):
    return [(2 * k + y, 2 * (k + 1) + y) for k in range(first, last) for y in range(2)]


def backwards(pairs):
    return [(7 - a, 7 - b) for a, b in pairs]


def line_sum(parts, z, meanwhile=()):
    right = left = None
    for step in (1, 2, 3):
        ahead = pick(parts, jnp.clip(z + 4 - step, 0, 3), 0)
        behind = pick(parts, jnp.clip(z + step - 4, 0, 3), 0)
        if right is not None:
            ahead, behind = ahead + right, behind + left
        right = lax.ppermute(ahead, "lat", along(0, step))
        left = lax.ppermute(behind, "lat", backwards(along(0, step)))
        if step <= len(meanwhile):
            right, left = tie((right, left), meanwhile[step - 1])
    return pick(parts, z, 0) + right + left


def ordered(mine, other, which, axis=0):
    shape = mine.shape
    at = jnp.arange(2).reshape((1,) * axis + (2,) + (1,) * (mine.ndim - axis))
    joined = jnp.where(at == which, jnp.expand_dims(mine, axis), jnp.expand_dims(other, axis))
    return joined.reshape(shape[:axis] + (2 * shape[axis],) + shape[axis + 1 :])


AXES = {"c": ("dp", 1, 3), "x": ("dp", 2, 2), "y": ("lat", 1, 1)}


class Halving:
    def __init__(self, buf, over):
        self.axis, self.bit, at = AXES[over]
        own = place_of()[at]
        bands, rows, lanes = buf.shape
        parts = buf.reshape((4, 2, rows, lanes) if over == "y" else (8, 2, rows // 2, lanes))
        self.keep, self.give = pick(parts, own, 1), pick(parts, 1 - own, 1)

    def ahead_of(self, value):
        value, self.give = lax.optimization_barrier((value, self.give))
        return value

    def done(self, beside=None):
        return self.keep + tie(swap(self.give, self.axis, self.bit), beside)


def halve(buf, over, beside=None):
    return Halving(buf, over).done(beside)


def over_x(quarters, sums):
    x = place_of()[2]
    return [ordered(v, swap(v, "dp", 2), x) for v in quarters] + [v + swap(v, "dp", 2) for v in sums]


def collect_kernel(sizes, core, *refs):
    halves_in, outs = refs[:10], refs[10:]
    first = core[0] == 0

    def joined(at):
        mine, got = halves_in[at][...], halves_in[at + 5][...]
        return jnp.concatenate([jnp.where(first, mine, got), jnp.where(first, got, mine)], axis=0)

    embed_o, in0_o, in1_o, out0_o, out1_o, up_o, back_o, fin_o, fout_o, head_o, extra_o = outs
    n_fin, n_in, n_out = sizes
    width = in0_o.shape[1]
    rows = embed_o.shape[1]
    part = joined(0)
    fin_o[...] = part[:n_fin, :]
    up_o[...], back_o[...] = part[n_fin:, :width], part[n_fin:, width:]
    part, late, early = joined(1), joined(2), joined(4)
    fout_o[...] = joined(3)
    for k in range(embed_o.shape[0]):
        embed_o[k] = part[k * rows : k * rows + rows, :]
        head_o[k] = late[k * rows : k * rows + rows, :]
    at = embed_o.shape[0] * rows
    n_pair = (n_in + n_out) // 2
    for block, into_in, into_out in ((late[at:, :], in1_o, out1_o), (early, in0_o, out0_o)):
        tall = jnp.concatenate([block[:n_pair, :width], block[:n_pair, width:]], axis=0)
        into_in[...] = tall[:n_in, :]
        into_out[...] = tall[n_in:, :]
    extra_o[...] = early[n_pair : n_pair + 8, :]


def collect(parts, rows_in, rows_out, rows_fin, rows_up, width):
    got = [swap(p, "dp", 1) for p in parts]
    shapes = [
        (8, width // 8, 2 * width), (rows_in, width), (rows_in, width), (rows_out, width),
        (rows_out, width), (rows_up, width), (rows_up, width), (rows_fin, 2 * width),
        (2 * parts[3].shape[0], 2 * width), (8, width // 8, 2 * width), (8, 2 * width),
    ]
    core = place_of()[3].reshape(1)
    return call(
        functools.partial(collect_kernel, (rows_fin, rows_in, rows_out)), shapes,
        [*parts, *got], smem=[core], name="collect",
    )


def tie(first, second):
    if second is None:
        return first
    return lax.optimization_barrier((first, second))[0]


def line_gather(piece, z, beside):
    right = left = piece
    arrived = []
    for step in (1, 2, 3):
        right = lax.ppermute(right, "lat", along(step - 1, 3))
        left = lax.ppermute(left, "lat", backwards(along(step - 1, 3)))
        if step <= len(beside):
            right, left = tie((right, left), beside[step - 1](arrived[-1:]))
        arrived.append((step, right, left))
    def at(k):
        chosen = piece
        for step, right, left in arrived:
            if k + step < 4:
                chosen = jnp.where(z == k + step, right, chosen)
            if k - step >= 0:
                chosen = jnp.where(z == k - step, left, chosen)
        return chosen

    return jnp.stack([at(k) for k in range(4)])


def gather_bands(q, h, beside):
    z, y, x, c = place_of()
    lanes = q.shape[-1]
    quarter, rest = q.shape[0] // 4, h.shape[0] // 2
    q = pick(q.reshape(4, quarter, lanes), c * 2 + x, 0)
    h = pick(h.reshape(2, rest, lanes), c, 0)
    return line_gather(jnp.concatenate([q, h]), z, beside), quarter


def gather_rest(full, quarter, first, second):
    z, y, x, c = place_of()
    q, h = full[:, :quarter], full[:, quarter:]
    lay = lambda mine, got: ordered(mine[:, None], got[:, None], y, axis=1).reshape(
        8, *mine.shape[1:]
    )
    got = tie(swap(q, "lat", 1), first)
    h = tie(h, got)
    q = lay(q, got)
    h_got, q_got = tie(swap(h, "lat", 1), second), tie(swap(q, "dp", 2), second)
    h, q = lay(h, h_got), ordered(q, q_got, x, axis=1)
    return q, swap(q, "dp", 1), h, swap(h, "dp", 1)


def join_kernel(core, q, q_got, h, h_got, q_out, h_out):
    first = core[0] == 0
    bands = q.shape[0]
    for mine, got, out in ((q, q_got, q_out), (h, h_got, h_out)):
        rows, half = out.shape[0] // bands, mine.shape[1]
        for band in range(bands):
            at = band * rows
            low, high = mine[band], got[band]
            out[at : at + half, :] = jnp.where(first, low, high)
            out[at + half : at + rows, :] = jnp.where(first, high, low)[: rows - half, :]


def join_cores(q, q_got, h, h_got, rows_q, rows_h):
    shapes = [(8 * rows_q, q.shape[2]), (8 * rows_h, q.shape[2])]
    core = place_of()[3].reshape(1)
    return call(join_kernel, shapes, [q, q_got, h, h_got], smem=[core], name="join")


def gather_all(shard):
    rows, lanes = shard.shape
    mine = pick(shard.reshape(4, rows // 4, lanes), lax.axis_index("dp"), 0)
    return lax.all_gather(mine, ("lat", "dp"), axis=0, tiled=True).reshape(-1, rows, lanes)


def widen_pair(top, bottom):
    both = jnp.concatenate([top, bottom], axis=-2)
    half = both.shape[-2] // 2
    return jnp.concatenate([both[..., :half, :], both[..., half:, :]], axis=-1)


def narrow_pair(both, rows):
    width = both.shape[-1] // 2
    flat = jnp.concatenate([both[..., :width], both[..., width:]], axis=-2)
    return flat[..., :rows, :], flat[..., rows:, :]


def flat(value):
    return value.reshape(-1, value.shape[-1])


def banded(value, bands):
    return value.reshape(bands, -1, value.shape[-1])


def gather_weights(shards, gains, beside):
    in0, in1, out0, out1, up, back, fin, fout, embed_w, head_w = shards
    if (lax.axis_size("dp"), lax.axis_size("lat")) != (4, 8):
        whole_of = lambda s: lax.all_gather(s, "lat", axis=0, tiled=True)
        embed_w, head_w = (
            whole_of(s.transpose(1, 0, 2)).transpose(1, 0, 2) for s in (embed_w, head_w)
        )
        rest = [whole_of(s) for s in shards[:8]]
        columns = [g.reshape(-1, 1) for g in whole_of(gains.T).T]
        columns[5:] = [jnp.concatenate(columns[5:7]), jnp.concatenate(columns[7:9])]
        return [*rest, embed_w, head_w], columns
    n_in, n_fin, width = in0.shape[0], fin.shape[0], in0.shape[1]
    n_embed = 8 * (width // 8)
    pair = widen_pair(in0, out0)
    n_pair = pair.shape[0]
    row = jnp.pad(gains.reshape(1, -1), ((0, 31), (0, 2 * width - gains.size)))
    early = jnp.concatenate([flat(embed_w), pair, jnp.concatenate([up, back], axis=-1), row])
    early = gather_all(early)
    spare = -n_fin % 32
    middle = gather_bands(jnp.pad(fin, ((0, spare), (0, 0))), fout, beside)
    late = [widen_pair(in1, out1), flat(head_w), jnp.zeros((16, 2 * width), F32)]
    late = gather_all(jnp.concatenate(late))
    n_out = out0.shape[0]
    w_embed, w_in0, w_out0, w_up, w_back, *all_gains = unpack_early(
        early, n_embed, n_in, n_out, up.shape[0], gains.shape[0], width
    )
    w_head, w_in1, w_out1 = unpack_late(late, n_embed, n_in, n_out, width)
    return [
        w_in0, w_in1, w_out0, w_out1, w_up, w_back, middle, None, w_embed, w_head
    ], all_gains


def unpack_chunks(ref, at, out):
    bands, chunks = ref.shape[0], out.shape[0]
    rows = out.shape[1] // bands
    for band in range(bands):
        for k in range(chunks):
            start = at + k * rows
            out[k, band * rows : band * rows + rows, :] = ref[band, start : start + rows, :]


def unpack_pair(ref, at, into_in, into_out):
    bands = ref.shape[0]
    width = into_in.shape[1]
    n_in, n_out = into_in.shape[0] // bands, into_out.shape[0] // bands
    end = at + (n_in + n_out) // 2
    for band in range(bands):
        block = ref[band, at:end, :]
        tall = jnp.concatenate([block[:, :width], block[:, width:]], axis=0)
        into_in[band * n_in : band * n_in + n_in, :] = tall[:n_in, :]
        into_out[band * n_out : band * n_out + n_out, :] = tall[n_in:, :]


def unpack_early_kernel(n_embed, early, embed_o, in_o, out_o, up_o, back_o, *gain_o):
    bands, width = early.shape[0], in_o.shape[1]
    unpack_chunks(early, 0, embed_o)
    unpack_pair(early, n_embed, in_o, out_o)
    n_up = up_o.shape[0] // bands
    at = n_embed + (in_o.shape[0] + out_o.shape[0]) // bands // 2
    part = width // bands
    for band in range(bands):
        rows = slice(band * n_up, band * n_up + n_up)
        up_o[rows, :] = early[band, at : at + n_up, :width]
        back_o[rows, :] = early[band, at : at + n_up, width:]
        line = early[band, at + n_up : at + n_up + 1, :]
        shape = (part, line.shape[1])
        start = 0
        for out in gain_o:
            for block in range(out.shape[0] // width):
                hit = iota(shape, 1) == start + iota(shape, 0)
                column = jnp.sum(jnp.where(hit, line, 0.0), axis=1, keepdims=True)
                row = block * width + band * part
                out[row : row + part, :] = column
                start += part


def unpack_early(early, n_embed, n_in, n_out, n_up, n_gain, width):
    shapes = [
        (8, width, early.shape[2]), (8 * n_in, width), (8 * n_out, width), (8 * n_up, width),
        (8 * n_up, width), *[(width, 1)] * (n_gain - 4), (2 * width, 1), (2 * width, 1),
    ]
    body = functools.partial(unpack_early_kernel, n_embed)
    return call(body, shapes, [early], name="unpack_early")


def unpack_late_kernel(late, head_o, in_o, out_o):
    unpack_pair(late, 0, in_o, out_o)
    unpack_chunks(late, (in_o.shape[0] + out_o.shape[0]) // late.shape[0] // 2, head_o)


def unpack_late(late, n_embed, n_in, n_out, width):
    shapes = [(8, width, late.shape[2]), (8 * n_in, width), (8 * n_out, width)]
    return call(unpack_late_kernel, shapes, [late], name="unpack_late")


def pack_early_kernel(gwin, gwout, gg0, gg1, gg2, gg3, gg4, gga, ggm, sums, out):
    bands, width = out.shape[0], gwin.shape[1]
    n_in, n_out = gwin.shape[0] // bands, gwout.shape[0] // bands
    n_pair, part = (n_in + n_out) // 2, width // bands
    for band in range(bands):
        tall = jnp.concatenate(
            [gwin[band * n_in : band * n_in + n_in, :], gwout[band * n_out : band * n_out + n_out, :]],
            axis=0,
        )
        out[band, :n_pair, :width] = tall[:n_pair, :]
        out[band, :n_pair, width:] = tall[n_pair:, :]
        line = []
        for ref in (gg0, gg1, gg2, gg3, gg4, gga, ggm):
            for start in range(band * part, ref.shape[1], width):
                line.append(ref[:, start : start + part])
        line += [sums[0:1, 0:1], sums[1:2, 0:1]]
        used = 9 * part + 2
        line = jnp.concatenate(line + [jnp.zeros((1, out.shape[2] - used), F32)], axis=1)
        out[band, n_pair:, :] = jnp.where(iota((out.shape[1] - n_pair, 1), 0) == 0, line, 0.0)


def pack_early(gwin, gwout, gains, sums):
    rows = (gwin.shape[0] + gwout.shape[0]) // 16 + 16
    shape = (8, rows, 2 * gwin.shape[1])
    return call(pack_early_kernel, [shape], [gwin, gwout, *gains, sums], name="pack_early")[0]


LINE = 384
OTHERS = 24
OWN_AT = 32


def pieces(ref):
    return [slice(at, min(at + LINE, ref.shape[1])) for at in range(0, ref.shape[1], LINE)]


def chunks_of(ref):
    return [ref[:, piece] for piece in pieces(ref)]


def squares(value, rescale):
    value = value * rescale
    return value * value + 1e-30


def as_lane(column):
    shape = (column.shape[0], LINE)
    return jnp.sum(jnp.where(iota(shape, 0) == iota(shape, 1), column, 0.0), axis=0, keepdims=True)


def as_column(line, rows):
    shape = (rows, LINE)
    return jnp.sum(jnp.where(iota(shape, 0) == iota(shape, 1), line, 0.0), axis=1, keepdims=True)


def at_lane(value, lane):
    return jnp.where(iota((1, LINE), 1) == lane, value, 0.0)


def total(value):
    return jnp.sum(jnp.sum(value, axis=1, keepdims=True), axis=0, keepdims=True)


def stats_kernel(bands, count, *refs):
    grads, mats = refs[:count], refs[count : 2 * count]
    rescale_ref, gains, out = refs[2 * count :]
    rescale = rescale_ref[...]
    out[...] = jnp.zeros_like(out)
    row = 0
    energy = jnp.zeros((1, LINE), F32)
    for i, (g, w) in enumerate(zip(grads, mats)):
        own = 0.0
        for part, weight in zip(chunks_of(g), chunks_of(w)):
            square = squares(part, rescale)
            own = own + jnp.sum(square, axis=1, keepdims=True)
            other = jnp.sum(square, axis=0, keepdims=True) / (square.shape[0] * bands)
            out[row : row + 1, : other.shape[1]] = other
            row += 1
            energy = energy + at_lane(total(weight * weight), i)
        out[OWN_AT + i : OWN_AT + i + 1, :] = as_lane(own / g.shape[1])
    out[row : row + 1, :] = energy
    out[row + 1 : row + 2, :] = as_lane(jnp.sum(gains[...] * gains[...], axis=1, keepdims=True))


def new_stats(i, row, g, rescale, turned, sums, other_stats, own_stats, own_mean):
    parts = chunks_of(g)
    own, others, mean_sum, stat_sum = 0.0, [], 0.0, 0.0
    for k, part in enumerate(parts):
        own = own + jnp.sum(squares(part, rescale), axis=1, keepdims=True)
        wide = part.shape[1]
        mean = sums[row + k : row + k + 1, :wide]
        stat = other_stats[row + k : row + k + 1, :wide]
        others.append(0.5 * stat + 0.5 * mean)
        mean_sum = mean_sum + total(mean)
        stat_sum = stat_sum + total(stat)
    columns = g.shape[1]
    own = 0.5 * as_column(own_stats[i : i + 1, :], own.shape[0]) + 0.5 * (own / columns)
    stat_mean = stat_sum / columns if turned else own_mean[0:1, i : i + 1]
    return others, own, 0.5 * stat_mean + 0.5 * (mean_sum / columns)


def update_kernel(turned, count, *refs):
    grads, own_stats = refs[:count], refs[count]
    rescale_ref, sums, other_stats, own_mean, g_gain, v_gain, out, next_v, *updates = refs[count + 1 :]
    rescale = rescale_ref[...]
    row = 0
    energy = jnp.zeros((1, LINE), F32)
    for i, g in enumerate(grads):
        others, own, mean = new_stats(
            i, row, g, rescale, turned[i], sums, other_stats, own_stats, own_mean
        )
        for piece, other in zip(pieces(g), others):
            update = g[:, piece] * rescale * lax.rsqrt(own * other / mean)
            updates[i][:, piece] = update
            energy = energy + at_lane(total(update * update), i)
        row += len(others)
    grad = g_gain[...] * rescale
    value = 0.5 * v_gain[...] + 0.5 * (grad * grad + 1e-30)
    next_v[...] = value
    update = grad * lax.rsqrt(value)
    updates[count][...] = update
    out[...] = jnp.zeros_like(out)
    out[0:1, :] = energy
    out[1:2, :] = as_lane(jnp.sum(update * update, axis=1, keepdims=True))


def step_kernel(bands, count, *refs):
    updates, mats = refs[: count + 1], refs[count + 1 : 2 * count + 2]
    squares_u, squares_w = refs[2 * count + 2 : 2 * count + 4]
    outs = refs[2 * count + 4 :]
    news, copies = outs[: len(outs) // 2], outs[len(outs) // 2 :]
    where = [(0, None), (1, 0), (1, 1), (2, 0), (2, 1), (3, 0), (3, 1)]
    where += [(4, None), (5, None), (6, None), (7, None)]
    for i, (u, w, (out, pair)) in enumerate(zip(updates, mats, where)):
        new, copy = news[out], copies[out]
        if i < count:
            entries = u.shape[0] * u.shape[1] * bands
            energy_u, energy_w = squares_u[0:1, i : i + 1], squares_w[0:1, i : i + 1]
        else:
            entries = u.shape[1] * bands
            energy_u, energy_w = (
                as_column(s[1:2, :], u.shape[0]) for s in (squares_u, squares_w)
            )
        clip = jnp.maximum(1.0, jnp.sqrt(energy_u / entries) / 0.25)
        size = jnp.maximum(0.001, jnp.sqrt(energy_w / entries))
        value = w[...] - size * (u[...] / clip)
        if out == 2:
            value = value.T
        at = Ellipsis if pair is None else pair
        new[at] = value
        copy[at] = value.astype(BF16)


def plain_call(body, shapes, args, name, rounded=()):
    vmem = pl.BlockSpec(memory_space=pltpu.VMEM)
    outs = [jax.ShapeDtypeStruct(tuple(s), F32) for s in shapes]
    outs += [jax.ShapeDtypeStruct(tuple(s), BF16) for s in rounded]
    shapes = outs
    return pl.pallas_call(
        body,
        out_shape=outs,
        in_specs=[vmem] * len(args),
        out_specs=[vmem] * len(shapes),
        compiler_params=pltpu.CompilerParams(vmem_limit_bytes=VMEM),
        cost_estimate=takes(4),
        name=name,
    )(*args)


def band_sum_and_gather(sums, mine):
    bit = 1
    while bit < lax.axis_size("lat"):
        got = swap(jnp.concatenate([sums, mine]), "lat", bit)
        n = sums.shape[0]
        sums = sums + got[:n]
        mine = ordered(mine, got[n:], (lax.axis_index("lat") // bit) % 2)
        bit *= 2
    return sums, mine


def lines(line):
    return jnp.pad(line, (0, -line.shape[0] % LINE)).reshape(-1, LINE)


class Moments:
    def __init__(self, mats, turned, row_stats, col_stats):
        bands, band = lax.axis_size("lat"), lax.axis_index("lat")
        self.mats, self.turned, self.bands = mats, turned, bands
        self.rows = [m.shape[-2] for m in mats]
        other_lines, self.own, means = [], [], []
        row_at = col_at = 0
        for m, turn in zip(mats, turned):
            split_size = m.shape[-2] * bands
            columns = m.shape[1]
            n_row, n_col = (columns, split_size) if turn else (split_size, columns)
            row, col = row_stats[row_at : row_at + n_row], col_stats[col_at : col_at + n_col]
            row_at, col_at = row_at + n_row, col_at + n_col
            other, mine = (row, col) if turn else (col, row)
            other_lines.append(lines(other))
            mine = lax.dynamic_slice_in_dim(mine, band * m.shape[-2], m.shape[-2])
            self.own.append(lines(mine))
            means.append(jnp.mean(row).reshape(1, 1))
        self.other = jnp.concatenate(other_lines)
        self.own = jnp.pad(jnp.concatenate(self.own), ((0, 16 - len(mats)), (0, 0)))
        self.mean = jnp.pad(jnp.concatenate(means, axis=1), ((0, 0), (0, LINE - len(mats))))
        self.row_stats, self.col_stats = row_stats, col_stats

    def step(self, grads, rescale, gains, g_gain, v_gain):
        count = len(grads)
        rescale = rescale.reshape(1, 1)
        shape = (OWN_AT + 16, LINE)
        (stats,) = plain_call(
            functools.partial(stats_kernel, self.bands, count), [shape],
            [*grads, *self.mats, rescale, gains], "stats",
        )
        sums, own = band_sum_and_gather(stats[:OWN_AT], stats[OWN_AT:])
        out, next_v, *updates = plain_call(
            functools.partial(update_kernel, tuple(self.turned), count),
            [(8, LINE), gains.shape, *[g.shape for g in grads], gains.shape],
            [*grads, self.own, rescale, sums, self.other, self.mean, g_gain, v_gain], "update",
        )
        bit = 1
        while bit < self.bands:
            out = out + swap(out, "lat", bit)
            bit *= 2
        shapes = [g.shape for g in grads]
        shapes = [
            shapes[0], (2, *shapes[1]), (2, *shapes[3][::-1]), (2, *shapes[5]), *shapes[7:], gains.shape
        ]
        news = plain_call(
            functools.partial(step_kernel, self.bands, count), shapes,
            [*updates, *self.mats, gains, out, sums[OTHERS : OTHERS + 8]], "step", shapes,
        )
        own = own.reshape(self.bands, 16, LINE)
        row_means, col_means = [], []
        row = 0
        for i, (m, turn) in enumerate(zip(self.mats, self.turned)):
            mine = own[:, i, : self.rows[i]].reshape(-1)
            taken = -(-m.shape[1] // LINE)
            other = sums[row : row + taken].reshape(-1)[: m.shape[1]]
            row += taken
            row_means.append(other if turn else mine)
            col_means.append(mine if turn else other)
        next_rows = 0.5 * self.row_stats + 0.5 * jnp.concatenate(row_means)
        next_cols = 0.5 * self.col_stats + 0.5 * jnp.concatenate(col_means)
        return news[: len(shapes)], news[len(shapes) :], next_rows, next_cols, next_v


def pixel_columns(flat_rows):
    rows, depth = flat_rows.shape
    moved = flat_rows.reshape(rows, depth // 16, 4, 4).transpose(3, 2, 0, 1)
    moved = jnp.pad(moved, ((0, 0), (0, 0), (0, 0), (0, CH - depth // 16)))
    return moved.reshape(8, 2, rows, CH).transpose(0, 2, 1, 3).reshape(8, rows, 2 * CH)


def channel_columns(chunks, chans):
    rows = chunks.shape[1]
    moved = chunks.reshape(4, 2, rows, 2, CH)[..., :chans]
    return moved.transpose(2, 4, 1, 3, 0).reshape(rows, chans * 16)


def shifted(value, axis, by):
    peers = lax.axis_size(axis)
    return lax.ppermute(value, axis, [(i, (i + by) % peers) for i in range(peers)])


def scatter_plain(grads, chunked, g_gain, total, count):
    scatter = lambda g, axis: lax.psum_scatter(g, "lat", scatter_dimension=axis, tiled=True)
    total, count = lax.psum((total, count), ("dp", "lat"))
    grads = [scatter(g, 0) for g in grads]
    chunked = [scatter(g, 1) for g in chunked]
    grads, chunked, g_gain = lax.psum((grads, chunked, scatter(g_gain, 1)), "dp")
    return grads, chunked, g_gain, total, count


def on_device(
    fields, target, valid_mask, sample_index, weight_table, lon_shift, w_embed, w_in, w_out,
    w_merge, w_fin, w_fout, w_head, gains, row_stats, col_stats, v_gain,
):
    band_count = lax.axis_size("lat")
    band_index = lax.axis_index("lat")
    samples, chans, rows_dev, across = fields.shape
    width = w_in.shape[1]
    total_rows = rows_dev * band_count
    pixel_rows = (band_index * rows_dev + jnp.arange(rows_dev)).astype(F32)
    coslat = jnp.cos((90.0 - (pixel_rows + 0.5) * 180.0 / total_rows) * (jnp.pi / 180.0))
    picked = (sample_index[:, None] == jnp.arange(weight_table.shape[0])[None, :]).astype(F32)
    sample_weight = jnp.sum(picked * weight_table[None, :], axis=1)
    weight = sample_weight[:, None, None] * coslat[None, :, None] * valid_mask.astype(F32)

    mats = [
        w_embed.T, w_in[0].T, w_in[1].T, w_out[0], w_out[1], w_merge[0].T, w_merge[1].T, w_fin.T,
        w_fout, w_head,
    ]
    turned = [True, True, True, False, False, True, True, True, False, False]
    moments = Moments(mats, turned, row_stats, col_stats)
    shards = mats[1:9] + [pixel_columns(mats[0]), pixel_columns(mats[9])]
    apart = (lax.axis_size("dp"), band_count) == (4, 8)
    high, low = prep(lon_shift, fields)
    lines_ready = (moments.own, moments.other, moments.mean)
    late = []

    def prepare(arrived):
        token = tie(lon_shift, [a[1:] for a in arrived]) if arrived else lon_shift
        late.append(prep(token, target, weight))
        return late[0]

    whole_weights, (*gain, gain_a, gain_m) = gather_weights(
        shards, gains, (lambda arrived: (high, lines_ready), prepare)
    )
    wanted = late[0] if late else prepare([])
    f_in0, f_in1, f_out0, f_out1, f_up, f_back, f_fin, f_fout, f_embed, f_head = whole_weights
    stream = embed(f_embed, high, low)
    own, stay, send, *kept_e = encoder(lon_shift, stream, f_in0, f_out0, gain[0], gain[1])
    if apart:
        q, q_got, h, h_got = gather_rest(*f_fin, stream, own)
        f_fin, f_fout = join_cores(q, q_got, h, h_got, w_fin.shape[1], w_fout.shape[0])
    send = shifted(send, "lat", -1)
    rolled, wide, last, stay, send, *kept_m = merging(
        stay, send, f_up, f_back, f_fin, f_fout, gain_a, gain_m
    )
    send = shifted(send, "lat", 1)
    start, out, *kept_d = decoder(lon_shift, own, stay, send, f_in1, f_out1, gain[2], gain[3])
    grad, g_head, gg_final, sums = head(
        out, gain[4], f_head, wanted, chans, 8 if apart else 1
    )
    b = lambda g: banded(g, 8)
    grad, stay, send, g_in1, g_out1, gg_2, gg_3 = decoder_back(
        lon_shift, grad, start, kept_d, f_in1, f_out1, gain[2], gain[3]
    )
    send = shifted(send, "lat", -1)
    if apart:
        s_a = halve(
            jnp.concatenate([g_head, widen_pair(b(g_in1), b(g_out1))], axis=1), "c"
        )
        s_a = lax.psum_scatter(flat(s_a), "lat", scatter_dimension=0, tiled=True)
    g_back, g_fout, gg_m, between, attended, g_fin = merging_mlp_back(
        stay, send, last, kept_m, f_back, f_fin, f_fout, gain_m
    )
    stay, send, g_up, gg_a, g_fin = merging_attention_back(
        between, attended, rolled, wide, kept_m, f_up, f_fin, gain_a, g_fin, stay.shape
    )
    send = shifted(send, "lat", 1)
    if apart:
        s_f = halve(b(g_fout), "c", beside=stay)
        s_m = [b(g_fin), jnp.concatenate([b(g_up), b(g_back)], axis=-1)]
        s_m = jnp.concatenate(s_m, axis=1)
        started_f, started_m = Halving(s_f, "y"), Halving(halve(s_m, "c"), "x")
        send = started_m.ahead_of(started_f.ahead_of(send))
    grad, g_in0, g_out0, gg_0, gg_1 = encoder_back(
        lon_shift, grad, stay, send, stream, kept_e, f_in0, f_out0, gain[0], gain[1]
    )
    gain_rows = [gg_0, gg_1, gg_2, gg_3, gg_final, gg_a, gg_m]
    if apart:
        z = place_of()[0]
        s_f, s_m = started_f.done(grad), started_m.done(grad)
        s_c = pack_early(g_in0, g_out0, gain_rows, sums)
        started_m, started_c = Halving(s_m, "y"), Halving(s_c, "c")
        grad = started_c.ahead_of(started_m.ahead_of(grad))
    g_embed = embed_back(grad, high, low, 8 if apart else 1)
    if apart:
        s_m, s_c = started_m.done(g_embed), started_c.done(g_embed)
        s_d = halve(g_embed, "c")
        s_c = halve(s_c, "y")
        s_d = halve(s_d, "x")
        s_d = halve(s_d, "y")
        n_d = s_d.shape[1]
        s_f = line_sum(s_f, z, (g_embed,))
        s_m = line_sum(s_m, z)
        s_c = line_sum(jnp.concatenate([s_d, s_c], axis=1), z)
        parts = over_x([s_m, s_c[:n_d]], [s_a, s_f, s_c[n_d:]])
        n_in, n_out, n_fin, n_up = (g.shape[0] // 8 for g in (g_in0, g_out0, g_fin, g_up))
        g_embed, *grads, g_head, row = collect(parts, n_in, n_out, n_fin, n_up, width)
        n_extra = gains.shape[0] * gains.shape[1]
        total, count = row[0, n_extra], chans * row[0, n_extra + 1]
        g_gain = row[0, :n_extra].reshape(gains.shape)
    else:
        g_gain = jnp.concatenate(gain_rows, axis=1).reshape(gains.shape[0], width)
        chunked = [g.reshape(8, width, -1) for g in (g_embed, g_head)]
        grads = [g_in0, g_in1, g_out0, g_out1, g_up, g_back, g_fin, g_fout]
        grads, (g_embed, g_head), g_gain, total, count = scatter_plain(
            grads, chunked, g_gain, sums[0, 0], chans * sums[1, 0]
        )
    grads = [channel_columns(g_embed, chans), *grads, channel_columns(g_head, chans)]
    loss = total / count
    rescale = 2.0 / count
    new, rounded, next_rows, next_cols, next_v_gain = moments.step(
        grads, rescale, gains, g_gain, v_gain
    )

    def laid_out(new):
        n_embed, n_in, n_out, n_merge, n_fin, n_fout, n_head, n_gains = new
        turn = lambda v: v.transpose(0, 2, 1)
        return [
            n_embed.T, turn(n_in), turn(n_out), turn(n_merge), n_fin.T,
            n_fout, n_head, n_gains,
        ]

    results, copies = laid_out(new), laid_out(rounded)
    return (loss, *results, next_rows, next_cols, next_v_gain, *copies)


def solution(mesh):
    placed = (
        P("dp", None, "lat", None),
        P("dp", None, "lat", None),
        P("dp", "lat", None),
        P("dp"),
        P(),
        P("dp"),
        P(None, "lat"),
        P(None, None, "lat"),
        P(None, "lat", None),
        P(None, None, "lat"),
        P(None, "lat"),
        P("lat", None),
        P("lat", None),
        P(None, "lat"),
        P(),
        P(),
        P(None, "lat"),
    )
    weights = placed[6:14]
    return jax.shard_map(
        on_device,
        mesh=mesh,
        in_specs=placed,
        out_specs=(P(), *weights, P(), P(), P(None, "lat"), *weights),
        check_vma=False,
    )
```

```python
import functools
import math

import jax
import jax.numpy as jnp
from jax import lax
from jax.experimental import pallas as pl
from jax.experimental.pallas import tpu as pltpu
from jax.sharding import PartitionSpec as P

F32 = jnp.float32
BF16 = jnp.bfloat16
HEAD = 32
PATCH = 4
WR = 4
WC = 16
CH = 192
VMEM = 60 * 1024 * 1024
ROOT = math.sqrt(2.0 / math.pi)
NN, NT, TN = (1, 0), (1, 1), (0, 0)


def takes(us):
    return pl.CostEstimate(
        flops=int(us * 0.4e9), bytes_accessed=int(us * 1.3e6), transcendentals=0
    )


def params(steps):
    return pltpu.CompilerParams(
        dimension_semantics=("arbitrary",) * steps, vmem_limit_bytes=VMEM
    )


def split(value):
    high = value.astype(BF16)
    return high, (value - high.astype(F32)).astype(BF16)


def dg(a, b, dims):
    return lax.dot_general(
        a, b, (((dims[0],), (dims[1],)), ((), ())), preferred_element_type=F32
    )


def dot3(a, b, dims):
    return dg(a[0], b[0], dims) + (dg(a[0], b[1], dims) + dg(a[1], b[0], dims))


def normalise(stream):
    centred = stream - jnp.mean(stream, axis=0, keepdims=True)
    scale = lax.rsqrt(jnp.mean(centred * centred, axis=0, keepdims=True) + 1e-05)
    return centred * scale, scale


def normalise_back(grad, hat, scale, gain):
    weighted = grad * gain
    return scale * (
        weighted
        - jnp.mean(weighted, axis=0, keepdims=True)
        - hat * jnp.mean(weighted * hat, axis=0, keepdims=True)
    )


def iota(shape, axis):
    return lax.broadcasted_iota(jnp.int32, shape, axis)


def roll_matrix(shift, tokens):
    lane = iota((tokens, tokens), 0)
    out = iota((tokens, tokens), 1)
    half, inner = out // (tokens // 2), out % (tokens // 2)
    row = jnp.where(half == 0, 2, 0) + (inner // WC) % 2
    columns = tokens // WR
    moved = ((inner // (2 * WC)) * WC + inner % WC + shift) % columns
    source = (moved // WC) * (WR * WC) + row * WC + moved % WC
    return (lane == source).astype(BF16)


def order_matrix(tokens):
    lane = iota((tokens, tokens), 0)
    out = iota((tokens, tokens), 1)
    window, row, col = out // (WR * WC), (out // WC) % WR, out % WC
    source = (row // 2) * (tokens // 2) + window * (2 * WC) + (row % 2) * WC + col
    return (lane == source).astype(BF16)


def permute(value, onehot, dims):
    high, low = split(value)
    rest = (value - high.astype(F32) - low.astype(F32)).astype(BF16)
    return dg(high, onehot, dims) + (dg(low, onehot, dims) + dg(rest, onehot, dims))


def pixel_matrix():
    lane = iota((512, 512), 0)
    out = iota((512, 512), 1)
    b, window, row, col = out // 128, (out // 64) % 2, (out // 16) % 4, out % 16
    return (lane == row * 128 + window * 64 + col * 4 + b).astype(BF16)


def prep_kernel(chans, with_weight, _, *refs):
    parts, refs = refs[:4], refs[4:]
    if with_weight:
        w_ref, out_ref, perm = refs
    else:
        hi_ref, lo_ref, perm = refs
    block = 64

    @pl.when((pl.program_id(0) == 0) & (pl.program_id(1) == 0))
    def _():
        perm[...] = pixel_matrix()

    row = iota((block, 512), 0) + pl.program_id(1) * block
    for pair, x_ref in enumerate(parts):
        lanes = slice(pair * 128, pair * 128 + 128)
        tiles = []
        for a in range(PATCH):
            tile = jnp.concatenate(
                [x_ref[pl.ds(4 * r + a, block, stride=16), :] for r in range(WR)], axis=1
            )
            tile = jnp.where(row < chans, tile, 0.0)
            if with_weight:
                extra = jnp.concatenate(
                    [w_ref[4 * r + a : 4 * r + a + 1, lanes] for r in range(WR)], axis=1
                )
                tile = jnp.where(row == chans, extra, tile)
            tiles.append(tile)
        high, low = split(jnp.concatenate(tiles, axis=0))
        moved = dg(jnp.concatenate([high, low], axis=0), perm[...], NN)
        for a in range(PATCH):
            for b in range(PATCH):
                at, piece = a * block, slice(b * 128, b * 128 + 128)
                above = moved[at : at + block, piece]
                below = moved[at + 256 : at + 256 + block, piece]
                if with_weight:
                    out_ref[b, a, :, lanes] = above + below
                else:
                    hi_ref[b, a, :, lanes] = above.astype(BF16)
                    lo_ref[b, a, :, lanes] = below.astype(BF16)


def prep(token, fields, weight=None):
    samples, chans, height, across = fields.shape
    flat = fields.reshape(samples, chans * height, across)
    padded = 192
    shape = (samples, 4, 4, padded, across)
    spec = pl.BlockSpec((None, 4, 4, 64, across), lambda s, c: (s, 0, 0, c, 0))
    in_specs = [pl.BlockSpec(memory_space=pltpu.SMEM)]
    for pair in range(4):
        in_specs.append(
            pl.BlockSpec((None, 64 * height, 128), lambda s, c, pair=pair: (s, c, pair))
        )
    if weight is not None:
        in_specs.append(pl.BlockSpec((None, height, across), lambda s, c: (s, 0, 0)))
        out_shape, out_specs = jax.ShapeDtypeStruct(shape, F32), spec
    else:
        out_shape = [jax.ShapeDtypeStruct(shape, BF16)] * 2
        out_specs = [spec] * 2
    outs = pl.pallas_call(
        functools.partial(prep_kernel, chans, weight is not None),
        out_shape=out_shape,
        grid=(samples, padded // 64),
        in_specs=in_specs,
        out_specs=out_specs,
        scratch_shapes=[pltpu.VMEM((512, 512), BF16)],
        compiler_params=params(2),
        cost_estimate=takes(14),
        name="prep",
    )(token, *[flat] * 4, *([] if weight is None else [weight]))
    return jax.tree.map(lambda a: a.reshape(samples, 16 * padded, across), outs)


def embed_kernel(w_ref, hi_ref, lo_ref, out_ref):
    total = None
    rows = w_ref.shape[2]
    for k in range(w_ref.shape[0]):
        at = slice(k * rows, k * rows + rows)
        part = dot3(split(w_ref[k]), (hi_ref[at, :], lo_ref[at, :]), NN)
        total = part if total is None else total + part
    out_ref[...] = total


def embed(weight, high, low):
    samples, depth, tokens = high.shape
    width = weight.shape[1]
    big = pl.BlockSpec((None, depth, tokens), lambda s: (s, 0, 0))
    return pl.pallas_call(
        embed_kernel,
        out_shape=jax.ShapeDtypeStruct((width, samples * tokens), F32),
        grid=(samples,),
        in_specs=[pl.BlockSpec(weight.shape, lambda s: (0, 0, 0)), big, big],
        out_specs=pl.BlockSpec((width, tokens), lambda s: (0, s)),
        compiler_params=params(1),
        cost_estimate=takes(10),
        name="embed",
    )(weight, high, low)


def put_bands(out_ref, value):
    rows = out_ref.shape[1]
    for band in range(out_ref.shape[0]):
        out_ref[band] = value[band * rows : band * rows + rows, :]


def embed_back_kernel(g_ref, hi_ref, lo_ref, out_ref):
    samples, _, tokens = hi_ref.shape
    total = None
    for s in range(samples):
        part = dot3(split(g_ref[:, s * tokens : s * tokens + tokens]), (hi_ref[s], lo_ref[s]), NT)
        total = part if total is None else total + part
    put_bands(out_ref, total)


def embed_back(grad, high, low, bands):
    samples, depth, tokens = high.shape
    width = grad.shape[0]
    rows = 2 * CH
    big = pl.BlockSpec((samples, rows, tokens), lambda k: (0, k, 0))
    return pl.pallas_call(
        embed_back_kernel,
        out_shape=jax.ShapeDtypeStruct((bands, depth // rows * width // bands, rows), F32),
        grid=(depth // rows,),
        in_specs=[pl.BlockSpec(grad.shape, lambda k: (0, 0)), big, big],
        out_specs=pl.BlockSpec((bands, width // bands, rows), lambda k: (0, k, 0)),
        compiler_params=params(1),
        cost_estimate=takes(12),
        name="embed_back",
    )(grad, high, low)


def rows_of(at, count):
    return pl.ds(pl.multiple_of(at * count, 16), count)


def chunk_of(rows):
    return next(c for c in (384, 288, 192) if rows % c == 0)


def loop(rows, body):
    count = chunk_of(rows)

    def step(at, carry):
        body(at, count)
        return carry

    lax.fori_loop(0, rows // count, step, 0)


def put(pair, value):
    pair[0][...], pair[1][...] = split(value)


def both(pair):
    return pair[0][...], pair[1][...]


def spread(compact, first):
    high, low = split(compact)
    zero = jnp.zeros_like(high)
    grow = lambda v: jnp.concatenate(
        [jnp.where(first, v, zero), jnp.where(first, zero, v)], axis=0
    )
    return grow(high), grow(low)


def thrice(high, low):
    above = jnp.concatenate([high, high], axis=1)
    return jnp.concatenate([above, jnp.concatenate([low, jnp.zeros_like(low)], axis=1)], axis=0)


def halves(value):
    return value[:HEAD] + value[HEAD:]


def head_rows(width, part, head):
    return slice(part * width + head * HEAD, part * width + head * HEAD + HEAD)


def attend(qkv, out, weights, width):
    heads = width // HEAD
    first = iota((64, 128), 1) < 64

    def body(pair, carry):
        lanes = pl.ds(pl.multiple_of(pair * 128, 128), 128)
        scores = []
        for h in range(heads):
            qh, ql = split(qkv[head_rows(width, 0, h), lanes] * HEAD**-0.5)
            kh, kl = split(qkv[head_rows(width, 1, h), lanes])
            full = dg(
                jnp.concatenate([kh, kh, kl], axis=0), jnp.concatenate([qh, ql, qh], axis=0), TN
            )
            scores.append(jnp.where(first, full[:64], full[64:]))
        scores = jnp.stack(scores)
        scores = jnp.exp(scores - jnp.max(scores, axis=1, keepdims=True))
        scores = scores * (1.0 / jnp.sum(scores, axis=1, keepdims=True))
        weights[pair] = scores
        for h in range(heads):
            values = thrice(*split(qkv[head_rows(width, 2, h), lanes]))
            full = jnp.concatenate(spread(scores[h], first), axis=0)
            out[head_rows(width, 0, h), lanes] = halves(dg(values, full, NN))
        return carry

    lax.fori_loop(0, weights.shape[0], body, 0)


def attend_back(qkv, weights, grad, high_out, low_out, width):
    heads = width // HEAD
    first = iota((64, 128), 1) < 64
    group = min(heads, 12)

    def body(at, carry):
        pair, base = at // (heads // group), (at % (heads // group)) * group
        lanes = pl.ds(pl.multiple_of(pair * 128, 128), 128)
        where = lambda part, h: pl.ds(
            pl.multiple_of(part * width + (base + h) * HEAD, HEAD), HEAD
        )
        def keep(part, h, value):
            rows = where(part, h)
            high_out[rows, lanes], low_out[rows, lanes] = split(value)

        dp = []
        for h in range(group):
            vh, vl = split(qkv[where(2, h), lanes])
            oh, ol = split(grad[where(0, h), lanes])
            full = dg(
                jnp.concatenate([vh, vh, vl], axis=0), jnp.concatenate([oh, ol, oh], axis=0), TN
            )
            dp.append(jnp.where(first, full[:64], full[64:]))
        dp = jnp.stack(dp)
        p = weights[pair, pl.ds(base, group)]
        ds = p * (dp - jnp.sum(dp * p, axis=1, keepdims=True))
        for h in range(group):
            full = jnp.concatenate(spread(p[h], first), axis=1)
            values = thrice(*split(grad[where(0, h), lanes]))
            keep(2, h, halves(dg(values, full, NT)))
        for h in range(group):
            high, low = spread(ds[h], first)
            keys = thrice(*split(qkv[where(1, h), lanes]))
            queries = thrice(*split(qkv[where(0, h), lanes] * HEAD**-0.5))
            full = dg(keys, jnp.concatenate([high, low], axis=0), NN)
            keep(0, h, halves(full) * HEAD**-0.5)
            full = dg(queries, jnp.concatenate([high, low], axis=1), NT)
            keep(1, h, halves(full))
        return carry

    lax.fori_loop(0, weights.shape[0] * (heads // group), body, 0)


def gelu_parts(u):
    t = jnp.tanh(ROOT * (u + 0.044715 * u * u * u))
    return 0.5 * u * (1.0 + t), t


def lane_sums(value):
    column = jnp.sum(value, axis=1, keepdims=True)
    shape = (value.shape[0],) * 2
    return jnp.sum(jnp.where(iota(shape, 0) == iota(shape, 1), column, 0.0), axis=0, keepdims=True)


def saved_shapes(width, hidden, tokens):
    return [
        (3 * width, tokens),
        (width, tokens),
        (width, tokens),
        (hidden, tokens),
        (tokens // 128, width // HEAD, 64, 128),
    ]


def forward_scratch(width, hidden, tokens):
    scratch = [pltpu.VMEM(s, F32) for s in saved_shapes(width, hidden, tokens)]
    scratch += [pltpu.VMEM((width, tokens), BF16)] * 2 + [pltpu.VMEM((hidden, tokens), BF16)] * 2
    return scratch + [pltpu.SemaphoreType.DMA((5,))]


def block_forward(x, win, wout, ga, gm, kept, scratch):
    qkv, out, mid, hidden, weights, nh, nl, hh, hl, sems = scratch
    width = x.shape[0]
    copies = [
        pltpu.make_async_copy(v, k, sems.at[i])
        for i, (v, k) in enumerate(zip((qkv, out, mid, hidden, weights), kept))
    ]
    put((nh, nl), normalise(x)[0] * ga)

    def project(at, count):
        rows = rows_of(at, count)
        qkv[rows, :] = dot3(split(win[rows, :]), both((nh, nl)), NN)

    loop(3 * width, project)
    copies[0].start()
    attend(qkv, out, weights, width)
    copies[1].start()
    copies[4].start()
    mid[...] = x + dot3(split(wout[:width, :]), split(out[...]), TN)
    copies[2].start()
    put((nh, nl), normalise(mid[...])[0] * gm)

    def feed(at, count):
        rows = rows_of(at, count)
        from_rows = pl.ds(pl.multiple_of(3 * width + at * count, 16), count)
        u = dot3(split(win[from_rows, :]), both((nh, nl)), NN)
        hidden[rows, :] = u
        hh[rows, :], hl[rows, :] = split(gelu_parts(u)[0])

    loop(hidden.shape[0], feed)
    copies[3].start()
    return mid[...] + dot3(split(wout[width:, :]), both((hh, hl)), TN), copies


def backward_scratch(width, hidden, tokens):
    scratch = [pltpu.VMEM(s, F32) for s in saved_shapes(width, hidden, tokens)]
    scratch += [pltpu.VMEM((width, tokens), F32)]
    scratch += [pltpu.VMEM((width, tokens), BF16)] * 4 + [pltpu.VMEM((hidden, tokens), BF16)] * 2
    return scratch + [pltpu.SemaphoreType.DMA((5,))]


def fetch(kept, slots, sems):
    copies = [
        pltpu.make_async_copy(k, v, sems.at[i]) for i, (k, v) in enumerate(zip(kept, slots))
    ]
    for copy in copies:
        copy.start()
    return copies


def mlp_back(dy, win, wout, gm, copies, slots, pairs, da, gwin, gwout, ggm):
    mid, hidden, out = slots
    norm, grad, wide = pairs
    width = dy.shape[0]
    put(grad, dy)
    copies[0].wait()
    hat, scale = normalise(mid[...])
    put(norm, hat * gm)
    copies[1].wait()

    def feed(at, count):
        rows = rows_of(at, count)
        out_rows = pl.ds(pl.multiple_of(width + at * count, 16), count)
        u = hidden[rows, :]
        value, t = gelu_parts(u)
        slope = 0.5 * (1.0 + t) + 0.5 * ROOT * u * (1.0 - t * t) * (1.0 + 3 * 0.044715 * u * u)
        gwout[out_rows, :] = dot3(split(value), both(grad), NT)
        du = split(slope * dot3(split(wout[out_rows, :]), both(grad), NN))
        wide[0][rows, :], wide[1][rows, :] = du
        gwin[rows, :] = dot3(du, both(norm), NT)

    loop(hidden.shape[0], feed)
    dn = dot3(split(win[...]), both(wide), TN)
    ggm[...] = lane_sums(dn * hat)
    dmid = dy + normalise_back(dn, hat, scale, gm)
    put(grad, dmid)
    da[...] = dot3(split(wout[:width, :]), both(grad), NN)
    copies[2].wait()
    gwout[:width, :] = dot3(split(out[...]), both(grad), NT)
    return dmid


def attention_back(dmid, x, win, ga, copies, slots, pairs, da, gwin, gga):
    weights, qkv = slots
    norm, wide = pairs
    width = x.shape[0]
    for copy in copies[:2]:
        copy.wait()
    attend_back(qkv, weights, da, *wide, width)
    for copy in copies[2:]:
        copy.wait()
    hat, scale = normalise(x)
    put(norm, hat * ga)

    def project(at, count):
        rows = rows_of(at, count)
        gwin[rows, :] = dot3((wide[0][rows, :], wide[1][rows, :]), both(norm), NT)

    loop(3 * width, project)
    grads = wide[0][: 3 * width, :], wide[1][: 3 * width, :]
    dn = dot3(split(win[...]), grads, TN)
    gga[...] = lane_sums(dn * hat)
    return dmid + normalise_back(dn, hat, scale, ga)


def block_backward(dy, x, win, wout, ga, gm, kept, scratch, gwin, gwout, gga, ggm):
    qkv, out, mid, hidden, weights, da, nh, nl, yh, yl, hh, hl, _ = scratch
    at = 3 * x.shape[0]
    norm, grad, wide = (nh, nl), (yh, yl), (hh, hl)
    dmid = mlp_back(
        dy, win.at[at:], wout, gm, kept[:3], (mid, hidden, out), (norm, grad, wide), da,
        gwin.at[at:], gwout, ggm,
    )
    return attention_back(
        dmid, x, win.at[:at], ga, kept[3:], (weights, qkv), (norm, wide), da, gwin.at[:at], gga
    )


def fetch_block(kept, scratch):
    order = (2, 3, 1, 4, 0)
    return fetch([kept[i] for i in order], [scratch[i] for i in order], scratch[-1])


def call(body, outs, ins, kept_in=(), kept_out=(), scratch=(), smem=(), name=None, aliases=None, cost=0.2):
    vmem = pl.BlockSpec(memory_space=pltpu.VMEM)
    hbm = pl.BlockSpec(memory_space=pl.ANY)
    shape = lambda s: jax.ShapeDtypeStruct(tuple(s), F32)
    return pl.pallas_call(
        body,
        out_shape=[shape(s) for s in (*outs, *kept_out)],
        in_specs=[pl.BlockSpec(memory_space=pltpu.SMEM)] * len(smem)
        + [vmem] * len(ins)
        + [hbm] * len(kept_in),
        out_specs=[vmem] * len(outs) + [hbm] * len(kept_out),
        scratch_shapes=list(scratch),
        input_output_aliases=aliases or {},
        cost_estimate=takes(cost),
        compiler_params=pltpu.CompilerParams(vmem_limit_bytes=VMEM),
        name=name,
    )(*smem, *ins, *kept_in)


def pack(shift_ref, value, stay, send):
    samples = shift_ref.shape[0]
    tokens = value.shape[1] // samples
    for s in range(samples):
        part = value[:, s * tokens : s * tokens + tokens]
        moved = permute(part, roll_matrix(shift_ref[s], tokens), NN)
        stay[s] = moved[:, : tokens // 2]
        send[s] = moved[:, tokens // 2 :]


def unpack(shift_ref, stay, send):
    parts = []
    for s in range(stay.shape[0]):
        joined = jnp.concatenate([stay[s], send[s]], axis=1)
        parts.append(permute(joined, roll_matrix(shift_ref[s], joined.shape[1]), NT))
    return jnp.concatenate(parts, axis=1)


def to_windows(stay, send):
    parts = [jnp.concatenate([stay[s], send[s]], axis=1) for s in range(stay.shape[0])]
    order = order_matrix(parts[0].shape[1])
    return jnp.concatenate([permute(p, order, NN) for p in parts], axis=1)


def from_windows(value, stay, send):
    tokens = value.shape[1] // stay.shape[0]
    order = order_matrix(tokens)
    for s in range(stay.shape[0]):
        moved = permute(value[:, s * tokens : s * tokens + tokens], order, NT)
        stay[s] = moved[:, : tokens // 2]
        send[s] = moved[:, tokens // 2 :]


def half_shape(shift, width, tokens):
    samples = shift.shape[0]
    return (samples, width, tokens // samples // 2)


def encoder_kernel(shift, x, win, wout, ga, gm, y, stay, send, *rest):
    out, copies = block_forward(x[...], win, wout, ga[...], gm[...], rest[:5], rest[5:])
    y[...] = out
    pack(shift, out, stay, send)
    for copy in copies:
        copy.wait()


def encoder(shift, x, win, wout, ga, gm):
    width, tokens = x.shape
    hidden = win.shape[0] - 3 * width
    half = half_shape(shift, width, tokens)
    return call(
        encoder_kernel, [x.shape, half, half], [x, win, wout, ga, gm],
        kept_out=saved_shapes(width, hidden, tokens),
        scratch=forward_scratch(width, hidden, tokens), smem=[shift], name="encoder", cost=14,
    )


def merging_kernel(stay_in, send_in, wup, wback, win, wout, ga, gm, x, wide, last, stay, send, *rest):
    start = to_windows(stay_in, send_in)
    x[...] = start
    raised = dot3(split(wup[...]), split(start), NN)
    wide[...] = raised
    out, copies = block_forward(raised, win, wout, ga[...], gm[...], rest[:5], rest[5:])
    last[...] = out
    from_windows(dot3(split(wback[...]), split(out), TN), stay, send)
    for copy in copies:
        copy.wait()


def merging(stay, arrived, wup, wback, win, wout, ga, gm):
    samples, narrow, half = stay.shape
    width, tokens = wup.shape[0], samples * 2 * half
    hidden = win.shape[0] - 3 * width
    wide = (width, tokens)
    return call(
        merging_kernel, [(narrow, tokens), wide, wide, stay.shape, stay.shape],
        [stay, arrived, wup, wback, win, wout, ga, gm],
        kept_out=saved_shapes(width, hidden, tokens),
        scratch=forward_scratch(width, hidden, tokens), name="merging", cost=32,
    )


def decoder_kernel(shift, y, stay_in, send_in, win, wout, ga, gm, x, last, *rest):
    start = y[...] + unpack(shift, stay_in, send_in)
    x[...] = start
    out, copies = block_forward(start, win, wout, ga[...], gm[...], rest[:5], rest[5:])
    last[...] = out
    for copy in copies:
        copy.wait()


def decoder(shift, y, stay, arrived, win, wout, ga, gm):
    width, tokens = y.shape
    hidden = win.shape[0] - 3 * width
    return call(
        decoder_kernel, [y.shape, y.shape], [y, stay, arrived, win, wout, ga, gm],
        kept_out=saved_shapes(width, hidden, tokens),
        scratch=forward_scratch(width, hidden, tokens), smem=[shift], name="decoder", cost=15,
    )


def gain_shape(win):
    return (1, win.shape[1])


def decoder_back_kernel(shift, dy, x, win, wout, ga, gm, *rest):
    kept, (dx, stay, send, gwin, gwout, gga, ggm), scratch = rest[:5], rest[5:12], rest[12:]
    copies = fetch_block(kept, scratch)
    grad = block_backward(
        dy[...], x[...], win, wout, ga[...], gm[...], copies, scratch, gwin, gwout, gga, ggm
    )
    dx[...] = grad
    pack(shift, grad, stay, send)


def decoder_back(shift, dy, x, saved, win, wout, ga, gm):
    width, tokens = x.shape
    half = half_shape(shift, width, tokens)
    return call(
        decoder_back_kernel,
        [x.shape, half, half, win.shape, wout.shape, gain_shape(win), gain_shape(win)],
        [dy, x, win, wout, ga, gm], kept_in=saved,
        scratch=backward_scratch(width, win.shape[0] - 3 * width, tokens),
        smem=[shift], name="decoder_back", cost=24,
    )


def merging_mlp_back_kernel(stay_in, send_in, last, wback, win, wout, gm, *rest):
    kept, (gback, gwout, ggm, dmid, da, gwin_out), scratch = rest[:3], rest[3:9], rest[9:]
    *slots, nh, nl, yh, yl, hh, hl, gwin, sems, sem = scratch
    copies = fetch(kept, slots, sems)
    dz = split(to_windows(stay_in, send_in))
    gback[...] = dot3(split(last[...]), dz, NT)
    dlast = dot3(split(wback[...]), dz, NN)
    at = win.shape[0] - gwin.shape[0]
    dmid[...] = mlp_back(
        dlast, win.at[at:], wout, gm[...], copies, slots, ((nh, nl), (yh, yl), (hh, hl)), da,
        gwin, gwout, ggm,
    )
    copy = pltpu.make_async_copy(gwin, gwin_out.at[at:], sem)
    copy.start()
    copy.wait()


def merging_mlp_back(stay, arrived, last, saved, wback, win, wout, gm):
    width, tokens = last.shape
    hidden = win.shape[0] - 3 * width
    wide = (width, tokens)
    scratch = [pltpu.VMEM(s, F32) for s in (wide, (hidden, tokens), wide)]
    scratch += [pltpu.VMEM(wide, BF16)] * 4 + [pltpu.VMEM((hidden, tokens), BF16)] * 2
    scratch += [pltpu.VMEM((hidden, width), F32), pltpu.SemaphoreType.DMA((3,)), pltpu.SemaphoreType.DMA]
    return call(
        merging_mlp_back_kernel, [wback.shape, wout.shape, gain_shape(win), wide, wide],
        [stay, arrived, last, wback, win, wout, gm],
        kept_in=[saved[2], saved[3], saved[1]], kept_out=[win.shape], scratch=scratch,
        name="merging_mlp_back", cost=36,
    )


def merging_attention_back_kernel(dmid, da, x, wide_x, wup, ga, *rest):
    (p_in, qkv_in, win_in, _), (stay, send, gup, gga, gwin_out) = rest[:4], rest[4:9]
    weights, qkv, win, nh, nl, hh, hl, gwin, sems, sem = rest[9:]
    copies = fetch([p_in, qkv_in, win_in.at[: win.shape[0]]], [weights, qkv, win], sems)
    grad = attention_back(
        dmid[...], wide_x[...], win, ga[...], copies, (weights, qkv), ((nh, nl), (hh, hl)), da,
        gwin, gga,
    )
    copy = pltpu.make_async_copy(gwin, gwin_out.at[: gwin.shape[0]], sem)
    copy.start()
    grad = split(grad)
    gup[...] = dot3(grad, split(x[...]), NT)
    from_windows(dot3(split(wup[...]), grad, TN), stay, send)
    copy.wait()


def merging_attention_back(dmid, da, x, wide_x, saved, wup, win, ga, gwin, halved):
    width, tokens = wide_x.shape
    rows = 3 * width
    scratch = [pltpu.VMEM(saved[4].shape, F32), pltpu.VMEM(saved[0].shape, F32)]
    scratch += [pltpu.VMEM((rows, width), F32)] + [pltpu.VMEM((width, tokens), BF16)] * 2
    scratch += [pltpu.VMEM((rows, tokens), BF16)] * 2 + [pltpu.VMEM((rows, width), F32)]
    return call(
        merging_attention_back_kernel, [halved, halved, wup.shape, gain_shape(win)],
        [dmid, da, x, wide_x, wup, ga], kept_in=[saved[4], saved[0], win, gwin],
        kept_out=[win.shape],
        scratch=scratch + [pltpu.SemaphoreType.DMA((3,)), pltpu.SemaphoreType.DMA],
        name="merging_attention_back", cost=27, aliases={9: 4},
    )


def encoder_back_kernel(shift, dy, stay_in, send_in, x, win, wout, ga, gm, *rest):
    kept, (dx, gwin, gwout, gga, ggm), scratch = rest[:5], rest[5:10], rest[10:]
    copies = fetch_block(kept, scratch)
    start = dy[...] + unpack(shift, stay_in, send_in)
    dx[...] = block_backward(
        start, x[...], win, wout, ga[...], gm[...], copies, scratch, gwin, gwout, gga, ggm
    )


def encoder_back(shift, dy, stay, arrived, x, saved, win, wout, ga, gm):
    width, tokens = x.shape
    return call(
        encoder_back_kernel,
        [x.shape, win.shape, wout.shape, gain_shape(win), gain_shape(win)],
        [dy, stay, arrived, x, win, wout, ga, gm], kept_in=saved,
        scratch=backward_scratch(width, win.shape[0] - 3 * width, tokens),
        smem=[shift], name="encoder_back", cost=23,
    )


def head_kernel(chans, x_ref, gain, w_ref, t_ref, gx, gw_ref, gg_ref, sums, nh, nl, dh, dl, acc, loss):
    k = pl.program_id(0)
    samples, rows, tokens = t_ref.shape

    @pl.when(k == 0)
    def _():
        put((nh, nl), normalise(x_ref[...])[0] * gain[...])
        loss[...] = jnp.zeros_like(loss)
        acc[...] = jnp.zeros_like(acc)

    weight = split(w_ref[...])
    pred = dot3(weight, both((nh, nl)), TN)
    for s in range(samples):
        lanes = slice(s * tokens, s * tokens + tokens)
        for at in range(0, rows, CH):
            target = t_ref[s, at : at + CH, :]
            scaled = target[chans : chans + 1, :]
            differ = pred[at : at + CH, lanes] - target
            differ = jnp.where(iota(target.shape, 0) < chans, differ, 0.0)
            dp = scaled * differ
            loss[0:1, :] += jnp.sum(dp * differ, axis=0, keepdims=True)
            loss[1:2, :] += scaled
            dh[at : at + CH, lanes], dl[at : at + CH, lanes] = split(dp)
    put_bands(gw_ref, dot3(both((nh, nl)), both((dh, dl)), NT))
    acc[...] += dot3(weight, both((dh, dl)), NN)

    @pl.when(k == pl.num_programs(0) - 1)
    def _():
        hat, scale = normalise(x_ref[...])
        dn = acc[...]
        gg_ref[...] = lane_sums(dn * hat)
        gx[...] = normalise_back(dn, hat, scale, gain[...])
        sums[...] = jnp.sum(loss[...], axis=1, keepdims=True) + jnp.zeros_like(sums)


def head(x, gain, weight, target, chans, bands):
    samples, _, tokens = target.shape
    width = x.shape[0]
    chunks, _, rows = weight.shape
    fixed = lambda shape: pl.BlockSpec(shape, lambda k: (0,) * len(shape))
    piece = pl.BlockSpec((None, width, rows), lambda k: (k, 0, 0))
    return pl.pallas_call(
        functools.partial(head_kernel, chans),
        out_shape=[
            jax.ShapeDtypeStruct(x.shape, F32),
            jax.ShapeDtypeStruct((bands, chunks * width // bands, rows), F32),
            jax.ShapeDtypeStruct((1, width), F32),
            jax.ShapeDtypeStruct((8, 128), F32),
        ],
        grid=(chunks,),
        in_specs=[
            fixed(x.shape),
            fixed((width, 1)),
            piece,
            pl.BlockSpec((samples, rows, tokens), lambda k: (0, k, 0)),
        ],
        out_specs=[
            fixed(x.shape),
            pl.BlockSpec((bands, width // bands, rows), lambda k: (0, k, 0)),
            fixed((1, width)),
            fixed((8, 128)),
        ],
        scratch_shapes=[pltpu.VMEM(x.shape, BF16)] * 2
        + [pltpu.VMEM((rows, x.shape[1]), BF16)] * 2
        + [pltpu.VMEM(x.shape, F32), pltpu.VMEM((8, tokens), F32)],
        compiler_params=params(1),
        cost_estimate=takes(25),
        name="head",
    )(x, gain, weight, target)


def swap(value, axis, bit):
    return lax.ppermute(value, axis, [(i, i ^ bit) for i in range(lax.axis_size(axis))])


def pick(value, at, axis):
    return lax.dynamic_index_in_dim(value, at, axis, keepdims=False)


def place_of():
    lat, dp = lax.axis_index("lat"), lax.axis_index("dp")
    return lat // 2, lat % 2, dp // 2, dp % 2


def along(first, last):
    return [(2 * k + y, 2 * (k + 1) + y) for k in range(first, last) for y in range(2)]


def backwards(pairs):
    return [(7 - a, 7 - b) for a, b in pairs]


def line_sum(parts, z, meanwhile=()):
    right = left = None
    for step in (1, 2, 3):
        ahead = pick(parts, jnp.clip(z + 4 - step, 0, 3), 0)
        behind = pick(parts, jnp.clip(z + step - 4, 0, 3), 0)
        if right is not None:
            ahead, behind = ahead + right, behind + left
        right = lax.ppermute(ahead, "lat", along(0, step))
        left = lax.ppermute(behind, "lat", backwards(along(0, step)))
        if step <= len(meanwhile):
            right, left = tie((right, left), meanwhile[step - 1])
    return pick(parts, z, 0) + right + left


def ordered(mine, other, which, axis=0):
    shape = mine.shape
    at = jnp.arange(2).reshape((1,) * axis + (2,) + (1,) * (mine.ndim - axis))
    joined = jnp.where(at == which, jnp.expand_dims(mine, axis), jnp.expand_dims(other, axis))
    return joined.reshape(shape[:axis] + (2 * shape[axis],) + shape[axis + 1 :])


AXES = {"c": ("dp", 1, 3), "x": ("dp", 2, 2), "y": ("lat", 1, 1)}


class Halving:
    def __init__(self, buf, over):
        self.axis, self.bit, at = AXES[over]
        own = place_of()[at]
        bands, rows, lanes = buf.shape
        parts = buf.reshape((4, 2, rows, lanes) if over == "y" else (8, 2, rows // 2, lanes))
        self.keep, self.give = pick(parts, own, 1), pick(parts, 1 - own, 1)

    def ahead_of(self, value):
        value, self.give = lax.optimization_barrier((value, self.give))
        return value

    def done(self, beside=None):
        return self.keep + tie(swap(self.give, self.axis, self.bit), beside)


def halve(buf, over, beside=None):
    return Halving(buf, over).done(beside)


def over_x(quarters, sums):
    x = place_of()[2]
    return [ordered(v, swap(v, "dp", 2), x) for v in quarters] + [v + swap(v, "dp", 2) for v in sums]


def collect_kernel(sizes, core, *refs):
    halves_in, outs = refs[:10], refs[10:]
    first = core[0] == 0

    def joined(at):
        mine, got = halves_in[at][...], halves_in[at + 5][...]
        return jnp.concatenate([jnp.where(first, mine, got), jnp.where(first, got, mine)], axis=0)

    embed_o, in0_o, in1_o, out0_o, out1_o, up_o, back_o, fin_o, fout_o, head_o, extra_o = outs
    n_fin, n_in, n_out = sizes
    width = in0_o.shape[1]
    rows = embed_o.shape[1]
    part = joined(0)
    fin_o[...] = part[:n_fin, :]
    up_o[...], back_o[...] = part[n_fin:, :width], part[n_fin:, width:]
    part, late, early = joined(1), joined(2), joined(4)
    fout_o[...] = joined(3)
    for k in range(embed_o.shape[0]):
        embed_o[k] = part[k * rows : k * rows + rows, :]
        head_o[k] = late[k * rows : k * rows + rows, :]
    at = embed_o.shape[0] * rows
    n_pair = (n_in + n_out) // 2
    for block, into_in, into_out in ((late[at:, :], in1_o, out1_o), (early, in0_o, out0_o)):
        tall = jnp.concatenate([block[:n_pair, :width], block[:n_pair, width:]], axis=0)
        into_in[...] = tall[:n_in, :]
        into_out[...] = tall[n_in:, :]
    extra_o[...] = early[n_pair : n_pair + 8, :]


def collect(parts, rows_in, rows_out, rows_fin, rows_up, width):
    got = [swap(p, "dp", 1) for p in parts]
    shapes = [
        (8, width // 8, 2 * width), (rows_in, width), (rows_in, width), (rows_out, width),
        (rows_out, width), (rows_up, width), (rows_up, width), (rows_fin, 2 * width),
        (2 * parts[3].shape[0], 2 * width), (8, width // 8, 2 * width), (8, 2 * width),
    ]
    core = place_of()[3].reshape(1)
    return call(
        functools.partial(collect_kernel, (rows_fin, rows_in, rows_out)), shapes,
        [*parts, *got], smem=[core], name="collect",
    )


def tie(first, second):
    if second is None:
        return first
    return lax.optimization_barrier((first, second))[0]


def line_gather(piece, z, beside):
    right = left = piece
    arrived = []
    for step in (1, 2, 3):
        right = lax.ppermute(right, "lat", along(step - 1, 3))
        left = lax.ppermute(left, "lat", backwards(along(step - 1, 3)))
        if step <= len(beside):
            right, left = tie((right, left), beside[step - 1](arrived[-1:]))
        arrived.append((step, right, left))
    def at(k):
        chosen = piece
        for step, right, left in arrived:
            if k + step < 4:
                chosen = jnp.where(z == k + step, right, chosen)
            if k - step >= 0:
                chosen = jnp.where(z == k - step, left, chosen)
        return chosen

    return jnp.stack([at(k) for k in range(4)])


def gather_bands(q, h, beside):
    z, y, x, c = place_of()
    lanes = q.shape[-1]
    quarter, rest = q.shape[0] // 4, h.shape[0] // 2
    q = pick(q.reshape(4, quarter, lanes), c * 2 + x, 0)
    h = pick(h.reshape(2, rest, lanes), c, 0)
    return line_gather(jnp.concatenate([q, h]), z, beside), quarter


def gather_rest(full, quarter, first, second):
    z, y, x, c = place_of()
    q, h = full[:, :quarter], full[:, quarter:]
    lay = lambda mine, got: ordered(mine[:, None], got[:, None], y, axis=1).reshape(
        8, *mine.shape[1:]
    )
    got = tie(swap(q, "lat", 1), first)
    h = tie(h, got)
    q = lay(q, got)
    h_got, q_got = tie(swap(h, "lat", 1), second), tie(swap(q, "dp", 2), second)
    h, q = lay(h, h_got), ordered(q, q_got, x, axis=1)
    return q, swap(q, "dp", 1), h, swap(h, "dp", 1)


def join_kernel(core, q, q_got, h, h_got, q_out, h_out):
    first = core[0] == 0
    bands = q.shape[0]
    for mine, got, out in ((q, q_got, q_out), (h, h_got, h_out)):
        rows, half = out.shape[0] // bands, mine.shape[1]
        for band in range(bands):
            at = band * rows
            low, high = mine[band], got[band]
            out[at : at + half, :] = jnp.where(first, low, high)
            out[at + half : at + rows, :] = jnp.where(first, high, low)[: rows - half, :]


def join_cores(q, q_got, h, h_got, rows_q, rows_h):
    shapes = [(8 * rows_q, q.shape[2]), (8 * rows_h, q.shape[2])]
    core = place_of()[3].reshape(1)
    return call(join_kernel, shapes, [q, q_got, h, h_got], smem=[core], name="join")


def gather_all(shard):
    rows, lanes = shard.shape
    mine = pick(shard.reshape(4, rows // 4, lanes), lax.axis_index("dp"), 0)
    return lax.all_gather(mine, ("lat", "dp"), axis=0, tiled=True).reshape(-1, rows, lanes)


def widen_pair(top, bottom):
    both = jnp.concatenate([top, bottom], axis=-2)
    half = both.shape[-2] // 2
    return jnp.concatenate([both[..., :half, :], both[..., half:, :]], axis=-1)


def narrow_pair(both, rows):
    width = both.shape[-1] // 2
    flat = jnp.concatenate([both[..., :width], both[..., width:]], axis=-2)
    return flat[..., :rows, :], flat[..., rows:, :]


def flat(value):
    return value.reshape(-1, value.shape[-1])


def banded(value, bands):
    return value.reshape(bands, -1, value.shape[-1])


def gather_weights(shards, gains, beside):
    in0, in1, out0, out1, up, back, fin, fout, embed_w, head_w = shards
    if (lax.axis_size("dp"), lax.axis_size("lat")) != (4, 8):
        whole_of = lambda s: lax.all_gather(s, "lat", axis=0, tiled=True)
        embed_w, head_w = (
            whole_of(s.transpose(1, 0, 2)).transpose(1, 0, 2) for s in (embed_w, head_w)
        )
        rest = [whole_of(s) for s in shards[:8]]
        columns = [g.reshape(-1, 1) for g in whole_of(gains.T).T]
        columns[5:] = [jnp.concatenate(columns[5:7]), jnp.concatenate(columns[7:9])]
        return [*rest, embed_w, head_w], columns
    n_in, n_fin, width = in0.shape[0], fin.shape[0], in0.shape[1]
    n_embed = 8 * (width // 8)
    pair = widen_pair(in0, out0)
    n_pair = pair.shape[0]
    row = jnp.pad(gains.reshape(1, -1), ((0, 31), (0, 2 * width - gains.size)))
    early = jnp.concatenate([flat(embed_w), pair, jnp.concatenate([up, back], axis=-1), row])
    early = gather_all(early)
    spare = -n_fin % 32
    middle = gather_bands(jnp.pad(fin, ((0, spare), (0, 0))), fout, beside)
    late = [widen_pair(in1, out1), flat(head_w), jnp.zeros((16, 2 * width), F32)]
    late = gather_all(jnp.concatenate(late))
    n_out = out0.shape[0]
    w_embed, w_in0, w_out0, w_up, w_back, *all_gains = unpack_early(
        early, n_embed, n_in, n_out, up.shape[0], gains.shape[0], width
    )
    w_head, w_in1, w_out1 = unpack_late(late, n_embed, n_in, n_out, width)
    return [
        w_in0, w_in1, w_out0, w_out1, w_up, w_back, middle, None, w_embed, w_head
    ], all_gains


def unpack_chunks(ref, at, out):
    bands, chunks = ref.shape[0], out.shape[0]
    rows = out.shape[1] // bands
    for band in range(bands):
        for k in range(chunks):
            start = at + k * rows
            out[k, band * rows : band * rows + rows, :] = ref[band, start : start + rows, :]


def unpack_pair(ref, at, into_in, into_out):
    bands = ref.shape[0]
    width = into_in.shape[1]
    n_in, n_out = into_in.shape[0] // bands, into_out.shape[0] // bands
    end = at + (n_in + n_out) // 2
    for band in range(bands):
        block = ref[band, at:end, :]
        tall = jnp.concatenate([block[:, :width], block[:, width:]], axis=0)
        into_in[band * n_in : band * n_in + n_in, :] = tall[:n_in, :]
        into_out[band * n_out : band * n_out + n_out, :] = tall[n_in:, :]


def unpack_early_kernel(n_embed, early, embed_o, in_o, out_o, up_o, back_o, *gain_o):
    bands, width = early.shape[0], in_o.shape[1]
    unpack_chunks(early, 0, embed_o)
    unpack_pair(early, n_embed, in_o, out_o)
    n_up = up_o.shape[0] // bands
    at = n_embed + (in_o.shape[0] + out_o.shape[0]) // bands // 2
    part = width // bands
    for band in range(bands):
        rows = slice(band * n_up, band * n_up + n_up)
        up_o[rows, :] = early[band, at : at + n_up, :width]
        back_o[rows, :] = early[band, at : at + n_up, width:]
        line = early[band, at + n_up : at + n_up + 1, :]
        shape = (part, line.shape[1])
        start = 0
        for out in gain_o:
            for block in range(out.shape[0] // width):
                hit = iota(shape, 1) == start + iota(shape, 0)
                column = jnp.sum(jnp.where(hit, line, 0.0), axis=1, keepdims=True)
                row = block * width + band * part
                out[row : row + part, :] = column
                start += part


def unpack_early(early, n_embed, n_in, n_out, n_up, n_gain, width):
    shapes = [
        (8, width, early.shape[2]), (8 * n_in, width), (8 * n_out, width), (8 * n_up, width),
        (8 * n_up, width), *[(width, 1)] * (n_gain - 4), (2 * width, 1), (2 * width, 1),
    ]
    body = functools.partial(unpack_early_kernel, n_embed)
    return call(body, shapes, [early], name="unpack_early")


def unpack_late_kernel(late, head_o, in_o, out_o):
    unpack_pair(late, 0, in_o, out_o)
    unpack_chunks(late, (in_o.shape[0] + out_o.shape[0]) // late.shape[0] // 2, head_o)


def unpack_late(late, n_embed, n_in, n_out, width):
    shapes = [(8, width, late.shape[2]), (8 * n_in, width), (8 * n_out, width)]
    return call(unpack_late_kernel, shapes, [late], name="unpack_late")


def pack_early_kernel(gwin, gwout, gg0, gg1, gg2, gg3, gg4, gga, ggm, sums, out):
    bands, width = out.shape[0], gwin.shape[1]
    n_in, n_out = gwin.shape[0] // bands, gwout.shape[0] // bands
    n_pair, part = (n_in + n_out) // 2, width // bands
    for band in range(bands):
        tall = jnp.concatenate(
            [gwin[band * n_in : band * n_in + n_in, :], gwout[band * n_out : band * n_out + n_out, :]],
            axis=0,
        )
        out[band, :n_pair, :width] = tall[:n_pair, :]
        out[band, :n_pair, width:] = tall[n_pair:, :]
        line = []
        for ref in (gg0, gg1, gg2, gg3, gg4, gga, ggm):
            for start in range(band * part, ref.shape[1], width):
                line.append(ref[:, start : start + part])
        line += [sums[0:1, 0:1], sums[1:2, 0:1]]
        used = 9 * part + 2
        line = jnp.concatenate(line + [jnp.zeros((1, out.shape[2] - used), F32)], axis=1)
        out[band, n_pair:, :] = jnp.where(iota((out.shape[1] - n_pair, 1), 0) == 0, line, 0.0)


def pack_early(gwin, gwout, gains, sums):
    rows = (gwin.shape[0] + gwout.shape[0]) // 16 + 16
    shape = (8, rows, 2 * gwin.shape[1])
    return call(pack_early_kernel, [shape], [gwin, gwout, *gains, sums], name="pack_early")[0]


LINE = 384
OTHERS = 24
OWN_AT = 32


def pieces(ref):
    return [slice(at, min(at + LINE, ref.shape[1])) for at in range(0, ref.shape[1], LINE)]


def chunks_of(ref):
    return [ref[:, piece] for piece in pieces(ref)]


def squares(value, rescale):
    value = value * rescale
    return value * value + 1e-30


def as_lane(column):
    shape = (column.shape[0], LINE)
    return jnp.sum(jnp.where(iota(shape, 0) == iota(shape, 1), column, 0.0), axis=0, keepdims=True)


def as_column(line, rows):
    shape = (rows, LINE)
    return jnp.sum(jnp.where(iota(shape, 0) == iota(shape, 1), line, 0.0), axis=1, keepdims=True)


def at_lane(value, lane):
    return jnp.where(iota((1, LINE), 1) == lane, value, 0.0)


def total(value):
    return jnp.sum(jnp.sum(value, axis=1, keepdims=True), axis=0, keepdims=True)


def stats_kernel(bands, count, *refs):
    grads, mats = refs[:count], refs[count : 2 * count]
    rescale_ref, gains, out = refs[2 * count :]
    rescale = rescale_ref[...]
    out[...] = jnp.zeros_like(out)
    row = 0
    energy = jnp.zeros((1, LINE), F32)
    for i, (g, w) in enumerate(zip(grads, mats)):
        own = 0.0
        for part, weight in zip(chunks_of(g), chunks_of(w)):
            square = squares(part, rescale)
            own = own + jnp.sum(square, axis=1, keepdims=True)
            other = jnp.sum(square, axis=0, keepdims=True) / (square.shape[0] * bands)
            out[row : row + 1, : other.shape[1]] = other
            row += 1
            energy = energy + at_lane(total(weight * weight), i)
        out[OWN_AT + i : OWN_AT + i + 1, :] = as_lane(own / g.shape[1])
    out[row : row + 1, :] = energy
    out[row + 1 : row + 2, :] = as_lane(jnp.sum(gains[...] * gains[...], axis=1, keepdims=True))


def new_stats(i, row, g, rescale, turned, sums, other_stats, own_stats, own_mean):
    parts = chunks_of(g)
    own, others, mean_sum, stat_sum = 0.0, [], 0.0, 0.0
    for k, part in enumerate(parts):
        own = own + jnp.sum(squares(part, rescale), axis=1, keepdims=True)
        wide = part.shape[1]
        mean = sums[row + k : row + k + 1, :wide]
        stat = other_stats[row + k : row + k + 1, :wide]
        others.append(0.5 * stat + 0.5 * mean)
        mean_sum = mean_sum + total(mean)
        stat_sum = stat_sum + total(stat)
    columns = g.shape[1]
    own = 0.5 * as_column(own_stats[i : i + 1, :], own.shape[0]) + 0.5 * (own / columns)
    stat_mean = stat_sum / columns if turned else own_mean[0:1, i : i + 1]
    return others, own, 0.5 * stat_mean + 0.5 * (mean_sum / columns)


def update_kernel(turned, count, *refs):
    grads, own_stats = refs[:count], refs[count]
    rescale_ref, sums, other_stats, own_mean, g_gain, v_gain, out, next_v, *updates = refs[count + 1 :]
    rescale = rescale_ref[...]
    row = 0
    energy = jnp.zeros((1, LINE), F32)
    for i, g in enumerate(grads):
        others, own, mean = new_stats(
            i, row, g, rescale, turned[i], sums, other_stats, own_stats, own_mean
        )
        for piece, other in zip(pieces(g), others):
            update = g[:, piece] * rescale * lax.rsqrt(own * other / mean)
            updates[i][:, piece] = update
            energy = energy + at_lane(total(update * update), i)
        row += len(others)
    grad = g_gain[...] * rescale
    value = 0.5 * v_gain[...] + 0.5 * (grad * grad + 1e-30)
    next_v[...] = value
    update = grad * lax.rsqrt(value)
    updates[count][...] = update
    out[...] = jnp.zeros_like(out)
    out[0:1, :] = energy
    out[1:2, :] = as_lane(jnp.sum(update * update, axis=1, keepdims=True))


def step_kernel(bands, count, *refs):
    updates, mats = refs[: count + 1], refs[count + 1 : 2 * count + 2]
    squares_u, squares_w = refs[2 * count + 2 : 2 * count + 4]
    outs = refs[2 * count + 4 :]
    news, copies = outs[: len(outs) // 2], outs[len(outs) // 2 :]
    where = [(0, None), (1, 0), (1, 1), (2, 0), (2, 1), (3, 0), (3, 1)]
    where += [(4, None), (5, None), (6, None), (7, None)]
    for i, (u, w, (out, pair)) in enumerate(zip(updates, mats, where)):
        new, copy = news[out], copies[out]
        if i < count:
            entries = u.shape[0] * u.shape[1] * bands
            energy_u, energy_w = squares_u[0:1, i : i + 1], squares_w[0:1, i : i + 1]
        else:
            entries = u.shape[1] * bands
            energy_u, energy_w = (
                as_column(s[1:2, :], u.shape[0]) for s in (squares_u, squares_w)
            )
        clip = jnp.maximum(1.0, jnp.sqrt(energy_u / entries) / 0.25)
        size = jnp.maximum(0.001, jnp.sqrt(energy_w / entries))
        value = w[...] - size * (u[...] / clip)
        if out == 2:
            value = value.T
        at = Ellipsis if pair is None else pair
        new[at] = value
        copy[at] = value.astype(BF16)


def plain_call(body, shapes, args, name, rounded=()):
    vmem = pl.BlockSpec(memory_space=pltpu.VMEM)
    outs = [jax.ShapeDtypeStruct(tuple(s), F32) for s in shapes]
    outs += [jax.ShapeDtypeStruct(tuple(s), BF16) for s in rounded]
    shapes = outs
    return pl.pallas_call(
        body,
        out_shape=outs,
        in_specs=[vmem] * len(args),
        out_specs=[vmem] * len(shapes),
        compiler_params=pltpu.CompilerParams(vmem_limit_bytes=VMEM),
        cost_estimate=takes(4),
        name=name,
    )(*args)


def band_sum_and_gather(sums, mine):
    bit = 1
    while bit < lax.axis_size("lat"):
        got = swap(jnp.concatenate([sums, mine]), "lat", bit)
        n = sums.shape[0]
        sums = sums + got[:n]
        mine = ordered(mine, got[n:], (lax.axis_index("lat") // bit) % 2)
        bit *= 2
    return sums, mine


def lines(line):
    return jnp.pad(line, (0, -line.shape[0] % LINE)).reshape(-1, LINE)


class Moments:
    def __init__(self, mats, turned, row_stats, col_stats):
        bands, band = lax.axis_size("lat"), lax.axis_index("lat")
        self.mats, self.turned, self.bands = mats, turned, bands
        self.rows = [m.shape[-2] for m in mats]
        other_lines, self.own, means = [], [], []
        row_at = col_at = 0
        for m, turn in zip(mats, turned):
            split_size = m.shape[-2] * bands
            columns = m.shape[1]
            n_row, n_col = (columns, split_size) if turn else (split_size, columns)
            row, col = row_stats[row_at : row_at + n_row], col_stats[col_at : col_at + n_col]
            row_at, col_at = row_at + n_row, col_at + n_col
            other, mine = (row, col) if turn else (col, row)
            other_lines.append(lines(other))
            mine = lax.dynamic_slice_in_dim(mine, band * m.shape[-2], m.shape[-2])
            self.own.append(lines(mine))
            means.append(jnp.mean(row).reshape(1, 1))
        self.other = jnp.concatenate(other_lines)
        self.own = jnp.pad(jnp.concatenate(self.own), ((0, 16 - len(mats)), (0, 0)))
        self.mean = jnp.pad(jnp.concatenate(means, axis=1), ((0, 0), (0, LINE - len(mats))))
        self.row_stats, self.col_stats = row_stats, col_stats

    def step(self, grads, rescale, gains, g_gain, v_gain):
        count = len(grads)
        rescale = rescale.reshape(1, 1)
        shape = (OWN_AT + 16, LINE)
        (stats,) = plain_call(
            functools.partial(stats_kernel, self.bands, count), [shape],
            [*grads, *self.mats, rescale, gains], "stats",
        )
        sums, own = band_sum_and_gather(stats[:OWN_AT], stats[OWN_AT:])
        out, next_v, *updates = plain_call(
            functools.partial(update_kernel, tuple(self.turned), count),
            [(8, LINE), gains.shape, *[g.shape for g in grads], gains.shape],
            [*grads, self.own, rescale, sums, self.other, self.mean, g_gain, v_gain], "update",
        )
        bit = 1
        while bit < self.bands:
            out = out + swap(out, "lat", bit)
            bit *= 2
        shapes = [g.shape for g in grads]
        shapes = [
            shapes[0], (2, *shapes[1]), (2, *shapes[3][::-1]), (2, *shapes[5]), *shapes[7:], gains.shape
        ]
        news = plain_call(
            functools.partial(step_kernel, self.bands, count), shapes,
            [*updates, *self.mats, gains, out, sums[OTHERS : OTHERS + 8]], "step", shapes,
        )
        own = own.reshape(self.bands, 16, LINE)
        row_means, col_means = [], []
        row = 0
        for i, (m, turn) in enumerate(zip(self.mats, self.turned)):
            mine = own[:, i, : self.rows[i]].reshape(-1)
            taken = -(-m.shape[1] // LINE)
            other = sums[row : row + taken].reshape(-1)[: m.shape[1]]
            row += taken
            row_means.append(other if turn else mine)
            col_means.append(mine if turn else other)
        next_rows = 0.5 * self.row_stats + 0.5 * jnp.concatenate(row_means)
        next_cols = 0.5 * self.col_stats + 0.5 * jnp.concatenate(col_means)
        return news[: len(shapes)], news[len(shapes) :], next_rows, next_cols, next_v


def pixel_columns(flat_rows):
    rows, depth = flat_rows.shape
    moved = flat_rows.reshape(rows, depth // 16, 4, 4).transpose(3, 2, 0, 1)
    moved = jnp.pad(moved, ((0, 0), (0, 0), (0, 0), (0, CH - depth // 16)))
    return moved.reshape(8, 2, rows, CH).transpose(0, 2, 1, 3).reshape(8, rows, 2 * CH)


def channel_columns(chunks, chans):
    rows = chunks.shape[1]
    moved = chunks.reshape(4, 2, rows, 2, CH)[..., :chans]
    return moved.transpose(2, 4, 1, 3, 0).reshape(rows, chans * 16)


def shifted(value, axis, by):
    peers = lax.axis_size(axis)
    return lax.ppermute(value, axis, [(i, (i + by) % peers) for i in range(peers)])


def scatter_plain(grads, chunked, g_gain, total, count):
    scatter = lambda g, axis: lax.psum_scatter(g, "lat", scatter_dimension=axis, tiled=True)
    total, count = lax.psum((total, count), ("dp", "lat"))
    grads = [scatter(g, 0) for g in grads]
    chunked = [scatter(g, 1) for g in chunked]
    grads, chunked, g_gain = lax.psum((grads, chunked, scatter(g_gain, 1)), "dp")
    return grads, chunked, g_gain, total, count


def on_device(
    fields, target, valid_mask, sample_index, weight_table, lon_shift, w_embed, w_in, w_out,
    w_merge, w_fin, w_fout, w_head, gains, row_stats, col_stats, v_gain,
):
    band_count = lax.axis_size("lat")
    band_index = lax.axis_index("lat")
    samples, chans, rows_dev, across = fields.shape
    width = w_in.shape[1]
    total_rows = rows_dev * band_count
    pixel_rows = (band_index * rows_dev + jnp.arange(rows_dev)).astype(F32)
    coslat = jnp.cos((90.0 - (pixel_rows + 0.5) * 180.0 / total_rows) * (jnp.pi / 180.0))
    picked = (sample_index[:, None] == jnp.arange(weight_table.shape[0])[None, :]).astype(F32)
    sample_weight = jnp.sum(picked * weight_table[None, :], axis=1)
    weight = sample_weight[:, None, None] * coslat[None, :, None] * valid_mask.astype(F32)

    mats = [
        w_embed.T, w_in[0].T, w_in[1].T, w_out[0], w_out[1], w_merge[0].T, w_merge[1].T, w_fin.T,
        w_fout, w_head,
    ]
    turned = [True, True, True, False, False, True, True, True, False, False]
    moments = Moments(mats, turned, row_stats, col_stats)
    shards = mats[1:9] + [pixel_columns(mats[0]), pixel_columns(mats[9])]
    apart = (lax.axis_size("dp"), band_count) == (4, 8)
    high, low = prep(lon_shift, fields)
    lines_ready = (moments.own, moments.other, moments.mean)
    late = []

    def prepare(arrived):
        token = tie(lon_shift, [a[1:] for a in arrived]) if arrived else lon_shift
        late.append(prep(token, target, weight))
        return late[0]

    whole_weights, (*gain, gain_a, gain_m) = gather_weights(
        shards, gains, (lambda arrived: (high, lines_ready), prepare)
    )
    wanted = late[0] if late else prepare([])
    f_in0, f_in1, f_out0, f_out1, f_up, f_back, f_fin, f_fout, f_embed, f_head = whole_weights
    stream = embed(f_embed, high, low)
    own, stay, send, *kept_e = encoder(lon_shift, stream, f_in0, f_out0, gain[0], gain[1])
    if apart:
        q, q_got, h, h_got = gather_rest(*f_fin, stream, own)
        f_fin, f_fout = join_cores(q, q_got, h, h_got, w_fin.shape[1], w_fout.shape[0])
    send = shifted(send, "lat", -1)
    rolled, wide, last, stay, send, *kept_m = merging(
        stay, send, f_up, f_back, f_fin, f_fout, gain_a, gain_m
    )
    send = shifted(send, "lat", 1)
    start, out, *kept_d = decoder(lon_shift, own, stay, send, f_in1, f_out1, gain[2], gain[3])
    grad, g_head, gg_final, sums = head(
        out, gain[4], f_head, wanted, chans, 8 if apart else 1
    )
    b = lambda g: banded(g, 8)
    grad, stay, send, g_in1, g_out1, gg_2, gg_3 = decoder_back(
        lon_shift, grad, start, kept_d, f_in1, f_out1, gain[2], gain[3]
    )
    send = shifted(send, "lat", -1)
    if apart:
        s_a = halve(
            jnp.concatenate([g_head, widen_pair(b(g_in1), b(g_out1))], axis=1), "c"
        )
        s_a = lax.psum_scatter(flat(s_a), "lat", scatter_dimension=0, tiled=True)
    g_back, g_fout, gg_m, between, attended, g_fin = merging_mlp_back(
        stay, send, last, kept_m, f_back, f_fin, f_fout, gain_m
    )
    stay, send, g_up, gg_a, g_fin = merging_attention_back(
        between, attended, rolled, wide, kept_m, f_up, f_fin, gain_a, g_fin, stay.shape
    )
    send = shifted(send, "lat", 1)
    if apart:
        s_f = halve(b(g_fout), "c", beside=stay)
        s_m = [b(g_fin), jnp.concatenate([b(g_up), b(g_back)], axis=-1)]
        s_m = jnp.concatenate(s_m, axis=1)
        started_f, started_m = Halving(s_f, "y"), Halving(halve(s_m, "c"), "x")
        send = started_m.ahead_of(started_f.ahead_of(send))
    grad, g_in0, g_out0, gg_0, gg_1 = encoder_back(
        lon_shift, grad, stay, send, stream, kept_e, f_in0, f_out0, gain[0], gain[1]
    )
    gain_rows = [gg_0, gg_1, gg_2, gg_3, gg_final, gg_a, gg_m]
    if apart:
        z = place_of()[0]
        s_f, s_m = started_f.done(grad), started_m.done(grad)
        s_c = pack_early(g_in0, g_out0, gain_rows, sums)
        started_m, started_c = Halving(s_m, "y"), Halving(s_c, "c")
        grad = started_c.ahead_of(started_m.ahead_of(grad))
    g_embed = embed_back(grad, high, low, 8 if apart else 1)
    if apart:
        s_m, s_c = started_m.done(g_embed), started_c.done(g_embed)
        s_d = halve(g_embed, "c")
        s_c = halve(s_c, "y")
        s_d = halve(s_d, "x")
        s_d = halve(s_d, "y")
        n_d = s_d.shape[1]
        s_f = line_sum(s_f, z, (g_embed,))
        s_m = line_sum(s_m, z)
        s_c = line_sum(jnp.concatenate([s_d, s_c], axis=1), z)
        parts = over_x([s_m, s_c[:n_d]], [s_a, s_f, s_c[n_d:]])
        n_in, n_out, n_fin, n_up = (g.shape[0] // 8 for g in (g_in0, g_out0, g_fin, g_up))
        g_embed, *grads, g_head, row = collect(parts, n_in, n_out, n_fin, n_up, width)
        n_extra = gains.shape[0] * gains.shape[1]
        total, count = row[0, n_extra], chans * row[0, n_extra + 1]
        g_gain = row[0, :n_extra].reshape(gains.shape)
    else:
        g_gain = jnp.concatenate(gain_rows, axis=1).reshape(gains.shape[0], width)
        chunked = [g.reshape(8, width, -1) for g in (g_embed, g_head)]
        grads = [g_in0, g_in1, g_out0, g_out1, g_up, g_back, g_fin, g_fout]
        grads, (g_embed, g_head), g_gain, total, count = scatter_plain(
            grads, chunked, g_gain, sums[0, 0], chans * sums[1, 0]
        )
    grads = [channel_columns(g_embed, chans), *grads, channel_columns(g_head, chans)]
    loss = total / count
    rescale = 2.0 / count
    new, rounded, next_rows, next_cols, next_v_gain = moments.step(
        grads, rescale, gains, g_gain, v_gain
    )

    def laid_out(new):
        n_embed, n_in, n_out, n_merge, n_fin, n_fout, n_head, n_gains = new
        turn = lambda v: v.transpose(0, 2, 1)
        return [
            n_embed.T, turn(n_in), turn(n_out), turn(n_merge), n_fin.T,
            n_fout, n_head, n_gains,
        ]

    results, copies = laid_out(new), laid_out(rounded)
    return (loss, *results, next_rows, next_cols, next_v_gain, *copies)


def solution(mesh):
    placed = (
        P("dp", None, "lat", None),
        P("dp", None, "lat", None),
        P("dp", "lat", None),
        P("dp"),
        P(),
        P("dp"),
        P(None, "lat"),
        P(None, None, "lat"),
        P(None, "lat", None),
        P(None, None, "lat"),
        P(None, "lat"),
        P("lat", None),
        P("lat", None),
        P(None, "lat"),
        P(),
        P(),
        P(None, "lat"),
    )
    weights = placed[6:14]
    return jax.shard_map(
        on_device,
        mesh=mesh,
        in_specs=placed,
        out_specs=(P(), *weights, P(), P(), P(None, "lat"), *weights),
        check_vma=False,
    )
```
